32 devices in a mesh: graph: 2 (over x), blk: 16 (over z, y, core).
Axes of the slice: x: 2, y: 2, z: 4, core: 2. Of those that a mesh axis runs over, the one named last changes fastest.
Arguments:
- node_state: float32 [32, 2048, 128], P('graph', 'blk'), may hold values from -120 to 120
- field_window: float32 [32, 2048, 25], P('graph', 'blk'), may hold values from -6 to 6
- edge_offset: int32 [32, 2048, 6], P('graph', 'blk'), may hold values from -3 to 3
- pde_id: int32 [32], P('graph'), may hold values from 0 to 7
- pde_table: float32 [8, 3], replicated, may hold values from -2 to 2
- cotangent: float32 [32, 2048, 128], P('graph', 'blk'), may hold values from -70 to 70
- edge_w1: float32 [2, 285, 128], replicated, may hold values from -0.375 to 0.375
- edge_b1: float32 [2, 128], replicated, may hold values from -3 to 3
- edge_w2: float32 [2, 128, 128], replicated, may hold values from -0.5 to 0.5
- edge_b2: float32 [2, 128], replicated, may hold values from -3 to 3
- node_w1: float32 [2, 259, 128], replicated, may hold values from -0.375 to 0.375
- node_b1: float32 [2, 128], replicated, may hold values from -3 to 3
- node_w2: float32 [2, 128, 128], replicated, may hold values from -0.5 to 0.5
- node_b2: float32 [2, 128], replicated, may hold values from -3 to 3
Outputs:
- state_out: float32 [32, 2048, 128], P('graph', 'blk')
- grad_state: float32 [32, 2048, 128], P('graph', 'blk')
- grad_edge_w1: float32 [2, 285, 128], replicated
- grad_edge_b1: float32 [2, 128], replicated
- grad_edge_w2: float32 [2, 128, 128], replicated
- grad_edge_b2: float32 [2, 128], replicated
- grad_node_w1: float32 [2, 259, 128], replicated
- grad_node_b1: float32 [2, 128], replicated
- grad_node_w2: float32 [2, 128, 128], replicated
- grad_node_b2: float32 [2, 128], replicated
The draws below stay inside these ranges and needn't reach their ends.
Inputs may be any that keep to these rules, and one draw needn't show every extreme that they name: `edge_offset`: 0 marks an empty slot; any other value o joins node i to node i + o of the same trajectory, taken around the periodic domain.
All inputs are finite; a program needn't handle non-finite values.
Results may differ from the reference program's by a relative error of at most 0.0003.
Values sent between devices are 32-bit elements; how exact they have to be, the bound alone decides.
A program may use at most 192 MiB of HBM per device.

```python
import math
from functools import partial
import jax
import jax.numpy as jnp
from jax import lax

D = 128
TW = 25
NPAR = 3
K = 6
HALO = 3
NPDE = 8
LAYERS = 2
NODE_DEV = 128
NODES = 2048
TRAJ = 32
EDGE_IN = 285
NODE_IN = 259


def profiled(key, base_scale, rise):
    keys = jax.random.split(key, 2)
    place = (jnp.arange(NODES, dtype=jnp.float32) / NODES)[None, :, None]
    row_scale = base_scale * 10.0 ** (rise * place)
    col_scale = jnp.exp(jax.random.uniform(keys[1], (TRAJ, 1, D), jnp.float32, 0.0, math.log(4.0)))
    rough = jax.random.truncated_normal(keys[0], -4.0, 4.0, (TRAJ, NODES, D), jnp.float32)
    return rough * row_scale * col_scale


def draw_node_state(key, part):
    key = jax.random.fold_in(key, 11)
    return profiled(key, 0.3, 1.0)


def draw_cotangent(key, part):
    key = jax.random.fold_in(key, 23)
    return profiled(key, 0.6, 0.5)


def set_ends(drawn, rng, low, largest):
    extent = drawn.shape
    spot = [jax.random.randint(jax.random.fold_in(rng, axis), (), 0, extent[axis]) for axis in range(len(extent))]
    drawn = drawn.at[tuple(spot)].set(low)
    longest = extent.index(max(extent))
    spot[longest] = (spot[longest] + 1) % extent[longest]
    return drawn.at[tuple(spot)].set(largest)


def steps_of(rng, dims, pieces, least, largest):
    gain = 1.0
    for position, blocks in pieces:
        draws = jax.random.uniform(jax.random.fold_in(jax.random.fold_in(rng, 6), position), (blocks,), jnp.float32, least / len(pieces), largest / len(pieces))
        gain = gain * jnp.repeat(jnp.exp(draws), dims[position] // blocks).reshape((-1,) + (1,) * (len(dims) - 1 - position))
    return gain


def scatter_about(key, dims, scale, most, cuts=(), kind=jnp.bfloat16):
    entries = scale * jax.random.normal(key, dims, jnp.float32)
    if cuts:
        entries = entries * steps_of(key, dims, cuts, -0.22, 0.18)
    return jnp.clip(entries, -most, most).astype(kind)


def setup_inputs(seed: int = 0) -> dict:
    arg_keys = jax.random.split(jax.random.key(seed), 15)
    node_state = draw_node_state(jax.random.fold_in(arg_keys[14], 71), 0)
    field_window = scatter_about(arg_keys[1], (TRAJ, NODES, TW), 1.0, 6.0, ((0, 2), (1, 16)), jnp.float32)
    edge_offset = set_ends(jax.random.randint(arg_keys[2], (TRAJ, NODES, K), -HALO, HALO + 1), jax.random.fold_in(arg_keys[2], 1), -HALO, HALO).astype(jnp.int32)
    pde_id = set_ends(jax.random.randint(arg_keys[3], (TRAJ,), 0, NPDE), jax.random.fold_in(arg_keys[3], 1), 0, NPDE - 1).astype(jnp.int32)
    pde_table = jnp.clip(jax.random.uniform(arg_keys[4], (NPDE, NPAR), jnp.float32, -2.0, 2.0), -2.0, 2.0)
    cotangent = draw_cotangent(jax.random.fold_in(arg_keys[14], 71), 0)
    edge_w1 = scatter_about(arg_keys[6], (LAYERS, EDGE_IN, D), EDGE_IN ** -0.5, 0.375, (), jnp.float32)
    edge_b1 = scatter_about(arg_keys[7], (LAYERS, D), 0.3, 3.0, (), jnp.float32)
    edge_w2 = scatter_about(arg_keys[8], (LAYERS, D, D), D ** -0.5, 0.5, (), jnp.float32)
    edge_b2 = scatter_about(arg_keys[9], (LAYERS, D), 0.3, 3.0, (), jnp.float32)
    node_w1 = scatter_about(arg_keys[10], (LAYERS, NODE_IN, D), NODE_IN ** -0.5, 0.375, (), jnp.float32)
    node_b1 = scatter_about(arg_keys[11], (LAYERS, D), 0.3, 3.0, (), jnp.float32)
    node_w2 = scatter_about(arg_keys[12], (LAYERS, D, D), D ** -0.5, 0.5, (), jnp.float32)
    node_b2 = scatter_about(arg_keys[13], (LAYERS, D), 0.3, 3.0, (), jnp.float32)
    return dict(node_state=node_state, field_window=field_window, edge_offset=edge_offset, pde_id=pde_id, pde_table=pde_table, cotangent=cotangent, edge_w1=edge_w1, edge_b1=edge_b1, edge_w2=edge_w2, edge_b2=edge_b2, node_w1=node_w1, node_b1=node_b1, node_w2=node_w2, node_b2=node_b2)


EPSILON = 1e-05
PRECISE = lax.Precision.HIGHEST

@jax.custom_vjp
def low(v):
    return lax.optimization_barrier(v.astype(jnp.bfloat16)).astype(jnp.float32)

@jax.custom_vjp
def low_back(v):
    return v

def low_keep(v):
    return (low(v), None)

def low_pass(kept, grad):
    return (grad,)

def back_keep(v):
    return (v, None)

def back_low(kept, grad):
    return (low(grad),)
low.defvjp(low_keep, low_pass)
low_back.defvjp(back_keep, back_low)

def swish_act(value):
    return value * jax.nn.sigmoid(value)

def project(left, right):
    return jnp.dot(left, right, precision=PRECISE)

def wrapped(values):
    return jnp.concatenate([values[-HALO:], values, values[:HALO]], 0)

def edge_block(state_ext, field_ext, offsets, pde_theta, weight_first, bias_first, weight_second, bias_second, start):
    state_rows = lax.dynamic_slice_in_dim(state_ext, start, NODE_DEV + 2 * HALO, 0)
    field_rows = lax.dynamic_slice_in_dim(field_ext, start, NODE_DEV + 2 * HALO, 0)
    slot_offsets = lax.dynamic_slice_in_dim(offsets, start, NODE_DEV, 0)
    places = jnp.arange(NODE_DEV, dtype=jnp.int32)[:, None] + HALO + slot_offsets
    state_self = jnp.broadcast_to(state_rows[HALO:HALO + NODE_DEV, None, :], (NODE_DEV, K, state_rows.shape[1]))
    state_far = state_rows[places]
    field_diff = field_rows[HALO:HALO + NODE_DEV, None, :] - field_rows[places]
    distance = (-slot_offsets.astype(jnp.float32) / HALO)[..., None]
    theta_rows = jnp.broadcast_to(pde_theta, (NODE_DEV, K, pde_theta.shape[0]))
    edge_input = jnp.concatenate([state_self, state_far, field_diff, distance, theta_rows], 2)
    edge_hidden = swish_act(project(edge_input, weight_first) + bias_first)
    message = swish_act(project(edge_hidden, weight_second) + bias_second)
    slot_mask = (slot_offsets != 0).astype(jnp.float32)[..., None]
    return lax.optimization_barrier(jnp.sum(message * slot_mask, 1)) / K

def trajectory(state, field_window, offsets, pde_theta, params):
    edge_w1, edge_b1, edge_w2, edge_b2, node_w1, node_b1, node_w2, node_b2 = params
    field_ext = wrapped(field_window)
    starts = jnp.arange(NODES // NODE_DEV, dtype=jnp.int32) * NODE_DEV
    for level in range(LAYERS):
        state_ext = wrapped(state)
        block_fn = jax.checkpoint(partial(edge_block, state_ext, field_ext, offsets, pde_theta, edge_w1[level], edge_b1[level], edge_w2[level], edge_b2[level]))
        aggregate = lax.map(block_fn, starts).reshape(NODES, state.shape[1])
        theta_rows = jnp.broadcast_to(pde_theta, (NODES, pde_theta.shape[0]))
        node_input = jnp.concatenate([state, aggregate, theta_rows], 1)
        node_hidden = swish_act(project(node_input, node_w1[level]) + node_b1[level])
        update = state + swish_act(project(node_hidden, node_w2[level]) + node_b2[level])
        center = lax.optimization_barrier(jnp.mean(update, 0))
        variance = lax.optimization_barrier(jnp.mean(jnp.square(update - center), 0))
        state = (update - center) * lax.rsqrt(variance + EPSILON)
    return state

def reference(node_state, field_window, edge_offset, pde_id, pde_table, cotangent, edge_w1, edge_b1, edge_w2, edge_b2, node_w1, node_b1, node_w2, node_b2):
    params = (edge_w1, edge_b1, edge_w2, edge_b2, node_w1, node_b1, node_w2, node_b2)

    def per_trajectory(items):
        state, field, offsets, ident, upstream = items
        pde_theta = pde_table[ident]

        def forward_fn(state_in, params_in):
            return trajectory(state_in, field, offsets, pde_theta, params_in)
        output, pullback = jax.vjp(forward_fn, state, params)
        grad_in, grad_params = pullback(upstream)
        return (output, grad_in, grad_params)
    outputs, grad_states, grad_params = lax.map(per_trajectory, (node_state, field_window, edge_offset, pde_id, cotangent))
    summed = tuple((lax.optimization_barrier(jnp.sum(member, 0)) for member in grad_params))
    return (outputs, grad_states, summed[0], summed[1], summed[2], summed[3], summed[4], summed[5], summed[6], summed[7])
```

```python
import functools

import jax
import jax.numpy as jnp
from jax import lax
from jax.experimental import pallas as pl
from jax.experimental.pallas import tpu as pltpu
from jax.sharding import PartitionSpec as P

D = 128
TW = 25
NPAR = 3
K = 6
HALO = 3
NPDE = 8
LAYERS = 2
EDGE_IN = 2 * D + TW + 1 + NPAR
NODE_IN = 2 * D + NPAR
OFFSETS = tuple(o for o in range(-HALO, HALO + 1) if o != 0)

EPSILON = 1e-05
RIM = 8
GROUPS = 2
AUX = 32
A_THETA = TW
A_ONE = TW + NPAR
A_PLACE = TW + NPAR + 1
UNIT_AUX = 3 * D
UNIT_BIAS = UNIT_AUX + AUX
UNIT_ROWS = UNIT_BIAS + 8

F32 = jnp.float32
BF16 = jnp.bfloat16
MESH = pl.DeviceIdType.MESH


def dot(left, right):
    return jnp.dot(left, right, preferred_element_type=F32)


def dot_t(left, right):
    return lax.dot_general(left, right, (((0,), (0,)), ((), ())), preferred_element_type=F32)


def split(value):
    head = value.astype(BF16)
    tail = (value - head.astype(F32)).astype(BF16)
    return head, tail


def pair(value):
    head, tail = split(value)
    return jnp.concatenate([head, tail], 1)


def halves(product):
    return product[:, :D] + product[:, D:]


def doubled(weight):
    both = pair(weight)
    return jnp.concatenate([both, both], 0)


def swish_parts(half):
    t = jnp.tanh(half)
    u = 1.0 + t
    act = half * u
    return act, u + act * (1.0 - t)


def digit_stages(count, sizes=(4,)):
    stages, stride, step = [], 1, 0
    while stride < count:
        size = sizes[min(step, len(sizes) - 1)]
        while count // stride % size:
            size -= 1
        stages.append((stride, size))
        stride *= size
        step += 1
    return stages


class Links:
    def __init__(self, blk, graph):
        self.blk, self.graph = blk, graph
        self.me = lax.axis_index("blk")
        self.mine = lax.axis_index("graph")
        self.stat_stages = digit_stages(blk)
        self.sum_stages = []
        for position, (stride, size) in enumerate(digit_stages(blk, (2, 2, 4))):
            digits = [("blk", stride, size)]
            if position == 1:
                digits.append(("graph", 1, graph))
            self.sum_stages.append(digits)

    def ring(self, shift):
        return (self.mine, lax.rem(self.me + shift + self.blk, self.blk))

    def stat_peer(self, stage, shift):
        stride, size = self.stat_stages[stage]
        digit = lax.rem(self.me // stride, size)
        other = lax.rem(digit + shift, size)
        return (self.mine, self.me + (other - digit) * stride)

    def sum_size(self, stage):
        size = 1
        for _, _, count in self.sum_stages[stage]:
            size *= count
        return size

    def sum_digit(self, stage):
        value = 0
        for axis, stride, size in self.sum_stages[stage]:
            place = self.me if axis == "blk" else self.mine
            value = value * size + lax.rem(place // stride, size)
        return value

    def sum_peer(self, stage, shift):
        size = self.sum_size(stage)
        other = lax.rem(self.sum_digit(stage) + shift, size)
        coords = {"blk": self.me, "graph": self.mine}
        rest = other
        for axis, stride, count in reversed(self.sum_stages[stage]):
            place = coords[axis]
            now = lax.rem(place // stride, count)
            coords[axis] = place + (lax.rem(rest, count) - now) * stride
            rest = rest // count
        return (coords["graph"], coords["blk"]), other

    def greeted(self):
        peers = [self.ring(1), self.ring(-1)]
        for stage, (_, size) in enumerate(self.stat_stages):
            peers += [self.stat_peer(stage, shift) for shift in range(1, size)]
        for stage in range(len(self.sum_stages)):
            peers += [self.sum_peer(stage, shift)[0] for shift in range(1, self.sum_size(stage))]
        return peers


def remote(src, dst, send_sem, recv_sem, device):
    return pltpu.make_async_remote_copy(
        src_ref=src,
        dst_ref=dst,
        send_sem=send_sem,
        recv_sem=recv_sem,
        device_id=device,
        device_id_type=MESH,
    )


def kernel_body(
    blk,
    graph,
    state_in,
    field_in,
    offset_in,
    id_in,
    table_in,
    cot_in,
    ew1,
    eb1,
    ew2,
    eb2,
    nw1,
    nb1,
    nw2,
    nb2,
    state_out,
    dst,
    unit_all,
    w_in,
    w_e2,
    w_e2t,
    w_agg,
    w_n2,
    w_n2t,
    w_np,
    w_ep,
    w_aux,
    spread,
    counts,
    weigh,
    aux_t,
    xs,
    xa,
    a_buf,
    r_buf,
    n_buf,
    slope,
    agg2,
    hid2,
    sn1,
    sn2,
    upd,
    y0,
    yh,
    dag,
    e1,
    dxh,
    dxl,
    acc_n2,
    acc_agg,
    acc_nx,
    acc_e2,
    acc_x,
    acc_b,
    stat,
    stat_recv,
    fin,
    h0s,
    h0r,
    hs,
    hr,
    rs,
    rr,
    unit,
    unit_recv,
    stat_ssem,
    stat_rsem,
    rim_ssem,
    rim_rsem,
    sum_ssem,
    sum_rsem,
):
    traj, nodes, _ = state_in.shape
    per = traj // GROUPS
    chunk = min(4, per)
    ext = nodes + 2 * RIM
    total = float(nodes * blk)
    links = Links(blk, graph)
    stages = links.stat_stages

    barrier = pltpu.get_barrier_semaphore()
    greeted = links.greeted()
    for peer in greeted:
        pl.semaphore_signal(barrier, inc=1, device_id=peer, device_id_type=MESH)

    offs = [offset_in[pl.ds(k * traj, traj), :] for k in range(K)]
    for i, o in enumerate(OFFSETS):
        many = jnp.zeros((traj, nodes), F32)
        for k in range(K):
            many = many + jnp.where(offs[k] == o, 1.0, 0.0)
        counts[pl.ds(i * traj, traj), :] = many
    counts[pl.ds(K * traj, 2 * traj), :] = jnp.zeros((2 * traj, nodes), F32)
    rows = lax.broadcasted_iota(jnp.int32, (D, K * D), 0)
    cols = lax.broadcasted_iota(jnp.int32, (D, K * D), 1)
    spread[...] = jnp.where(rows == 3 * AUX + cols // D, 1.0, 0.0).astype(BF16)
    aux_t[...] = jnp.zeros_like(aux_t)
    place = lax.broadcasted_iota(jnp.int32, (1, nodes), 1).astype(F32) - nodes / 2

    def prepare(t, slot):
        tile = aux_t.at[slot]
        tile[pl.ds(0, TW), :] = field_in[pl.ds(t, TW, stride=traj), :]
        row = id_in[t]
        for q in range(NPAR):
            tile[pl.ds(A_THETA + q, 1), :] = jnp.full((1, nodes), table_in[q, row], F32)
        tile[pl.ds(A_ONE, 1), :] = jnp.ones((1, nodes), F32)
        tile[pl.ds(A_PLACE, 1), :] = place
        head, tail = split(tile[pl.ds(0, AUX), :])
        head, tail = head.astype(F32), tail.astype(F32)
        full = jnp.concatenate(
            [
                head,
                tail,
                head,
                counts[pl.ds(t, 8, stride=traj), :],
                jnp.zeros((D - 3 * AUX - 8, nodes), F32),
            ],
            0,
        )
        back = full.T
        h0s[0, 1, t] = back[:RIM]
        h0s[1, 1, t] = back[nodes - RIM :]
        h0s[0, 0, t] = state_in[t, pl.ds(0, RIM), :]
        h0s[1, 0, t] = state_in[t, pl.ds(nodes - RIM, RIM), :]
        low = back.astype(BF16)
        xa[t, pl.ds(0, nodes), :] = low
        return low

    def prepare_chunk(j, _):
        lows = [prepare(j * chunk + c, c) for c in range(chunk)]
        many = dot(jnp.concatenate(lows, 0), spread[...])
        for c in range(chunk):
            for i in range(K):
                weigh[j * chunk + c, pl.ds(i * nodes, nodes), :] = many[
                    c * nodes : (c + 1) * nodes, i * D : (i + 1) * D
                ]
        return 0

    lax.fori_loop(0, traj // chunk, prepare_chunk, 0)

    pl.semaphore_wait(barrier, len(greeted))

    def halo0(way):
        return remote(
            h0s.at[way],
            h0r.at[way],
            rim_ssem.at[0, way],
            rim_rsem.at[0, way],
            links.ring(1 if way else -1),
        )

    for way in range(2):
        halo0(way).start()

    e1[...] = jnp.zeros_like(e1)
    for l in range(LAYERS):
        w_self = ew1[pl.ds(0, D), l, :]
        w_far = ew1[pl.ds(D, D), l, :]
        n_self = nw1[pl.ds(0, D), l, :]
        n_agg = nw1[pl.ds(D, D), l, :]
        for i, w in enumerate((w_self, w_far, n_self)):
            head, tail = split(0.5 * w)
            cut = pl.ds(i * D, D)
            w_in[l, pl.ds(0, D), cut] = head
            w_in[l, pl.ds(D, D), cut] = head
            w_in[l, pl.ds(2 * D, D), cut] = tail
        w_field = 0.5 * ew1[pl.ds(2 * D, TW), l, :]
        w_place = (0.5 / HALO) * ew1[pl.ds(2 * D + TW, 1), l, :]
        w_theta = 0.5 * ew1[pl.ds(2 * D + TW + 1, NPAR), l, :]
        n_theta = 0.5 * nw1[pl.ds(2 * D, NPAR), l, :]
        w_aux[...] = jnp.zeros_like(w_aux)
        w_aux[pl.ds(0, TW), pl.ds(0, D)] = w_field
        w_aux[pl.ds(0, TW), pl.ds(D, D)] = -w_field
        w_aux[pl.ds(A_THETA, NPAR), pl.ds(0, D)] = w_theta
        w_aux[pl.ds(A_THETA, NPAR), pl.ds(2 * D, D)] = n_theta
        w_aux[pl.ds(A_ONE, 1), pl.ds(0, D)] = 0.5 * eb1[pl.ds(l, 1), :]
        w_aux[pl.ds(A_ONE, 1), pl.ds(2 * D, D)] = 0.5 * nb1[pl.ds(l, 1), :]
        w_aux[pl.ds(A_PLACE, 1), pl.ds(0, D)] = w_place
        w_aux[pl.ds(A_PLACE, 1), pl.ds(D, D)] = -w_place
        head, tail = split(w_aux[...])
        w_in[l, pl.ds(3 * D, AUX), :] = head
        w_in[l, pl.ds(3 * D + AUX, AUX), :] = head
        w_in[l, pl.ds(3 * D + 2 * AUX, AUX), :] = tail
        w_in[l, pl.ds(3 * D + 3 * AUX, AUX), :] = jnp.zeros((AUX, 3 * D), BF16)
        second = 0.5 * ew2[l]
        w_e2[l] = doubled(second)
        w_e2t[l] = doubled(second.T)
        w_agg[l] = doubled(0.5 * n_agg)
        w_n2[l] = doubled(0.5 * nw2[l])
        w_n2t[l] = doubled(nw2[l].T)
        head, tail = split(jnp.concatenate([n_self.T, 0.5 * n_agg.T], 1))
        w_np[l, pl.ds(0, D), :] = head
        w_np[l, pl.ds(D, D), :] = head
        w_np[l, pl.ds(2 * D, D), :] = tail
        w_ep[l, pl.ds(0, D), :] = pair(w_self.T)
        w_ep[l, pl.ds(D, D), :] = pair(w_far.T)

    def stat_copy(event, stage, shift):
        size = stages[stage][1]
        return remote(
            stat.at[event, stage],
            stat_recv.at[event, stage, shift - 1],
            stat_ssem.at[event, stage, shift - 1],
            stat_rsem.at[event, stage, shift - 1],
            links.stat_peer(stage, shift),
        )

    def stat_send(event, stage):
        for shift in range(1, stages[stage][1]):
            stat_copy(event, stage, shift).start()

    def stat_merge(event, stage):
        stride, size = stages[stage]
        for shift in range(1, size):
            stat_copy(event, stage, shift).wait_recv()
        parts = [stat.at[event, stage]] + [
            stat_recv.at[event, stage, shift - 1] for shift in range(1, size)
        ]

        def row(q):
            return [part[pl.ds(q * per, per), :] for part in parts]

        u, c = row(2), row(3)
        if event >= 4:
            return None, None, sum(u[1:], u[0]), sum(c[1:], c[0])
        m, m2 = row(0), row(1)
        mean = sum(m[1:], m[0]) * (1.0 / size)
        gaps = [value - mean for value in m]
        spread2 = sum((gap * gap for gap in gaps[1:]), gaps[0] * gaps[0])
        m2_all = sum(m2[1:], m2[0]) + spread2 * float(nodes * stride)
        u_all = sum(u[1:], u[0])
        c_all = sum(c[1:], c[0])
        for gap, value in zip(gaps, u):
            c_all = c_all + gap * value
        return mean, m2_all, u_all, c_all

    def stat_forward(event):
        for stage in range(1, len(stages)):
            merged = stat_merge(event, stage - 1)
            for q, value in enumerate(merged):
                if value is not None:
                    stat[event, stage, pl.ds(q * per, per), :] = value
            stat_send(event, stage)

    def stat_finish(event):
        mean, m2, u, c = stat_merge(event, len(stages) - 1)
        if event < 4:
            scale = lax.rsqrt(m2 * (1.0 / total) + EPSILON)
            fin[event, 0] = mean
            fin[event, 1] = scale
            fin[event, 2] = u * (1.0 / total)
            fin[event, 3] = scale * c * (1.0 / total)
        else:
            fin[event, 2] = u * (1.0 / total)
            fin[event, 3] = c * (1.0 / total)

    def rim_copy(kind, send, recv, way):
        return remote(
            send.at[way],
            recv.at[way],
            rim_ssem.at[kind, way],
            rim_rsem.at[kind, way],
            links.ring(1 if way else -1),
        )

    def rows_of(buf, l, t, c, start, size):
        return buf[l, pl.ds(t, c), pl.ds(start, size), :].reshape(c * size, buf.shape[-1])

    def forward(l, g, hook):
        base = g * per
        event = 2 * l + g
        if l == 0:
            if g == 0:
                for way in range(2):
                    halo0(way).wait_recv()
        else:
            stat_finish(g)
            for way in range(2):
                rim_copy(1 + g, hs.at[g], hr.at[g], way).wait_recv()
        lane = lax.broadcasted_iota(jnp.int32, (RIM, D), 1)
        moved = jnp.where((lane == A_PLACE) | (lane == 2 * AUX + A_PLACE), float(nodes), 0.0)

        def enter(j, _):
            for c in range(chunk):
                s = j * chunk + c
                t = base + s
                if l == 0:
                    xs[0, t, pl.ds(0, nodes), :] = pair(state_in[t])
                    near = jnp.concatenate([h0r[1, 0, t], h0r[0, 0, t]], 0)
                    xs[0, t, pl.ds(nodes, 2 * RIM), :] = pair(near)
                    side = jnp.concatenate([h0r[1, 1, t] - moved, h0r[0, 1, t] + moved], 0)
                    xa[t, pl.ds(nodes, 2 * RIM), :] = side.astype(BF16)
                else:
                    mean = fin[g, 0, pl.ds(s, 1), :]
                    scale = fin[g, 1, pl.ds(s, 1), :]
                    y = (upd[t] - mean) * scale
                    y0[t] = y
                    xs[1, t, pl.ds(0, nodes), :] = pair(y)
                    near = jnp.concatenate([hr[g, 1, s], hr[g, 0, s]], 0)
                    near = (near - mean) * scale
                    yh[t] = near
                    xs[1, t, pl.ds(nodes, 2 * RIM), :] = pair(near)
            t = base + j * chunk
            x = rows_of(xs, l, t, chunk, 0, ext)
            side = xa[pl.ds(t, chunk)].reshape(chunk * ext, D)
            p = dot(x, w_in[l, pl.ds(0, 2 * D), :])
            p = p + dot(jnp.concatenate([x[:, :D], side], 1), w_in[l, pl.ds(2 * D, 2 * D), :])
            for c in range(chunk):
                at = c * ext
                a_buf[l, t + c] = p[at : at + nodes, :D]
                r_buf[l, t + c, pl.ds(RIM, nodes), :] = p[at : at + nodes, D : 2 * D]
                r_buf[l, t + c, pl.ds(0, RIM), :] = p[at + nodes : at + nodes + RIM, D : 2 * D]
                r_buf[l, t + c, pl.ds(RIM + nodes, RIM), :] = p[
                    at + nodes + RIM : at + ext, D : 2 * D
                ]
                n_buf[j * chunk + c] = p[at : at + nodes, 2 * D :]
            return 0

        lax.fori_loop(0, per // chunk, enter, 0)

        bias2 = 0.5 * eb2[pl.ds(l, 1), :]

        def edge(t, s):
            hidden = []
            for o in OFFSETS:
                half = a_buf[l, t] + r_buf[l, t, pl.ds(RIM + o, nodes), :]
                hidden.append(pair(half * (1.0 + jnp.tanh(half))))
            p = dot(jnp.concatenate(hidden, 0), w_e2[l])
            summed = None
            for i in range(K):
                half = halves(p[i * nodes : (i + 1) * nodes]) + bias2
                tanh = jnp.tanh(half)
                scaled = weigh[t, pl.ds(i * nodes, nodes), :] * (1.0 + tanh)
                message = scaled * half
                summed = message if summed is None else summed + message
                slope[l, t, pl.ds(i * nodes, nodes), :] = scaled + message * (1.0 - tanh)
            dag[s] = summed * (1.0 / K)

        half_way = per // 4

        def edge_pair(j, _):
            for c in range(2):
                edge(base + 2 * j + c, 2 * j + c)
            return 0

        lax.fori_loop(0, half_way, edge_pair, 0)
        hook()
        lax.fori_loop(half_way, per // 2, edge_pair, 0)

        node2 = 0.5 * nb2[pl.ds(l, 1), :]

        def node(j, _):
            s = j * chunk
            t = base + s
            both = pair(dag[pl.ds(s, chunk)].reshape(chunk * nodes, D))
            agg2[l, pl.ds(t, chunk)] = both.reshape(chunk, nodes, 2 * D)
            half = n_buf[pl.ds(s, chunk)].reshape(chunk * nodes, D) + halves(dot(both, w_agg[l]))
            act, rise = swish_parts(half)
            sn1[l, pl.ds(t, chunk)] = (0.5 * rise).reshape(chunk, nodes, D)
            both = pair(act)
            hid2[l, pl.ds(t, chunk)] = both.reshape(chunk, nodes, 2 * D)
            half = halves(dot(both, w_n2[l])) + node2
            act, rise = swish_parts(half)
            sn2[l, pl.ds(t, chunk)] = (0.5 * rise).reshape(chunk, nodes, D)
            for c in range(chunk):
                before = state_in[t + c] if l == 0 else y0[t + c]
                new = before + act[c * nodes : (c + 1) * nodes]
                (upd if l == 0 else state_out)[t + c] = new
                mean = jnp.sum(new, 0, keepdims=True) * (1.0 / nodes)
                gap = new - mean
                stat[event, 0, pl.ds(s + c, 1), :] = mean
                stat[event, 0, pl.ds(per + s + c, 1), :] = jnp.sum(gap * gap, 0, keepdims=True)
                if l == LAYERS - 1:
                    up = cot_in[t + c]
                    stat[event, 0, pl.ds(2 * per + s + c, 1), :] = jnp.sum(up, 0, keepdims=True)
                    stat[event, 0, pl.ds(3 * per + s + c, 1), :] = jnp.sum(
                        up * gap, 0, keepdims=True
                    )
                else:
                    hs[g, 0, s + c] = new[:RIM]
                    hs[g, 1, s + c] = new[nodes - RIM :]
            return 0

        if l < LAYERS - 1:
            stat[event, 0, pl.ds(2 * per, 2 * per), :] = jnp.zeros((2 * per, D), F32)
        lax.fori_loop(0, per // chunk, node, 0)
        stat_send(event, 0)
        if l < LAYERS - 1:
            for way in range(2):
                rim_copy(1 + g, hs.at[g], hr.at[g], way).start()

    def backward(l, g, hook):
        base = g * per
        event = 4 + g
        source = 2 + g if l == LAYERS - 1 else 4 + g
        if l == LAYERS - 1:
            stat_finish(2 + g)
        else:
            stat_finish(4 + g)
            for way in range(2):
                rim_copy(3 + g, rs.at[1, g], rr.at[1, g], way).wait_recv()
        own = 2 * l + g

        def node(j, _):
            s0 = j * chunk
            t0 = base + s0
            deltas, firsts = [], []
            for c in range(chunk):
                s, t = s0 + c, t0 + c
                scale = fin[own, 1, pl.ds(s, 1), :]
                mu = fin[source, 2, pl.ds(s, 1), :]
                cross = fin[source, 3, pl.ds(s, 1), :]
                if l == LAYERS - 1:
                    up = cot_in[t]
                    y = (state_out[t] - fin[own, 0, pl.ds(s, 1), :]) * scale
                    state_out[t] = y
                else:
                    dst[t, pl.ds(0, RIM), :] += rr[1, g, 1, s]
                    dst[t, pl.ds(nodes - RIM, RIM), :] += rr[1, g, 0, s]
                    up = dst[t]
                    y = y0[t]
                delta = scale * (up - mu - y * cross)
                first = delta * sn2[l, t]
                acc_b[l, 0] += jnp.sum(first.reshape(nodes // 8, 8, D), 0)
                deltas.append(delta)
                firsts.append(first)
            d2 = pair(jnp.concatenate(firsts, 0))
            x = rows_of(xs, l, t0, chunk, 0, nodes)
            side = xa[pl.ds(t0, chunk), pl.ds(0, nodes), :].reshape(chunk * nodes, D)
            size = chunk * nodes
            acc_n2[l] += dot_t(hid2[l, pl.ds(t0, chunk)].reshape(size, 2 * D), d2)
            d1 = halves(dot(d2, w_n2t[l])) * sn1[l, pl.ds(t0, chunk)].reshape(size, D)
            d1 = pair(d1)
            p = dot(jnp.concatenate([d1, d1[:, :D]], 1), w_np[l])
            for c in range(chunk):
                at = c * nodes
                dst[t0 + c] = deltas[c] + p[at : at + nodes, :D]
                dag[s0 + c] = p[at : at + nodes, D:] * (1.0 / K)
            acc_agg[l] += dot_t(agg2[l, pl.ds(t0, chunk)].reshape(size, 2 * D), d1)
            acc_nx[l] += dot_t(jnp.concatenate([x, side], 1), d1)
            return 0

        lax.fori_loop(0, per // chunk, node, 0)

        def edge(t, s, slot):
            hidden, deltas, rises = [], [], []
            coming = dag[s]
            bias = None
            for i, o in enumerate(OFFSETS):
                half = a_buf[l, t] + r_buf[l, t, pl.ds(RIM + o, nodes), :]
                act, rise = swish_parts(half)
                rises.append(rise)
                hidden.append(pair(act))
                delta = coming * slope[l, t, pl.ds(i * nodes, nodes), :]
                bias = delta if bias is None else bias + delta
                deltas.append(pair(delta))
            d2 = jnp.concatenate(deltas, 0)
            acc_e2[l] += dot_t(jnp.concatenate(hidden, 0), d2)
            acc_b[l, 1] += jnp.sum(bias.reshape(nodes // 8, 8, D), 0)
            p = dot(d2, w_e2t[l])
            near = None
            for i in range(K):
                d1 = halves(p[i * nodes : (i + 1) * nodes]) * rises[i]
                near = d1 if near is None else near + d1
                e1[slot, i, pl.ds(RIM, nodes), :] = d1
            far = None
            left = None
            right = None
            for i, o in enumerate(OFFSETS):
                part = e1[slot, i, pl.ds(RIM - o, nodes), :]
                far = part if far is None else far + part
                if o < 0:
                    part = e1[slot, i, pl.ds(-o, RIM), :]
                    left = part if left is None else left + part
                else:
                    part = e1[slot, i, pl.ds(RIM + nodes - o, RIM), :]
                    right = part if right is None else right + part
            rims = jnp.concatenate([left, right], 0)
            head, tail = split(near)
            head_f, tail_f = split(far)
            head_r, tail_r = split(rims)
            nothing = jnp.zeros((2 * RIM, D), BF16)
            dxh[s, pl.ds(0, nodes), :] = jnp.concatenate([head, head_f], 1)
            dxl[s, pl.ds(0, nodes), :] = jnp.concatenate([tail, tail_f], 1)
            dxh[s, pl.ds(nodes, 2 * RIM), :] = jnp.concatenate([nothing, head_r], 1)
            dxl[s, pl.ds(nodes, 2 * RIM), :] = jnp.concatenate([nothing, tail_r], 1)

        half_way = per // 4

        def edge_pair(j, _):
            for c in range(2):
                edge(base + 2 * j + c, 2 * j + c, c)
            return 0

        lax.fori_loop(0, half_way, edge_pair, 0)
        hook()
        lax.fori_loop(half_way, per // 2, edge_pair, 0)

        def leave(j, _):
            s0 = j * chunk
            t0 = base + s0
            size = chunk * ext
            x = rows_of(xs, l, t0, chunk, 0, ext)
            side = xa[pl.ds(t0, chunk)].reshape(size, D)
            high = dxh[pl.ds(s0, chunk)].reshape(size, 2 * D)
            low = dxl[pl.ds(s0, chunk)].reshape(size, 2 * D)
            p = halves(dot(high, w_ep[l]) + dot(low, w_ep[l]))
            for c in range(chunk):
                s, t, at = s0 + c, t0 + c, c * ext
                new = dst[t] + p[at : at + nodes]
                dst[t] = new
                rims = p[at + nodes : at + ext]
                rs[l, g, 0, s] = rims[:RIM]
                rs[l, g, 1, s] = rims[RIM:]
                if l > 0:
                    stat[event, 0, pl.ds(2 * per + s, 1), :] = jnp.sum(
                        new, 0, keepdims=True
                    ) + jnp.sum(rims, 0, keepdims=True)
                    stat[event, 0, pl.ds(3 * per + s, 1), :] = jnp.sum(
                        new * y0[t], 0, keepdims=True
                    ) + jnp.sum(rims * yh[t], 0, keepdims=True)
            inputs = jnp.concatenate([x, side], 1)
            acc_x[l] += dot_t(inputs, high) + dot_t(inputs, low)
            return 0

        if l > 0:
            stat[event, 0, pl.ds(0, 2 * per), :] = jnp.zeros((2 * per, D), F32)
        lax.fori_loop(0, per // chunk, leave, 0)
        if l > 0:
            stat_send(event, 0)
        for way in range(2):
            rim_copy(3 + 2 * (1 - l) + g, rs.at[l, g], rr.at[l, g], way).start()

    sums = links.sum_stages

    def quarter(acc, rows):
        return (
            acc[pl.ds(0, rows), pl.ds(0, D)]
            + acc[pl.ds(D, rows), pl.ds(0, D)]
            + acc[pl.ds(0, rows), pl.ds(D, D)]
            + acc[pl.ds(D, rows), pl.ds(D, D)]
        )

    def fold8(value):
        return jnp.sum(value, 0, keepdims=True)

    def node_unit(l, out):
        out[pl.ds(0, D), :] = quarter(acc_nx.at[l], D)
        out[pl.ds(D, D), :] = quarter(acc_agg.at[l], D)
        out[pl.ds(2 * D, D), :] = quarter(acc_n2.at[l], D)
        side = acc_nx[l, pl.ds(2 * D, AUX), :] + acc_nx[l, pl.ds(2 * D + AUX, AUX), :]
        out[pl.ds(UNIT_AUX, AUX), :] = halves(side)
        out[pl.ds(UNIT_BIAS, 1), :] = fold8(acc_b[l, 0])

    def edge_unit(l, out):
        both = acc_x[l, pl.ds(0, D), :] + acc_x[l, pl.ds(D, D), :]
        out[pl.ds(0, D), :] = both[:, :D]
        out[pl.ds(D, D), :] = both[:, D:]
        out[pl.ds(2 * D, D), :] = quarter(acc_e2.at[l], D)
        side = acc_x[l, pl.ds(2 * D, AUX), :] + acc_x[l, pl.ds(2 * D + AUX, AUX), :]
        row = lax.broadcasted_iota(jnp.int32, (AUX, D), 0)
        both = side[:, :D] - side[:, D:]
        out[pl.ds(UNIT_AUX, AUX), :] = jnp.where(
            row < TW, both, jnp.where(row == A_PLACE, both * (1.0 / HALO), side[:, :D])
        )
        out[pl.ds(UNIT_BIAS, 1), :] = fold8(acc_b[l, 1])

    unit_rows = unit_sizes(blk, graph)
    unit_at = [0, unit_rows[0], unit_rows[0] + unit_rows[1]]
    share = [1]
    for stage in range(len(sums)):
        share.append(share[-1] * links.sum_size(stage))

    def seg_rows(n, stage):
        return unit_rows[n] // share[stage + 1]

    def seg_start(n, stage):
        start = unit_at[n]
        for s in range(stage):
            start = start + links.sum_digit(s) * seg_rows(n, s)
        return start

    def recv_start(n, stage):
        at = sum(unit_rows[:n])
        for s in range(stage):
            at += (links.sum_size(s) - 1) * seg_rows(n, s)
        return at

    sem_start = []
    at = 0
    for stage in range(len(sums)):
        sem_start.append(at)
        at += links.sum_size(stage) - 1
    sem_count = at

    def rows_at(start, rows):
        return pl.ds(pl.multiple_of(start, 8), rows)

    def scatter_copy(n, stage, shift):
        peer, digit = links.sum_peer(stage, shift)
        rows = seg_rows(n, stage)
        sem = sem_start[stage] + shift - 1
        return remote(
            unit.at[rows_at(seg_start(n, stage) + digit * rows, rows), :],
            unit_recv.at[pl.ds(recv_start(n, stage) + (shift - 1) * rows, rows), :],
            sum_ssem.at[n, sem],
            sum_rsem.at[n, sem],
            peer,
        )

    def gather_copy(n, stage, shift):
        peer, _ = links.sum_peer(stage, shift)
        rows = seg_rows(n, stage)
        sem = sem_count + sem_start[stage] + shift - 1
        cut = rows_at(seg_start(n, stage + 1), rows)
        return remote(
            unit_all.at[cut, :],
            unit_all.at[cut, :],
            sum_ssem.at[n, sem],
            sum_rsem.at[n, sem],
            peer,
        )

    def gathered(n, stage, shift):
        peer, digit = links.sum_peer(stage, links.sum_size(stage) - shift)
        rows = seg_rows(n, stage)
        sem = sem_count + sem_start[stage] + shift - 1
        cut = rows_at(seg_start(n, stage) + digit * rows, rows)
        return remote(
            unit_all.at[cut, :],
            unit_all.at[cut, :],
            sum_ssem.at[n, sem],
            sum_rsem.at[n, sem],
            peer,
        )

    def shifts(stage):
        return range(1, links.sum_size(stage))

    def sum_step(n, step):
        count = len(sums)
        if 0 < step <= count:
            stage = step - 1
            rows = seg_rows(n, stage)
            for shift in shifts(stage):
                scatter_copy(n, stage, shift).wait_recv()
            cut = rows_at(seg_start(n, step), rows)
            value = unit[cut, :]
            for shift in shifts(stage):
                value = value + unit_recv[
                    pl.ds(recv_start(n, stage) + (shift - 1) * rows, rows), :
                ]
            if step < count:
                unit[cut, :] = value
            else:
                unit_all[cut, :] = value
        if step < count:
            for shift in shifts(step):
                scatter_copy(n, step, shift).start()
            return
        if step > count:
            stage = 2 * count - step
            for shift in shifts(stage):
                gathered(n, stage, shift).wait_recv()
        if step < 2 * count:
            for shift in shifts(2 * count - 1 - step):
                gather_copy(n, 2 * count - 1 - step, shift).start()

    steps = 2 * len(sums)

    def sum_drain(n):
        for stage in range(len(sums)):
            for shift in shifts(stage):
                scatter_copy(n, stage, shift).wait_send()
                gather_copy(n, stage, shift).wait_send()

    for acc in (acc_n2, acc_agg, acc_nx, acc_e2, acc_x, acc_b):
        acc[...] = jnp.zeros_like(acc)

    def nothing():
        pass

    forward(0, 0, nothing)
    forward(0, 1, lambda: stat_forward(0))
    forward(1, 0, lambda: stat_forward(1))
    forward(1, 1, lambda: stat_forward(2))
    backward(1, 0, lambda: stat_forward(3))
    backward(1, 1, lambda: stat_forward(4))
    def unit_part(at):
        return unit.at[pl.ds(at, UNIT_ROWS), :]

    filled = unit_at[0] + 2 * UNIT_ROWS, unit_at[1] + UNIT_ROWS, unit_at[2] + UNIT_ROWS
    for n in range(3):
        left = unit_at[n] + unit_rows[n] - filled[n]
        if left:
            unit[pl.ds(filled[n], left), :] = jnp.zeros((left, D), F32)
    for at in (0, UNIT_ROWS, unit_at[1], unit_at[2]):
        unit[pl.ds(at + UNIT_ROWS - 8, 8), :] = jnp.zeros((8, D), F32)
    node_unit(1, unit_part(0))
    edge_unit(1, unit_part(UNIT_ROWS))
    sum_step(0, 0)

    def hook_a():
        stat_forward(5)
        sum_step(0, 1)

    backward(0, 0, hook_a)
    sum_step(0, 2)
    backward(0, 1, lambda: sum_step(0, 3))
    node_unit(0, unit_part(unit_at[1]))
    edge_unit(0, unit_part(unit_at[2]))
    sum_step(1, 0)
    sum_step(2, 0)
    sum_step(0, 4)
    for step in range(1, steps + 1):
        sum_step(1, step)
        sum_step(2, step)
        if step == 1:
            for g in range(GROUPS):
                for way in range(2):
                    rim_copy(5 + g, rs.at[0, g], rr.at[0, g], way).wait_recv()
                for s in range(per):
                    t = g * per + s
                    dst[t, pl.ds(0, RIM), :] += rr[0, g, 1, s]
                    dst[t, pl.ds(nodes - RIM, RIM), :] += rr[0, g, 0, s]
    for step in range(5, steps + 1):
        sum_step(0, step)

    for way in range(2):
        halo0(way).wait_send()
    for g in range(GROUPS):
        for way in range(2):
            rim_copy(1 + g, hs.at[g], hr.at[g], way).wait_send()
            rim_copy(3 + g, rs.at[1, g], rr.at[1, g], way).wait_send()
            rim_copy(5 + g, rs.at[0, g], rr.at[0, g], way).wait_send()
    for event in range(6):
        for stage in range(len(stages)):
            for shift in range(1, stages[stage][1]):
                stat_copy(event, stage, shift).wait_send()
    for n in range(3):
        sum_drain(n)


def unit_sizes(blk, graph):
    share = 8 * blk * graph
    return [-(-rows // share) * share for rows in (2 * UNIT_ROWS, UNIT_ROWS, UNIT_ROWS)]


def assemble(
    traj,
    unit_at,
    state_mid,
    grad_mid,
    units,
    state_out,
    grad_out,
    g_ew1,
    g_eb1,
    g_ew2,
    g_eb2,
    g_nw1,
    g_nb1,
    g_nw2,
    g_nb2,
    sems,
):
    parts = 4
    rows = traj // parts
    copies = []
    for i, (src, dst) in enumerate(((state_mid, state_out), (grad_mid, grad_out))):
        for part in range(parts):
            cut = pl.ds(part * rows, rows)
            copies.append(pltpu.make_async_copy(src.at[cut], dst.at[cut], sems.at[i, part]))
            copies[-1].start()
    for l in range(LAYERS):
        node_at = 0 if l else unit_at[1]
        edge_at = UNIT_ROWS if l else unit_at[2]

        def rows_of(at, start, count):
            return units[pl.ds(at + start, count), :]

        g_nw1[pl.ds(0, 2 * D), l, :] = rows_of(node_at, 0, 2 * D)
        g_nw1[pl.ds(2 * D, NPAR), l, :] = rows_of(node_at, UNIT_AUX + A_THETA, NPAR)
        g_nb1[pl.ds(l, 1), :] = rows_of(node_at, UNIT_AUX + A_ONE, 1)
        g_nw2[l] = rows_of(node_at, 2 * D, D)
        g_nb2[pl.ds(l, 1), :] = rows_of(node_at, UNIT_BIAS, 1)
        g_ew1[pl.ds(0, 2 * D), l, :] = rows_of(edge_at, 0, 2 * D)
        g_ew1[pl.ds(2 * D, TW), l, :] = rows_of(edge_at, UNIT_AUX, TW)
        g_ew1[pl.ds(2 * D + TW, 1), l, :] = rows_of(edge_at, UNIT_AUX + A_PLACE, 1)
        g_ew1[pl.ds(2 * D + TW + 1, NPAR), l, :] = rows_of(edge_at, UNIT_AUX + A_THETA, NPAR)
        g_eb1[pl.ds(l, 1), :] = rows_of(edge_at, UNIT_AUX + A_ONE, 1)
        g_ew2[l] = rows_of(edge_at, 2 * D, D)
        g_eb2[pl.ds(l, 1), :] = rows_of(edge_at, UNIT_BIAS, 1)
    for copy in copies:
        copy.wait()


def on_device(
    blk,
    graph,
    node_state,
    field_window,
    edge_offset,
    pde_id,
    pde_table,
    cotangent,
    edge_w1,
    edge_b1,
    edge_w2,
    edge_b2,
    node_w1,
    node_b1,
    node_w2,
    node_b2,
):
    traj, nodes, _ = node_state.shape
    per = traj // GROUPS
    ext = nodes + 2 * RIM
    field = jnp.transpose(field_window, (2, 0, 1)).reshape(TW * traj, nodes)
    offset = jnp.transpose(edge_offset, (2, 0, 1)).reshape(K * traj, nodes)
    table = jnp.transpose(pde_table, (1, 0))
    ew1 = jnp.transpose(edge_w1, (1, 0, 2))
    nw1 = jnp.transpose(node_w1, (1, 0, 2))
    vmem = pl.BlockSpec(memory_space=pltpu.VMEM)
    smem = pl.BlockSpec(memory_space=pltpu.SMEM)
    stages = digit_stages(blk)
    peers = max([size - 1 for _, size in stages] + [1])
    rows = unit_sizes(blk, graph)
    unit_at = [0, rows[0], rows[0] + rows[1]]
    rows = sum(rows)
    sum_peers = 0
    for position, (_, size) in enumerate(digit_stages(blk, (2, 2, 4))):
        sum_peers += (size * graph if position == 1 else size) - 1

    def f(*shape):
        return pltpu.VMEM(shape, F32)

    def b(*shape):
        return pltpu.VMEM(shape, BF16)

    L = LAYERS
    scratch = [
        b(L, 4 * D, 3 * D),
        b(L, 2 * D, 2 * D),
        b(L, 2 * D, 2 * D),
        b(L, 2 * D, 2 * D),
        b(L, 2 * D, 2 * D),
        b(L, 2 * D, 2 * D),
        b(L, 3 * D, 2 * D),
        b(L, 2 * D, 2 * D),
        f(AUX, 3 * D),
        b(D, K * D),
        f(8 * traj, nodes),
        f(traj, K * nodes, D),
        f(4, AUX, nodes),
        b(L, traj, ext, 2 * D),
        b(traj, ext, D),
        f(L, traj, nodes, D),
        f(L, traj, ext, D),
        f(per, nodes, D),
        f(L, traj, K * nodes, D),
        b(L, traj, nodes, 2 * D),
        b(L, traj, nodes, 2 * D),
        f(L, traj, nodes, D),
        f(L, traj, nodes, D),
        f(traj, nodes, D),
        f(traj, nodes, D),
        f(traj, 2 * RIM, D),
        f(per, nodes, D),
        f(2, K, ext, D),
        b(per, ext, 2 * D),
        b(per, ext, 2 * D),
        f(L, 2 * D, 2 * D),
        f(L, 2 * D, 2 * D),
        f(L, 3 * D, 2 * D),
        f(L, 2 * D, 2 * D),
        f(L, 3 * D, 2 * D),
        f(L, 2, 8, D),
        f(6, len(stages), 4 * per, D),
        f(6, len(stages), peers, 4 * per, D),
        f(6, 4, per, D),
        f(2, 2, traj, RIM, D),
        f(2, 2, traj, RIM, D),
        f(GROUPS, 2, per, RIM, D),
        f(GROUPS, 2, per, RIM, D),
        f(L, GROUPS, 2, per, RIM, D),
        f(L, GROUPS, 2, per, RIM, D),
        f(rows, D),
        f(rows, D),
        pltpu.SemaphoreType.DMA((6, len(stages), peers)),
        pltpu.SemaphoreType.DMA((6, len(stages), peers)),
        pltpu.SemaphoreType.DMA((7, 2)),
        pltpu.SemaphoreType.DMA((7, 2)),
        pltpu.SemaphoreType.DMA((3, 2 * sum_peers)),
        pltpu.SemaphoreType.DMA((3, 2 * sum_peers)),
    ]
    any_space = pl.BlockSpec(memory_space=pl.ANY)
    mid = pl.pallas_call(
        functools.partial(kernel_body, blk, graph),
        out_shape=[
            jax.ShapeDtypeStruct((traj, nodes, D), F32),
            jax.ShapeDtypeStruct((traj, nodes, D), F32),
            jax.ShapeDtypeStruct((rows, D), F32),
        ],
        in_specs=[vmem, vmem, vmem, smem, smem] + [vmem] * 9,
        out_specs=[vmem] * 3,
        scratch_shapes=scratch,
        compiler_params=pltpu.CompilerParams(
            collective_id=0, has_side_effects=True, vmem_limit_bytes=62 * 2**20
        ),
        name="processor",
    )(
        node_state,
        field,
        offset,
        pde_id,
        table,
        cotangent,
        ew1,
        edge_b1,
        edge_w2,
        edge_b2,
        nw1,
        node_b1,
        node_w2,
        node_b2,
    )
    shapes = [
        (traj, nodes, D),
        (traj, nodes, D),
        (EDGE_IN, L, D),
        (L, D),
        (L, D, D),
        (L, D),
        (NODE_IN, L, D),
        (L, D),
        (L, D, D),
        (L, D),
    ]
    out = pl.pallas_call(
        functools.partial(assemble, traj, unit_at),
        out_shape=[jax.ShapeDtypeStruct(shape, F32) for shape in shapes],
        in_specs=[vmem] * 3,
        out_specs=[any_space, any_space] + [vmem] * 8,
        scratch_shapes=[pltpu.SemaphoreType.DMA((2, 4))],
        name="assemble",
    )(*mid)
    out = list(out)
    out[2] = jnp.transpose(out[2], (1, 0, 2))
    out[6] = jnp.transpose(out[6], (1, 0, 2))
    return tuple(out)


def solution(mesh):
    rows = P("graph", "blk", None)
    return jax.shard_map(
        functools.partial(on_device, mesh.shape["blk"], mesh.shape["graph"]),
        mesh=mesh,
        in_specs=(rows, rows, rows, P("graph"), P(), rows) + (P(),) * 8,
        out_specs=(rows, rows) + (P(),) * 8,
        check_vma=False,
    )
```

```python
import functools

import jax
import jax.numpy as jnp
from jax import lax
from jax.experimental import pallas as pl
from jax.experimental.pallas import tpu as pltpu
from jax.sharding import PartitionSpec as P

D = 128
TW = 25
NPAR = 3
K = 6
HALO = 3
NPDE = 8
LAYERS = 2
EDGE_IN = 2 * D + TW + 1 + NPAR
NODE_IN = 2 * D + NPAR
OFFSETS = tuple(o for o in range(-HALO, HALO + 1) if o != 0)

EPSILON = 1e-05
RIM = 8
GROUPS = 4
AUX = 32
A_THETA = TW
A_ONE = TW + NPAR
A_PLACE = TW + NPAR + 1
UNIT_AUX = 3 * D
UNIT_BIAS = UNIT_AUX + AUX
UNIT_ROWS = UNIT_BIAS + 8

F32 = jnp.float32
BF16 = jnp.bfloat16
MESH = pl.DeviceIdType.MESH


def dot(left, right):
    return jnp.dot(left, right, preferred_element_type=F32)


def dot_t(left, right):
    return lax.dot_general(left, right, (((0,), (0,)), ((), ())), preferred_element_type=F32)


def split(value):
    head = value.astype(BF16)
    tail = (value - head.astype(F32)).astype(BF16)
    return head, tail


def pair(value):
    head, tail = split(value)
    return jnp.concatenate([head, tail], 1)


def halves(product):
    return product[:, :D] + product[:, D:]


def doubled(weight):
    both = pair(weight)
    return jnp.concatenate([both, both], 0)


def swish_parts(half):
    t = jnp.tanh(half)
    u = 1.0 + t
    act = half * u
    return act, u + act * (1.0 - t)


def digit_stages(count, sizes=(4,)):
    stages, stride, step = [], 1, 0
    while stride < count:
        size = sizes[min(step, len(sizes) - 1)]
        while count // stride % size:
            size -= 1
        stages.append((stride, size))
        stride *= size
        step += 1
    return stages


class Links:
    def __init__(self, blk, graph):
        self.blk, self.graph = blk, graph
        self.me = lax.axis_index("blk")
        self.mine = lax.axis_index("graph")
        self.stat_stages = digit_stages(blk)
        self.share_stages = [[("blk", 1, 2)], [("blk", 2, 2), ("graph", 1, graph)]]
        self.swap_stages = digit_stages(blk // 4)
        self.swap_stages = [(stride * 4, size) for stride, size in self.swap_stages]

    def ring(self, shift):
        return (self.mine, lax.rem(self.me + shift + self.blk, self.blk))

    def digit_peer(self, stride, size, shift):
        digit = lax.rem(self.me // stride, size)
        other = lax.rem(digit + shift, size)
        return (self.mine, self.me + (other - digit) * stride)

    def share_size(self, stage):
        size = 1
        for _, _, count in self.share_stages[stage]:
            size *= count
        return size

    def share_digit(self, stage):
        value = 0
        for axis, stride, size in self.share_stages[stage]:
            place = self.me if axis == "blk" else self.mine
            value = value * size + lax.rem(place // stride, size)
        return value

    def share_peer(self, stage, shift):
        other = lax.rem(self.share_digit(stage) + shift, self.share_size(stage))
        coords = {"blk": self.me, "graph": self.mine}
        rest = other
        for axis, stride, count in reversed(self.share_stages[stage]):
            place = coords[axis]
            now = lax.rem(place // stride, count)
            coords[axis] = place + (lax.rem(rest, count) - now) * stride
            rest = rest // count
        return (coords["graph"], coords["blk"]), other

    def greeted(self):
        peers = [self.ring(1), self.ring(-1)]
        for stride, size in self.stat_stages + self.swap_stages:
            peers += [self.digit_peer(stride, size, shift) for shift in range(1, size)]
        for stage in range(len(self.share_stages)):
            peers += [self.share_peer(stage, shift)[0] for shift in range(1, self.share_size(stage))]
        return peers


def remote(src, dst, send_sem, recv_sem, device):
    return pltpu.make_async_remote_copy(
        src_ref=src,
        dst_ref=dst,
        send_sem=send_sem,
        recv_sem=recv_sem,
        device_id=device,
        device_id_type=MESH,
    )


def kernel_body(
    blk,
    graph,
    state_hbm,
    field_hbm,
    offset_hbm,
    id_in,
    table_in,
    cot_hbm,
    ew1_hbm,
    eb1,
    ew2_hbm,
    eb2,
    nw1_hbm,
    nb1,
    nw2_hbm,
    nb2,
    state_out,
    grad_out,
    unit_out,
    state_in,
    field_in,
    offset_in,
    ew1,
    ew2,
    nw1,
    nw2,
    w_in,
    w_e2,
    w_e2t,
    w_agg,
    w_n2,
    w_n2t,
    w_np,
    w_ep,
    w_aux,
    spread,
    counts,
    weigh,
    aux_t,
    xs,
    xa,
    a_buf,
    r_buf,
    n_buf,
    slope,
    agg2,
    hid2,
    sn1,
    sn2,
    upd,
    y0,
    yh,
    y1,
    dst,
    dag,
    e1,
    dxh,
    dxl,
    acc_n2,
    acc_agg,
    acc_nx,
    acc_e2,
    acc_x,
    acc_b,
    stat,
    stat_recv,
    fin,
    h0s,
    h0r,
    hs,
    hr,
    rs,
    rr,
    unit,
    unit_recv,
    swap,
    swap_recv,
    unit_all,
    load_sem,
    store_sem,
    stat_ssem,
    stat_rsem,
    rim_ssem,
    rim_rsem,
    sum_ssem,
    sum_rsem,
):
    traj, nodes, _ = state_in.shape
    per = traj // GROUPS
    ext = nodes + 2 * RIM
    total = float(nodes * blk)
    links = Links(blk, graph)
    stages = links.stat_stages

    barrier = pltpu.get_barrier_semaphore()
    greeted = links.greeted()
    for peer in greeted:
        pl.semaphore_signal(barrier, inc=1, device_id=peer, device_id_type=MESH)

    loads = [
        pltpu.make_async_copy(src, to, load_sem.at[i])
        for i, (src, to) in enumerate(
            (
                (offset_hbm, offset_in),
                (field_hbm, field_in),
                (state_hbm, state_in),
                (ew1_hbm, ew1),
                (nw1_hbm, nw1),
                (ew2_hbm, ew2),
                (nw2_hbm, nw2),
                (cot_hbm, dst),
            )
        )
    ]
    for load in loads:
        load.start()

    rows = lax.broadcasted_iota(jnp.int32, (D, K * D), 0)
    cols = lax.broadcasted_iota(jnp.int32, (D, K * D), 1)
    spread[...] = jnp.where(rows == 3 * AUX + cols // D, 1.0, 0.0).astype(BF16)
    aux_t[...] = jnp.zeros_like(aux_t)
    place = lax.broadcasted_iota(jnp.int32, (1, nodes), 1).astype(F32) - nodes / 2
    loads[0].wait()
    offs = [offset_in[pl.ds(k * traj, traj), :] for k in range(K)]
    for i, o in enumerate(OFFSETS):
        many = jnp.zeros((traj, nodes), F32)
        for k in range(K):
            many = many + jnp.where(offs[k] == o, 1.0, 0.0)
        counts[pl.ds(i * traj, traj), :] = many
    counts[pl.ds(K * traj, 2 * traj), :] = jnp.zeros((2 * traj, nodes), F32)
    loads[1].wait()
    loads[2].wait()

    def prepare(j, _):
        for c in range(per):
            t = j * per + c
            tile = aux_t.at[c]
            tile[pl.ds(0, TW), :] = field_in[pl.ds(t, TW, stride=traj), :]
            row = id_in[t]
            for q in range(NPAR):
                tile[pl.ds(A_THETA + q, 1), :] = jnp.full((1, nodes), table_in[q, row], F32)
            tile[pl.ds(A_ONE, 1), :] = jnp.ones((1, nodes), F32)
            tile[pl.ds(A_PLACE, 1), :] = place
            head, tail = split(tile[pl.ds(0, AUX), :])
            head, tail = head.astype(F32), tail.astype(F32)
            full = jnp.concatenate(
                [
                    head,
                    tail,
                    head,
                    counts[pl.ds(t, 8, stride=traj), :],
                    jnp.zeros((D - 3 * AUX - 8, nodes), F32),
                ],
                0,
            )
            back = full.T
            h0s[0, 1, t] = back[:RIM]
            h0s[1, 1, t] = back[nodes - RIM :]
            h0s[0, 0, t] = state_in[t, pl.ds(0, RIM), :]
            h0s[1, 0, t] = state_in[t, pl.ds(nodes - RIM, RIM), :]
            xa[t, pl.ds(0, nodes), :] = back.astype(BF16)
        return 0

    lax.fori_loop(0, GROUPS, prepare, 0)

    pl.semaphore_wait(barrier, len(greeted))

    def rim_copy(kind, send, recv, way):
        return remote(
            send.at[way],
            recv.at[way],
            rim_ssem.at[kind, way],
            rim_rsem.at[kind, way],
            links.ring(1 if way else -1),
        )

    for way in range(2):
        rim_copy(0, h0s, h0r, way).start()

    e1[...] = jnp.zeros_like(e1)
    for acc in (acc_n2, acc_agg, acc_nx, acc_e2, acc_x, acc_b):
        acc[...] = jnp.zeros_like(acc)

    def multiply(j, _):
        for c in range(per):
            t = j * per + c
            many = dot(xa[t, pl.ds(0, nodes), :], spread[...])
            for i in range(K):
                weigh[t, pl.ds(i * nodes, nodes), :] = many[:, i * D : (i + 1) * D]
        return 0

    lax.fori_loop(0, GROUPS, multiply, 0)
    for load in loads[3:]:
        load.wait()
    for l in range(LAYERS):
        w_self = ew1[pl.ds(0, D), l, :]
        w_far = ew1[pl.ds(D, D), l, :]
        n_self = nw1[pl.ds(0, D), l, :]
        n_agg = nw1[pl.ds(D, D), l, :]
        for i, w in enumerate((w_self, w_far, n_self)):
            head, tail = split(0.5 * w)
            cut = pl.ds(i * D, D)
            w_in[l, pl.ds(0, D), cut] = head
            w_in[l, pl.ds(D, D), cut] = head
            w_in[l, pl.ds(2 * D, D), cut] = tail
        w_field = 0.5 * ew1[pl.ds(2 * D, TW), l, :]
        w_place = (0.5 / HALO) * ew1[pl.ds(2 * D + TW, 1), l, :]
        w_theta = 0.5 * ew1[pl.ds(2 * D + TW + 1, NPAR), l, :]
        n_theta = 0.5 * nw1[pl.ds(2 * D, NPAR), l, :]
        w_aux[...] = jnp.zeros_like(w_aux)
        w_aux[pl.ds(0, TW), pl.ds(0, D)] = w_field
        w_aux[pl.ds(0, TW), pl.ds(D, D)] = -w_field
        w_aux[pl.ds(A_THETA, NPAR), pl.ds(0, D)] = w_theta
        w_aux[pl.ds(A_THETA, NPAR), pl.ds(2 * D, D)] = n_theta
        w_aux[pl.ds(A_ONE, 1), pl.ds(0, D)] = 0.5 * eb1[pl.ds(l, 1), :]
        w_aux[pl.ds(A_ONE, 1), pl.ds(2 * D, D)] = 0.5 * nb1[pl.ds(l, 1), :]
        w_aux[pl.ds(A_PLACE, 1), pl.ds(0, D)] = w_place
        w_aux[pl.ds(A_PLACE, 1), pl.ds(D, D)] = -w_place
        head, tail = split(w_aux[...])
        w_in[l, pl.ds(3 * D, AUX), :] = head
        w_in[l, pl.ds(3 * D + AUX, AUX), :] = head
        w_in[l, pl.ds(3 * D + 2 * AUX, AUX), :] = tail
        w_in[l, pl.ds(3 * D + 3 * AUX, AUX), :] = jnp.zeros((AUX, 3 * D), BF16)
        second = 0.5 * ew2[l]
        w_e2[l] = doubled(second)
        w_e2t[l] = doubled(second.T)
        w_agg[l] = doubled(0.5 * n_agg)
        w_n2[l] = doubled(0.5 * nw2[l])
        w_n2t[l] = doubled(nw2[l].T)
        head, tail = split(jnp.concatenate([n_self.T, 0.5 * n_agg.T], 1))
        w_np[l, pl.ds(0, D), :] = head
        w_np[l, pl.ds(D, D), :] = head
        w_np[l, pl.ds(2 * D, D), :] = tail
        w_ep[l, pl.ds(0, D), :] = pair(w_self.T)
        w_ep[l, pl.ds(D, D), :] = pair(w_far.T)

    def stat_copy(event, stage, shift):
        stride, size = stages[stage]
        return remote(
            stat.at[event, stage],
            stat_recv.at[event, stage, shift - 1],
            stat_ssem.at[event, stage, shift - 1],
            stat_rsem.at[event, stage, shift - 1],
            links.digit_peer(stride, size, shift),
        )

    def stat_send(event, stage):
        for shift in range(1, stages[stage][1]):
            stat_copy(event, stage, shift).start()

    def stat_merge(event, stage):
        stride, size = stages[stage]
        for shift in range(1, size):
            stat_copy(event, stage, shift).wait_recv()
        parts = [stat.at[event, stage]] + [
            stat_recv.at[event, stage, shift - 1] for shift in range(1, size)
        ]
        m, m2, u, c = [
            [part[pl.ds(q * per, per), :] for part in parts] for q in range(4)
        ]
        mean = sum(m[1:], m[0]) * (1.0 / size)
        gaps = [value - mean for value in m]
        spread2 = sum((gap * gap for gap in gaps[1:]), gaps[0] * gaps[0])
        m2_all = sum(m2[1:], m2[0]) + spread2 * float(nodes * stride)
        u_all = sum(u[1:], u[0])
        c_all = sum(c[1:], c[0])
        for gap, value in zip(gaps, u):
            c_all = c_all + gap * value
        return mean, m2_all, u_all, c_all

    def stat_forward(event):
        for stage in range(1, len(stages)):
            merged = stat_merge(event, stage - 1)
            for q, value in enumerate(merged):
                stat[event, stage, pl.ds(q * per, per), :] = value
            stat_send(event, stage)

    def stat_finish(event, forward):
        mean, m2, u, c = stat_merge(event, len(stages) - 1)
        fin[event, 2] = u * (1.0 / total)
        if forward:
            scale = lax.rsqrt(m2 * (1.0 / total) + EPSILON)
            fin[event, 0] = mean
            fin[event, 1] = scale
            fin[event, 3] = scale * c * (1.0 / total)
        else:
            fin[event, 3] = c * (1.0 / total)

    def rows_of(buf, l, t, start, size):
        return buf[l, pl.ds(t, per), pl.ds(start, size), :].reshape(per * size, buf.shape[-1])

    lane = lax.broadcasted_iota(jnp.int32, (RIM, D), 1)
    moved = jnp.where((lane == A_PLACE) | (lane == 2 * AUX + A_PLACE), float(nodes), 0.0)

    def forward(l, g):
        base = g * per
        event = GROUPS * l + g
        if l > 0:
            before = GROUPS * (l - 1) + g
            stat_finish(before, True)
            for way in range(2):
                rim_copy(1 + g, hs.at[g], hr.at[g], way).wait_recv()
        for c in range(per):
            t = base + c
            if l == 0:
                xs[0, t, pl.ds(0, nodes), :] = pair(state_in[t])
                near = jnp.concatenate([h0r[1, 0, t], h0r[0, 0, t]], 0)
                xs[0, t, pl.ds(nodes, 2 * RIM), :] = pair(near)
                side = jnp.concatenate([h0r[1, 1, t] - moved, h0r[0, 1, t] + moved], 0)
                xa[t, pl.ds(nodes, 2 * RIM), :] = side.astype(BF16)
            else:
                mean = fin[before, 0, pl.ds(c, 1), :]
                scale = fin[before, 1, pl.ds(c, 1), :]
                y = (upd[t] - mean) * scale
                y0[t] = y
                xs[1, t, pl.ds(0, nodes), :] = pair(y)
                near = jnp.concatenate([hr[g, 1, c], hr[g, 0, c]], 0)
                near = (near - mean) * scale
                yh[t] = near
                xs[1, t, pl.ds(nodes, 2 * RIM), :] = pair(near)
        x = rows_of(xs, l, base, 0, ext)
        side = xa[pl.ds(base, per)].reshape(per * ext, D)
        p = dot(x, w_in[l, pl.ds(0, 2 * D), :])
        p = p + dot(jnp.concatenate([x[:, :D], side], 1), w_in[l, pl.ds(2 * D, 2 * D), :])
        for c in range(per):
            at = c * ext
            a_buf[l, base + c] = p[at : at + nodes, :D]
            r_buf[l, base + c, pl.ds(RIM, nodes), :] = p[at : at + nodes, D : 2 * D]
            r_buf[l, base + c, pl.ds(0, RIM), :] = p[at + nodes : at + nodes + RIM, D : 2 * D]
            r_buf[l, base + c, pl.ds(RIM + nodes, RIM), :] = p[
                at + nodes + RIM : at + ext, D : 2 * D
            ]
            n_buf[c] = p[at : at + nodes, 2 * D :]

        bias2 = 0.5 * eb2[pl.ds(l, 1), :]

        def edge(t, s):
            hidden = []
            for o in OFFSETS:
                half = a_buf[l, t] + r_buf[l, t, pl.ds(RIM + o, nodes), :]
                hidden.append(pair(half * (1.0 + jnp.tanh(half))))
            p = dot(jnp.concatenate(hidden, 0), w_e2[l])
            summed = None
            for i in range(K):
                half = halves(p[i * nodes : (i + 1) * nodes]) + bias2
                tanh = jnp.tanh(half)
                scaled = weigh[t, pl.ds(i * nodes, nodes), :] * (1.0 + tanh)
                message = scaled * half
                summed = message if summed is None else summed + message
                slope[l, t, pl.ds(i * nodes, nodes), :] = scaled + message * (1.0 - tanh)
            dag[s] = summed * (1.0 / K)

        def edge_pair(j, _):
            if l == 0:

                @pl.when((j == 1) & (g >= 2))
                def _():
                    stat_forward(event - 2)

            else:

                @pl.when(j == 1)
                def _():
                    stat_forward(event - 2)

            for c in range(2):
                edge(base + 2 * j + c, 2 * j + c)
            return 0

        lax.fori_loop(0, per // 2, edge_pair, 0)

        node2 = 0.5 * nb2[pl.ds(l, 1), :]
        both = pair(dag[...].reshape(per * nodes, D))
        agg2[l, pl.ds(base, per)] = both.reshape(per, nodes, 2 * D)
        half = n_buf[...].reshape(per * nodes, D) + halves(dot(both, w_agg[l]))
        act, rise = swish_parts(half)
        sn1[l, pl.ds(base, per)] = (0.5 * rise).reshape(per, nodes, D)
        both = pair(act)
        hid2[l, pl.ds(base, per)] = both.reshape(per, nodes, 2 * D)
        half = halves(dot(both, w_n2[l])) + node2
        act, rise = swish_parts(half)
        sn2[l, pl.ds(base, per)] = (0.5 * rise).reshape(per, nodes, D)
        last = l == LAYERS - 1
        for c in range(per):
            new = (y0 if l else state_in)[base + c] + act[c * nodes : (c + 1) * nodes]
            (y1 if last else upd)[base + c] = new
            mean = jnp.sum(new, 0, keepdims=True) * (1.0 / nodes)
            gap = new - mean
            stat[event, 0, pl.ds(c, 1), :] = mean
            stat[event, 0, pl.ds(per + c, 1), :] = jnp.sum(gap * gap, 0, keepdims=True)
            if last:
                up = dst[base + c]
                stat[event, 0, pl.ds(2 * per + c, 1), :] = jnp.sum(up, 0, keepdims=True)
                stat[event, 0, pl.ds(3 * per + c, 1), :] = jnp.sum(up * gap, 0, keepdims=True)
            else:
                hs[g, 0, c] = new[:RIM]
                hs[g, 1, c] = new[nodes - RIM :]
        if not last:
            stat[event, 0, pl.ds(2 * per, 2 * per), :] = jnp.zeros((2 * per, D), F32)
        stat_send(event, 0)
        if not last:
            for way in range(2):
                rim_copy(1 + g, hs.at[g], hr.at[g], way).start()
        return 0

    def backward(l, g):
        base = g * per
        last = l == LAYERS - 1
        order = LAYERS if last else LAYERS + 1
        event = GROUPS * order + g
        source = event - GROUPS
        own = GROUPS * l + g
        stat_finish(source, last)
        if not last:
            for way in range(2):
                rim_copy(1 + GROUPS + g, rs.at[1, g], rr.at[1, g], way).wait_recv()
        deltas, firsts = [], []
        for c in range(per):
            t = base + c
            scale = fin[own, 1, pl.ds(c, 1), :]
            mu = fin[source, 2, pl.ds(c, 1), :]
            cross = fin[source, 3, pl.ds(c, 1), :]
            if last:
                up = dst[t]
                y = (y1[t] - fin[own, 0, pl.ds(c, 1), :]) * scale
                y1[t] = y
            else:
                dst[t, pl.ds(0, RIM), :] += rr[1, g, 1, c]
                dst[t, pl.ds(nodes - RIM, RIM), :] += rr[1, g, 0, c]
                up = dst[t]
                y = y0[t]
            delta = scale * (up - mu - y * cross)
            first = delta * sn2[l, t]
            acc_b[l, 0] += jnp.sum(first.reshape(nodes // 8, 8, D), 0)
            deltas.append(delta)
            firsts.append(first)
        if last:
            pltpu.make_async_copy(
                y1.at[pl.ds(base, per)], state_out.at[pl.ds(base, per)], store_sem.at[0, g]
            ).start()
        d2 = pair(jnp.concatenate(firsts, 0))
        x = rows_of(xs, l, base, 0, nodes)
        side = xa[pl.ds(base, per), pl.ds(0, nodes), :].reshape(per * nodes, D)
        size = per * nodes
        acc_n2[l] += dot_t(hid2[l, pl.ds(base, per)].reshape(size, 2 * D), d2)
        d1 = halves(dot(d2, w_n2t[l])) * sn1[l, pl.ds(base, per)].reshape(size, D)
        d1 = pair(d1)
        p = dot(jnp.concatenate([d1, d1[:, :D]], 1), w_np[l])
        for c in range(per):
            at = c * nodes
            dst[base + c] = deltas[c] + p[at : at + nodes, :D]
            dag[c] = p[at : at + nodes, D:] * (1.0 / K)
        acc_agg[l] += dot_t(agg2[l, pl.ds(base, per)].reshape(size, 2 * D), d1)
        acc_nx[l] += dot_t(jnp.concatenate([x, side], 1), d1)

        if not last:
            @pl.when(g == GROUPS - 1)
            def _():
                node_unit(0, unit_part(unit_at[1]))
                sum_step(1, 0)

            @pl.when(g == 2)
            def _():
                sum_step(0, 2)

        def edge(t, s, slot):
            hidden, deltas, rises = [], [], []
            coming = dag[s]
            bias = None
            for i, o in enumerate(OFFSETS):
                half = a_buf[l, t] + r_buf[l, t, pl.ds(RIM + o, nodes), :]
                act, rise = swish_parts(half)
                rises.append(rise)
                hidden.append(pair(act))
                delta = coming * slope[l, t, pl.ds(i * nodes, nodes), :]
                bias = delta if bias is None else bias + delta
                deltas.append(pair(delta))
            d2 = jnp.concatenate(deltas, 0)
            acc_e2[l] += dot_t(jnp.concatenate(hidden, 0), d2)
            acc_b[l, 1] += jnp.sum(bias.reshape(nodes // 8, 8, D), 0)
            p = dot(d2, w_e2t[l])
            near = None
            for i in range(K):
                d1 = halves(p[i * nodes : (i + 1) * nodes]) * rises[i]
                near = d1 if near is None else near + d1
                e1[slot, i, pl.ds(RIM, nodes), :] = d1
            far = None
            left = None
            right = None
            for i, o in enumerate(OFFSETS):
                part = e1[slot, i, pl.ds(RIM - o, nodes), :]
                far = part if far is None else far + part
                if o < 0:
                    part = e1[slot, i, pl.ds(-o, RIM), :]
                    left = part if left is None else left + part
                else:
                    part = e1[slot, i, pl.ds(RIM + nodes - o, RIM), :]
                    right = part if right is None else right + part
            rims = jnp.concatenate([left, right], 0)
            head, tail = split(near)
            head_f, tail_f = split(far)
            head_r, tail_r = split(rims)
            nothing = jnp.zeros((2 * RIM, D), BF16)
            dxh[s, pl.ds(0, nodes), :] = jnp.concatenate([head, head_f], 1)
            dxl[s, pl.ds(0, nodes), :] = jnp.concatenate([tail, tail_f], 1)
            dxh[s, pl.ds(nodes, 2 * RIM), :] = jnp.concatenate([nothing, head_r], 1)
            dxl[s, pl.ds(nodes, 2 * RIM), :] = jnp.concatenate([nothing, tail_r], 1)

        def edge_pair(j, _):
            if last:

                @pl.when(j == 1)
                def _():
                    stat_forward(event - 2)

            else:

                @pl.when((j == 1) & (g < 2))
                def _():
                    stat_forward(event - 2)

                @pl.when((j == 1) & (g == 0))
                def _():
                    sum_step(0, 1)

                @pl.when((j == 1) & (g == GROUPS - 1))
                def _():
                    sum_step(1, 1)

            for c in range(2):
                edge(base + 2 * j + c, 2 * j + c, c)
            return 0

        lax.fori_loop(0, per // 2, edge_pair, 0)

        size = per * ext
        x = rows_of(xs, l, base, 0, ext)
        side = xa[pl.ds(base, per)].reshape(size, D)
        high = dxh[...].reshape(size, 2 * D)
        low = dxl[...].reshape(size, 2 * D)
        p = halves(dot(high, w_ep[l]) + dot(low, w_ep[l]))
        for c in range(per):
            t, at = base + c, c * ext
            new = dst[t] + p[at : at + nodes]
            dst[t] = new
            rims = p[at + nodes : at + ext]
            rs[l, g, 0, c] = rims[:RIM]
            rs[l, g, 1, c] = rims[RIM:]
            if last:
                stat[event, 0, pl.ds(2 * per + c, 1), :] = jnp.sum(
                    new, 0, keepdims=True
                ) + jnp.sum(rims, 0, keepdims=True)
                stat[event, 0, pl.ds(3 * per + c, 1), :] = jnp.sum(
                    new * y0[t], 0, keepdims=True
                ) + jnp.sum(rims * yh[t], 0, keepdims=True)
        inputs = jnp.concatenate([x, side], 1)
        acc_x[l] += dot_t(inputs, high) + dot_t(inputs, low)
        if last:
            stat[event, 0, pl.ds(0, 2 * per), :] = jnp.zeros((2 * per, D), F32)
            stat_send(event, 0)
        for way in range(2):
            rim_copy(
                1 + GROUPS * (2 if not last else 1) + g, rs.at[l, g], rr.at[l, g], way
            ).start()
        return 0

    def quarter(acc, rows):
        return (
            acc[pl.ds(0, rows), pl.ds(0, D)]
            + acc[pl.ds(D, rows), pl.ds(0, D)]
            + acc[pl.ds(0, rows), pl.ds(D, D)]
            + acc[pl.ds(D, rows), pl.ds(D, D)]
        )

    def fold8(value):
        return jnp.sum(value, 0, keepdims=True)

    def node_unit(l, out):
        out[pl.ds(0, D), :] = quarter(acc_nx.at[l], D)
        out[pl.ds(D, D), :] = quarter(acc_agg.at[l], D)
        out[pl.ds(2 * D, D), :] = quarter(acc_n2.at[l], D)
        side = acc_nx[l, pl.ds(2 * D, AUX), :] + acc_nx[l, pl.ds(2 * D + AUX, AUX), :]
        out[pl.ds(UNIT_AUX, AUX), :] = halves(side)
        out[pl.ds(UNIT_BIAS, 1), :] = fold8(acc_b[l, 0])

    def edge_unit(l, out):
        both = acc_x[l, pl.ds(0, D), :] + acc_x[l, pl.ds(D, D), :]
        out[pl.ds(0, D), :] = both[:, :D]
        out[pl.ds(D, D), :] = both[:, D:]
        out[pl.ds(2 * D, D), :] = quarter(acc_e2.at[l], D)
        side = acc_x[l, pl.ds(2 * D, AUX), :] + acc_x[l, pl.ds(2 * D + AUX, AUX), :]
        row = lax.broadcasted_iota(jnp.int32, (AUX, D), 0)
        both = side[:, :D] - side[:, D:]
        out[pl.ds(UNIT_AUX, AUX), :] = jnp.where(
            row < TW, both, jnp.where(row == A_PLACE, both * (1.0 / HALO), side[:, :D])
        )
        out[pl.ds(UNIT_BIAS, 1), :] = fold8(acc_b[l, 1])

    unit_rows = unit_sizes(graph)
    unit_at = unit_starts(graph)
    shares = len(links.share_stages)
    swaps = links.swap_stages
    pieces = [1]
    for stage in range(shares):
        pieces.append(pieces[-1] * links.share_size(stage))

    def unit_part(at):
        return unit.at[pl.ds(at, UNIT_ROWS), :]

    def seg_rows(n, stage):
        return unit_rows[n] // pieces[stage]

    def seg(n, stage):
        start = unit_at[n]
        for s in range(stage):
            start = start + links.share_digit(s) * seg_rows(n, s + 1)
        return pl.ds(pl.multiple_of(start, 8), seg_rows(n, stage))

    def peer_seg(n, stage, digit):
        start = unit_at[n]
        for s in range(stage):
            start = start + links.share_digit(s) * seg_rows(n, s + 1)
        rows = seg_rows(n, stage + 1)
        return pl.ds(pl.multiple_of(start + digit * rows, 8), rows)

    def recv_seg(n, stage, shift):
        at = unit_at[n]
        for s in range(stage):
            at += (links.share_size(s) - 1) * seg_rows(n, s + 1)
        rows = seg_rows(n, stage + 1)
        return pl.ds(at + (shift - 1) * rows, rows)

    def share_sem(stage, shift):
        return sum(links.share_size(s) - 1 for s in range(stage)) + shift - 1

    share_sems = share_sem(shares, 1)

    def swap_sem(stage, shift):
        return 2 * share_sems + sum(size - 1 for _, size in swaps[:stage]) + shift - 1

    def swap_seg(n):
        return pl.ds(unit_at[n] // pieces[-1], seg_rows(n, shares))

    def share_copy(n, stage, shift):
        peer, digit = links.share_peer(stage, shift)
        sem = share_sem(stage, shift)
        return remote(
            unit.at[peer_seg(n, stage, digit), :],
            unit_recv.at[recv_seg(n, stage, shift), :],
            sum_ssem.at[n, sem],
            sum_rsem.at[n, sem],
            peer,
        )

    def swap_copy(n, stage, shift):
        stride, size = swaps[stage]
        sem = swap_sem(stage, shift)
        return remote(
            swap.at[stage, swap_seg(n), :],
            swap_recv.at[stage, shift - 1, swap_seg(n), :],
            sum_ssem.at[n, sem],
            sum_rsem.at[n, sem],
            links.digit_peer(stride, size, shift),
        )

    def gather_copy(n, stage, shift, arriving):
        size = links.share_size(stage)
        peer, digit = links.share_peer(stage, size - shift if arriving else shift)
        sem = share_sems + share_sem(stage, shift)
        cut = peer_seg(n, stage, digit) if arriving else seg(n, stage + 1)
        return remote(
            unit_all.at[cut, :],
            unit_all.at[cut, :],
            sum_ssem.at[n, sem],
            sum_rsem.at[n, sem],
            peer,
        )

    steps = 2 * shares + len(swaps)

    def shifts(size):
        return range(1, size)

    def sum_step(n, step):
        done = step - 1
        value = None
        if 0 <= done < shares:
            for shift in shifts(links.share_size(done)):
                share_copy(n, done, shift).wait_recv()
            value = unit[seg(n, done + 1), :]
            for shift in shifts(links.share_size(done)):
                value = value + unit_recv[recv_seg(n, done, shift), :]
        elif 0 <= done < shares + len(swaps):
            stage = done - shares
            size = swaps[stage][1]
            for shift in shifts(size):
                swap_copy(n, stage, shift).wait_recv()
            value = swap[stage, swap_seg(n), :]
            for shift in shifts(size):
                value = value + swap_recv[stage, shift - 1, swap_seg(n), :]
        elif done >= 0:
            stage = steps - 1 - done
            for shift in shifts(links.share_size(stage)):
                gather_copy(n, stage, shift, True).wait_recv()
        if step < shares:
            if value is not None:
                unit[seg(n, step), :] = value
            for shift in shifts(links.share_size(step)):
                share_copy(n, step, shift).start()
        elif step < shares + len(swaps):
            stage = step - shares
            swap[stage, swap_seg(n), :] = value
            for shift in shifts(swaps[stage][1]):
                swap_copy(n, stage, shift).start()
        elif step < steps:
            if value is not None:
                unit_all[seg(n, shares), :] = value
            stage = steps - 1 - step
            for shift in shifts(links.share_size(stage)):
                gather_copy(n, stage, shift, False).start()

    def sum_drain(n):
        for stage in range(shares):
            for shift in shifts(links.share_size(stage)):
                share_copy(n, stage, shift).wait_send()
                gather_copy(n, stage, shift, False).wait_send()
        for stage, (_, size) in enumerate(swaps):
            for shift in shifts(size):
                swap_copy(n, stage, shift).wait_send()

    for way in range(2):
        rim_copy(0, h0s, h0r, way).wait_recv()
    lax.fori_loop(0, GROUPS, lambda g, _: forward(0, g), 0)
    lax.fori_loop(0, GROUPS, lambda g, _: forward(1, g), 0)
    lax.fori_loop(0, GROUPS, lambda g, _: backward(1, g), 0)
    for n, filled in enumerate((2 * UNIT_ROWS, UNIT_ROWS, UNIT_ROWS)):
        left = unit_rows[n] - filled
        if left:
            unit[pl.ds(unit_at[n] + filled, left), :] = jnp.zeros((left, D), F32)
    for at in (0, UNIT_ROWS, unit_at[1], unit_at[2]):
        unit[pl.ds(at + UNIT_ROWS - 8, 8), :] = jnp.zeros((8, D), F32)
    node_unit(1, unit_part(0))
    edge_unit(1, unit_part(UNIT_ROWS))
    sum_step(0, 0)
    lax.fori_loop(0, GROUPS, lambda g, _: backward(0, g), 0)
    edge_unit(0, unit_part(unit_at[2]))
    sum_step(2, 0)
    sum_step(0, 3)
    stores = []
    for g in range(GROUPS):
        for way in range(2):
            rim_copy(1 + 2 * GROUPS + g, rs.at[0, g], rr.at[0, g], way).wait_recv()
        for c in range(per):
            t = g * per + c
            dst[t, pl.ds(0, RIM), :] += rr[0, g, 1, c]
            dst[t, pl.ds(nodes - RIM, RIM), :] += rr[0, g, 0, c]
        cut = pl.ds(g * per, per)
        stores.append(pltpu.make_async_copy(dst.at[cut], grad_out.at[cut], store_sem.at[1, g]))
        stores[-1].start()
    for step in range(1, steps + 1):
        sum_step(2, step)
        if step + 1 <= steps:
            sum_step(1, step + 1)
        if step + 3 <= steps:
            sum_step(0, step + 3)
    stores.append(pltpu.make_async_copy(unit_all, unit_out, store_sem.at[2, 0]))
    stores[-1].start()

    for way in range(2):
        rim_copy(0, h0s, h0r, way).wait_send()
    for g in range(GROUPS):
        for way in range(2):
            rim_copy(1 + g, hs.at[g], hr.at[g], way).wait_send()
            rim_copy(1 + GROUPS + g, rs.at[1, g], rr.at[1, g], way).wait_send()
            rim_copy(1 + 2 * GROUPS + g, rs.at[0, g], rr.at[0, g], way).wait_send()
        cut = pl.ds(g * per, per)
        pltpu.make_async_copy(y1.at[cut], state_out.at[cut], store_sem.at[0, g]).wait()

    def drain(event, _):
        for stage in range(len(stages)):
            for shift in range(1, stages[stage][1]):
                stat_copy(event, stage, shift).wait_send()
        return 0

    lax.fori_loop(0, 3 * GROUPS, drain, 0)
    for n in range(3):
        sum_drain(n)
    for store in stores:
        store.wait()


def unit_sizes(graph):
    share = 8 * 4 * graph
    return [-(-rows // share) * share for rows in (2 * UNIT_ROWS, UNIT_ROWS, UNIT_ROWS)]


def unit_starts(graph):
    sizes = unit_sizes(graph)
    return [0, sizes[0], sizes[0] + sizes[1]]


def assemble(
    traj,
    unit_at,
    state_mid,
    grad_mid,
    units,
    state_out,
    grad_out,
    g_ew1,
    g_eb1,
    g_ew2,
    g_eb2,
    g_nw1,
    g_nb1,
    g_nw2,
    g_nb2,
    sems,
):
    parts = 4
    rows = traj // parts
    copies = []
    for i, (src, dst) in enumerate(((state_mid, state_out), (grad_mid, grad_out))):
        for part in range(parts):
            cut = pl.ds(part * rows, rows)
            copies.append(pltpu.make_async_copy(src.at[cut], dst.at[cut], sems.at[i, part]))
            copies[-1].start()
    for l in range(LAYERS):
        node_at = 0 if l else unit_at[1]
        edge_at = UNIT_ROWS if l else unit_at[2]

        def rows_of(at, start, count):
            return units[pl.ds(at + start, count), :]

        g_nw1[pl.ds(0, 2 * D), l, :] = rows_of(node_at, 0, 2 * D)
        g_nw1[pl.ds(2 * D, NPAR), l, :] = rows_of(node_at, UNIT_AUX + A_THETA, NPAR)
        g_nb1[pl.ds(l, 1), :] = rows_of(node_at, UNIT_AUX + A_ONE, 1)
        g_nw2[l] = rows_of(node_at, 2 * D, D)
        g_nb2[pl.ds(l, 1), :] = rows_of(node_at, UNIT_BIAS, 1)
        g_ew1[pl.ds(0, 2 * D), l, :] = rows_of(edge_at, 0, 2 * D)
        g_ew1[pl.ds(2 * D, TW), l, :] = rows_of(edge_at, UNIT_AUX, TW)
        g_ew1[pl.ds(2 * D + TW, 1), l, :] = rows_of(edge_at, UNIT_AUX + A_PLACE, 1)
        g_ew1[pl.ds(2 * D + TW + 1, NPAR), l, :] = rows_of(edge_at, UNIT_AUX + A_THETA, NPAR)
        g_eb1[pl.ds(l, 1), :] = rows_of(edge_at, UNIT_AUX + A_ONE, 1)
        g_ew2[l] = rows_of(edge_at, 2 * D, D)
        g_eb2[pl.ds(l, 1), :] = rows_of(edge_at, UNIT_BIAS, 1)
    for copy in copies:
        copy.wait()


def on_device(
    blk,
    graph,
    node_state,
    field_window,
    edge_offset,
    pde_id,
    pde_table,
    cotangent,
    edge_w1,
    edge_b1,
    edge_w2,
    edge_b2,
    node_w1,
    node_b1,
    node_w2,
    node_b2,
):
    traj, nodes, _ = node_state.shape
    per = traj // GROUPS
    ext = nodes + 2 * RIM
    field = jnp.transpose(field_window, (2, 0, 1)).reshape(TW * traj, nodes)
    offset = jnp.transpose(edge_offset, (2, 0, 1)).reshape(K * traj, nodes)
    table = jnp.transpose(pde_table, (1, 0))
    ew1 = jnp.transpose(edge_w1, (1, 0, 2))
    nw1 = jnp.transpose(node_w1, (1, 0, 2))
    vmem = pl.BlockSpec(memory_space=pltpu.VMEM)
    smem = pl.BlockSpec(memory_space=pltpu.SMEM)
    any_space = pl.BlockSpec(memory_space=pl.ANY)
    stages = digit_stages(blk)
    peers = max(size - 1 for _, size in stages)
    swaps = digit_stages(blk // 4)
    swap_peers = max([size - 1 for _, size in swaps] + [1])
    sum_sems = 2 * (1 + 2 * graph - 1) + sum(size - 1 for _, size in swaps)
    unit_at = unit_starts(graph)
    rows = sum(unit_sizes(graph))
    pieces = 4 * graph
    events = 3 * GROUPS

    def f(*shape):
        return pltpu.VMEM(shape, F32)

    def b(*shape):
        return pltpu.VMEM(shape, BF16)

    L = LAYERS
    scratch = [
        f(traj, nodes, D),
        f(TW * traj, nodes),
        pltpu.VMEM((K * traj, nodes), jnp.int32),
        f(EDGE_IN, L, D),
        f(L, D, D),
        f(NODE_IN, L, D),
        f(L, D, D),
        b(L, 4 * D, 3 * D),
        b(L, 2 * D, 2 * D),
        b(L, 2 * D, 2 * D),
        b(L, 2 * D, 2 * D),
        b(L, 2 * D, 2 * D),
        b(L, 2 * D, 2 * D),
        b(L, 3 * D, 2 * D),
        b(L, 2 * D, 2 * D),
        f(AUX, 3 * D),
        b(D, K * D),
        f(8 * traj, nodes),
        f(traj, K * nodes, D),
        f(per, AUX, nodes),
        b(L, traj, ext, 2 * D),
        b(traj, ext, D),
        f(L, traj, nodes, D),
        f(L, traj, ext, D),
        f(per, nodes, D),
        f(L, traj, K * nodes, D),
        b(L, traj, nodes, 2 * D),
        b(L, traj, nodes, 2 * D),
        f(L, traj, nodes, D),
        f(L, traj, nodes, D),
        f(traj, nodes, D),
        f(traj, nodes, D),
        f(traj, 2 * RIM, D),
        f(traj, nodes, D),
        f(traj, nodes, D),
        f(per, nodes, D),
        f(2, K, ext, D),
        b(per, ext, 2 * D),
        b(per, ext, 2 * D),
        f(L, 2 * D, 2 * D),
        f(L, 2 * D, 2 * D),
        f(L, 3 * D, 2 * D),
        f(L, 2 * D, 2 * D),
        f(L, 3 * D, 2 * D),
        f(L, 2, 8, D),
        f(events, len(stages), 4 * per, D),
        f(events, len(stages), peers, 4 * per, D),
        f(events, 4, per, D),
        f(2, 2, traj, RIM, D),
        f(2, 2, traj, RIM, D),
        f(GROUPS, 2, per, RIM, D),
        f(GROUPS, 2, per, RIM, D),
        f(L, GROUPS, 2, per, RIM, D),
        f(L, GROUPS, 2, per, RIM, D),
        f(rows, D),
        f(rows, D),
        f(len(swaps), rows // pieces, D),
        f(len(swaps), swap_peers, rows // pieces, D),
        f(rows, D),
        pltpu.SemaphoreType.DMA((8,)),
        pltpu.SemaphoreType.DMA((3, GROUPS)),
        pltpu.SemaphoreType.DMA((events, len(stages), peers)),
        pltpu.SemaphoreType.DMA((events, len(stages), peers)),
        pltpu.SemaphoreType.DMA((1 + 3 * GROUPS, 2)),
        pltpu.SemaphoreType.DMA((1 + 3 * GROUPS, 2)),
        pltpu.SemaphoreType.DMA((3, sum_sems)),
        pltpu.SemaphoreType.DMA((3, sum_sems)),
    ]
    hbm = any_space
    mid = pl.pallas_call(
        functools.partial(kernel_body, blk, graph),
        out_shape=[
            jax.ShapeDtypeStruct((traj, nodes, D), F32),
            jax.ShapeDtypeStruct((traj, nodes, D), F32),
            jax.ShapeDtypeStruct((rows, D), F32),
        ],
        in_specs=[hbm, hbm, hbm, smem, smem, hbm, hbm, vmem, hbm, vmem, hbm, vmem, hbm, vmem],
        out_specs=[hbm] * 3,
        scratch_shapes=scratch,
        compiler_params=pltpu.CompilerParams(
            collective_id=0, has_side_effects=True, vmem_limit_bytes=62 * 2**20
        ),
        name="processor",
    )(
        node_state,
        field,
        offset,
        pde_id,
        table,
        cotangent,
        ew1,
        edge_b1,
        edge_w2,
        edge_b2,
        nw1,
        node_b1,
        node_w2,
        node_b2,
    )
    shapes = [
        (traj, nodes, D),
        (traj, nodes, D),
        (EDGE_IN, L, D),
        (L, D),
        (L, D, D),
        (L, D),
        (NODE_IN, L, D),
        (L, D),
        (L, D, D),
        (L, D),
    ]
    out = pl.pallas_call(
        functools.partial(assemble, traj, unit_at),
        out_shape=[jax.ShapeDtypeStruct(shape, F32) for shape in shapes],
        in_specs=[vmem] * 3,
        out_specs=[any_space, any_space] + [vmem] * 8,
        scratch_shapes=[pltpu.SemaphoreType.DMA((2, 4))],
        name="assemble",
    )(*mid)
    out = list(out)
    out[2] = jnp.transpose(out[2], (1, 0, 2))
    out[6] = jnp.transpose(out[6], (1, 0, 2))
    return tuple(out)


def solution(mesh):
    rows = P("graph", "blk", None)
    return jax.shard_map(
        functools.partial(on_device, mesh.shape["blk"], mesh.shape["graph"]),
        mesh=mesh,
        in_specs=(rows, rows, rows, P("graph"), P(), rows) + (P(),) * 8,
        out_specs=(rows, rows) + (P(),) * 8,
        check_vma=False,
    )
```

```python
import functools

import jax
import jax.numpy as jnp
from jax import lax
from jax.experimental import pallas as pl
from jax.experimental.pallas import tpu as pltpu
from jax.sharding import PartitionSpec as P

D = 128
TW = 25
NPAR = 3
K = 6
HALO = 3
NPDE = 8
LAYERS = 2
EDGE_IN = 2 * D + TW + 1 + NPAR
NODE_IN = 2 * D + NPAR
OFFSETS = tuple(o for o in range(-HALO, HALO + 1) if o != 0)

EPSILON = 1e-05
RIM = 8
GROUPS = 4
AUX = 32
A_THETA = TW
A_ONE = TW + NPAR
A_PLACE = TW + NPAR + 1
UNIT_AUX = 3 * D
UNIT_BIAS = UNIT_AUX + AUX
UNIT_ROWS = UNIT_BIAS + 8
STAT_SIZES = (2, 8)
ORDER_NODE = "1012112001020020"
ORDER_EDGES = ""
ORDER_ENTER = "002011220001111"
ORDER_LEAVE = "1020101130001133"
ORDER_BACK = ""
ORDER_BACK_NODE = "2020101222002211011"

F32 = jnp.float32
BF16 = jnp.bfloat16
MESH = pl.DeviceIdType.MESH


def dot(left, right):
    return jnp.dot(left, right, preferred_element_type=F32)


def dot_t(left, right):
    return lax.dot_general(left, right, (((0,), (0,)), ((), ())), preferred_element_type=F32)


def split(value):
    head = value.astype(BF16)
    tail = (value - head.astype(F32)).astype(BF16)
    return head, tail


def pair(value):
    head, tail = split(value)
    return jnp.concatenate([head, tail], 1)


def halves(product):
    return product[:, :D] + product[:, D:]


def doubled(weight):
    both = pair(weight)
    return jnp.concatenate([both, both], 0)


def swish_parts(half):
    t = jnp.tanh(half)
    u = 1.0 + t
    act = half * u
    return act, u + act * (1.0 - t)


def digit_stages(count, sizes):
    stages, stride, step = [], 1, 0
    while stride < count:
        size = sizes[min(step, len(sizes) - 1)]
        while count // stride % size:
            size -= 1
        stages.append((stride, size))
        stride *= size
        step += 1
    return stages


class Links:
    def __init__(self, blk, graph):
        self.blk, self.graph = blk, graph
        self.me = lax.axis_index("blk")
        self.mine = lax.axis_index("graph")
        self.stat_stages = digit_stages(blk, STAT_SIZES)
        self.share_digits = [("blk", 1, 2), ("blk", 2, 2), ("graph", 1, graph)]
        self.shares = 4 * graph
        self.swap_stages = [(stride * 4, size) for stride, size in digit_stages(blk // 4, (4,))]

    def ring(self, shift):
        return (self.mine, lax.rem(self.me + shift + self.blk, self.blk))

    def digit_peer(self, stride, size, shift):
        digit = lax.rem(self.me // stride, size)
        other = lax.rem(digit + shift, size)
        return (self.mine, self.me + (other - digit) * stride)

    def share_digit(self):
        value = 0
        for axis, stride, size in self.share_digits:
            place = self.me if axis == "blk" else self.mine
            value = value * size + lax.rem(place // stride, size)
        return value

    def share_peer(self, shift):
        other = lax.rem(self.share_digit() + shift, self.shares)
        coords = {"blk": self.me, "graph": self.mine}
        rest = other
        for axis, stride, count in reversed(self.share_digits):
            place = coords[axis]
            now = lax.rem(place // stride, count)
            coords[axis] = place + (lax.rem(rest, count) - now) * stride
            rest = rest // count
        return (coords["graph"], coords["blk"]), other

    def greeted(self):
        peers = [self.ring(1), self.ring(-1)]
        for stride, size in self.stat_stages + self.swap_stages:
            peers += [self.digit_peer(stride, size, shift) for shift in range(1, size)]
        peers += [self.share_peer(shift)[0] for shift in range(1, self.shares)]
        return peers


def div(value, by):
    return value // by if isinstance(value, int) else lax.div(value, jnp.int32(by))


def rem(value, by):
    return value % by if isinstance(value, int) else lax.rem(value, jnp.int32(by))


def weave(order, *parts):
    for name in order:
        next(parts[int(name)], None)
    for part in parts:
        for _ in part:
            pass


def remote(src, dst, send_sem, recv_sem, device):
    return pltpu.make_async_remote_copy(
        src_ref=src,
        dst_ref=dst,
        send_sem=send_sem,
        recv_sem=recv_sem,
        device_id=device,
        device_id_type=MESH,
    )


def kernel_body(
    blk,
    graph,
    state_hbm,
    field_hbm,
    offset_hbm,
    id_hbm,
    table_hbm,
    cot_hbm,
    ew1_hbm,
    eb1_hbm,
    ew2_hbm,
    eb2_hbm,
    nw1_hbm,
    nb1_hbm,
    nw2_hbm,
    nb2_hbm,
    raw,
    dst,
    unit_all,
    field_in,
    offset_in,
    id_in,
    table_in,
    ew1,
    eb1,
    ew2,
    eb2,
    nw1,
    nb1,
    nw2,
    nb2,
    w_in,
    w_e2,
    w_e2t,
    w_agg,
    w_n2,
    w_n2t,
    w_np,
    w_ep,
    w_aux,
    spread,
    counts,
    weigh,
    aux_t,
    xs,
    xa,
    a_buf,
    r_buf,
    n_buf,
    slope,
    agg2,
    hid2,
    sn1,
    sn2,
    yh,
    dag,
    e1,
    dxh,
    dxl,
    acc_n2,
    acc_agg,
    acc_nx,
    acc_e2,
    acc_x,
    acc_bn,
    acc_be,
    fin,
    hs,
    hr,
    rs,
    rr,
    unit,
    unit_recv,
    load_sem,
    rim_ssem,
    rim_rsem,
    share_ssem,
    share_rsem,
    *staged,
):
    _, traj, nodes, _ = raw.shape
    state_in = raw.at[0]
    per = traj // GROUPS
    ext = nodes + 2 * RIM
    total = float(nodes * blk)
    links = Links(blk, graph)
    stages = links.stat_stages
    swaps = links.swap_stages
    staged = list(staged)
    stat, stat_recv, stat_ssem, stat_rsem = [
        [staged.pop(0) for _ in stages] for _ in range(4)
    ]
    swap, swap_recv, swap_ssem, swap_rsem = [
        [staged.pop(0) for _ in swaps] for _ in range(4)
    ]

    barrier = pltpu.get_barrier_semaphore()
    greeted = links.greeted()
    for peer in greeted:
        pl.semaphore_signal(barrier, inc=1, device_id=peer, device_id_type=MESH)

    parts = [
        (offset_hbm, offset_in),
        (field_hbm, field_in),
        (id_hbm, id_in),
        (table_hbm, table_in),
        (state_hbm, raw.at[0]),
        (eb1_hbm, eb1),
        (eb2_hbm, eb2),
        (nb1_hbm, nb1),
        (nb2_hbm, nb2),
        (ew2_hbm, ew2),
        (nw2_hbm, nw2),
        (cot_hbm, dst),
    ]
    for l in range(LAYERS):
        parts.append((ew1_hbm.at[:, l, :], ew1.at[l, pl.ds(0, EDGE_IN), :]))
        parts.append((nw1_hbm.at[:, l, :], nw1.at[l, pl.ds(0, NODE_IN), :]))
    loads = [pltpu.make_async_copy(src, to, load_sem.at[i]) for i, (src, to) in enumerate(parts)]
    for load in loads:
        load.start()

    rows = lax.broadcasted_iota(jnp.int32, (D, K * D), 0)
    cols = lax.broadcasted_iota(jnp.int32, (D, K * D), 1)
    spread[...] = jnp.where(rows == 3 * AUX + cols // D, 1.0, 0.0).astype(BF16)
    aux_t[...] = jnp.zeros_like(aux_t)
    place = lax.broadcasted_iota(jnp.int32, (1, nodes), 1).astype(F32) - nodes / 2
    loads[0].wait()
    offs = [offset_in[pl.ds(k * traj, traj), :] for k in range(K)]
    for i, o in enumerate(OFFSETS):
        many = jnp.zeros((traj, nodes), F32)
        for k in range(K):
            many = many + jnp.where(offs[k] == o, 1.0, 0.0)
        counts[pl.ds(i * traj, traj), :] = many
    counts[pl.ds(K * traj, 2 * traj), :] = jnp.zeros((2 * traj, nodes), F32)
    for load in loads[1:5]:
        load.wait()

    near_row = lax.broadcasted_iota(jnp.int32, (RIM, D), 0)

    def prepare(j, _):
        for c in range(per):
            t = j * per + c
            tile = aux_t.at[c]
            tile[pl.ds(0, TW), :] = field_in[pl.ds(t, TW, stride=traj), :]
            row = id_in[t]
            for q in range(NPAR):
                tile[pl.ds(A_THETA + q, 1), :] = jnp.full((1, nodes), table_in[q, row], F32)
            tile[pl.ds(A_ONE, 1), :] = jnp.ones((1, nodes), F32)
            tile[pl.ds(A_PLACE, 1), :] = place
            head, tail = split(tile[pl.ds(0, AUX), :])
            head, tail = head.astype(F32), tail.astype(F32)
            full = jnp.concatenate(
                [
                    head,
                    tail,
                    head,
                    counts[pl.ds(t, 8, stride=traj), :],
                    jnp.zeros((D - 3 * AUX - 8, nodes), F32),
                ],
                0,
            )
            back = full.T
            ahead, behind = raw[0, t, pl.ds(0, RIM), :], raw[0, t, pl.ds(nodes - RIM, RIM), :]
            hs[0, 0, t] = jnp.where(near_row < HALO, ahead, pltpu.roll(back[:RIM], HALO, 0))
            hs[1, 0, t] = jnp.where(
                near_row >= RIM - HALO, behind, pltpu.roll(back[nodes - RIM :], RIM - HALO, 0)
            )
            xa[t, pl.ds(0, nodes), :] = back.astype(BF16)
        return 0

    lax.fori_loop(0, GROUPS, prepare, 0)

    pl.semaphore_wait(barrier, len(greeted))

    def ring_send(src, dst, kind, back=0):
        for way in range(2):
            remote(
                src.at[way],
                dst.at[way],
                rim_ssem.at[back],
                rim_rsem.at[kind],
                links.ring(1 if way else -1),
            ).start()

    def arrived(dst, sem):
        pltpu.make_async_copy(dst, dst, sem).wait()

    first = hs.at[:, 0], hr.at[:, 0]
    ring_send(*first, 0)

    def layer_rims(g):
        cut = pl.ds(g * per, per)
        return hs.at[:, 1, cut], hr.at[:, 1, cut]

    def grad_rims(p):
        cut = pl.ds(rem(p, GROUPS) * per, per)
        back = div(p, GROUPS)
        return rs.at[back, :, cut], rr.at[back + 1, :, cut]

    e1[...] = jnp.zeros_like(e1)
    for acc in (acc_n2, acc_agg, acc_nx, acc_e2, acc_x, acc_bn, acc_be):
        acc[...] = jnp.zeros_like(acc)

    def multiply(j, _):
        for c in range(per):
            t = j * per + c
            many = dot(xa[t, pl.ds(0, nodes), :], spread[...])
            for i in range(K):
                weigh[t, pl.ds(i * nodes, nodes), :] = many[:, i * D : (i + 1) * D]
        return 0

    lax.fori_loop(0, GROUPS, multiply, 0)
    for load in loads[5:]:
        load.wait()
    for l in range(LAYERS):
        w_self = ew1[l, pl.ds(0, D), :]
        w_far = ew1[l, pl.ds(D, D), :]
        n_self = nw1[l, pl.ds(0, D), :]
        n_agg = nw1[l, pl.ds(D, D), :]
        for i, w in enumerate((w_self, w_far, n_self)):
            head, tail = split(0.5 * w)
            cut = pl.ds(i * D, D)
            w_in[l, pl.ds(0, D), cut] = head
            w_in[l, pl.ds(D, D), cut] = head
            w_in[l, pl.ds(2 * D, D), cut] = tail
        w_field = 0.5 * ew1[l, pl.ds(2 * D, TW), :]
        w_place = (0.5 / HALO) * ew1[l, pl.ds(2 * D + TW, 1), :]
        w_theta = 0.5 * ew1[l, pl.ds(2 * D + TW + 1, NPAR), :]
        n_theta = 0.5 * nw1[l, pl.ds(2 * D, NPAR), :]
        w_aux[...] = jnp.zeros_like(w_aux)
        w_aux[pl.ds(0, TW), pl.ds(0, D)] = w_field
        w_aux[pl.ds(0, TW), pl.ds(D, D)] = -w_field
        w_aux[pl.ds(A_THETA, NPAR), pl.ds(0, D)] = w_theta
        w_aux[pl.ds(A_THETA, NPAR), pl.ds(2 * D, D)] = n_theta
        w_aux[pl.ds(A_ONE, 1), pl.ds(0, D)] = 0.5 * eb1[pl.ds(l, 1), :]
        w_aux[pl.ds(A_ONE, 1), pl.ds(2 * D, D)] = 0.5 * nb1[pl.ds(l, 1), :]
        w_aux[pl.ds(A_PLACE, 1), pl.ds(0, D)] = w_place
        w_aux[pl.ds(A_PLACE, 1), pl.ds(D, D)] = -w_place
        head, tail = split(w_aux[...])
        w_in[l, pl.ds(3 * D, AUX), :] = head
        w_in[l, pl.ds(3 * D + AUX, AUX), :] = head
        w_in[l, pl.ds(3 * D + 2 * AUX, AUX), :] = tail
        w_in[l, pl.ds(3 * D + 3 * AUX, AUX), :] = jnp.zeros((AUX, 3 * D), BF16)
        second = 0.5 * ew2[l]
        w_e2[l] = doubled(second)
        w_e2t[l] = doubled(second.T)
        w_agg[l] = doubled(0.5 * n_agg)
        w_n2[l] = doubled(0.5 * nw2[l])
        w_n2t[l] = doubled(nw2[l].T)
        head, tail = split(jnp.concatenate([n_self.T, 0.5 * n_agg.T], 1))
        w_np[l, pl.ds(0, D), :] = head
        w_np[l, pl.ds(D, D), :] = head
        w_np[l, pl.ds(2 * D, D), :] = tail
        w_ep[l, pl.ds(0, D), :] = pair(w_self.T)
        w_ep[l, pl.ds(D, D), :] = pair(w_far.T)

    phases = LAYERS * GROUPS
    kinds = (
        (0, GROUPS, pl.ds(0, 2 * per)),
        (GROUPS, phases, pl.ds(0, 4 * per)),
        (phases, phases + GROUPS, pl.ds(2 * per, 2 * per)),
    )

    def by_kind(event, action):
        for low, high, cut in kinds:
            if isinstance(event, int):
                if low <= event < high:
                    action(cut)
            else:
                pl.when((event >= low) & (event < high))(functools.partial(action, cut))

    def stat_send(event, stage):
        stride, size = stages[stage]

        def send(cut):
            for shift in range(1, size):
                remote(
                    stat[stage].at[event, cut],
                    stat_recv[stage].at[event, shift - 1, cut],
                    stat_ssem[stage].at[0],
                    stat_rsem[stage].at[event],
                    links.digit_peer(stride, size, shift),
                ).start()

        by_kind(event, send)

    def stat_merge(event, stage):
        stride, size = stages[stage]
        by_kind(
            event,
            lambda cut: arrived(stat_recv[stage].at[event, :, cut], stat_rsem[stage].at[event]),
        )
        parts = [stat[stage].at[event]] + [
            stat_recv[stage].at[event, shift - 1] for shift in range(1, size)
        ]
        m, m2, u, c = [[part[pl.ds(q * per, per), :] for part in parts] for q in range(4)]
        mean = sum(m[1:], m[0]) * (1.0 / size)
        gaps = [value - mean for value in m]
        spread2 = sum((gap * gap for gap in gaps[1:]), gaps[0] * gaps[0])
        m2_all = sum(m2[1:], m2[0]) + spread2 * float(nodes * stride)
        u_all = sum(u[1:], u[0])
        c_all = sum(c[1:], c[0])
        for gap, value in zip(gaps, u):
            c_all = c_all + gap * value
        return mean, m2_all, u_all, c_all

    def stat_forward(event):
        for stage in range(1, len(stages)):
            merged = stat_merge(event, stage - 1)
            for q, value in enumerate(merged):
                stat[stage][event, pl.ds(q * per, per), :] = value
            stat_send(event, stage)

    def stat_finish(event):
        mean, m2, u, c = stat_merge(event, len(stages) - 1)
        scale = lax.rsqrt(m2 * (1.0 / total) + EPSILON)
        at = event + GROUPS
        fin[at, 0] = mean
        fin[at, 1] = scale
        fin[at, 2] = u * (1.0 / total)
        fin[at, 3] = jnp.where(event < phases, scale, 1.0) * c * (1.0 / total)

    fin[pl.ds(0, GROUPS), 0] = jnp.zeros((GROUPS, per, D), F32)
    fin[pl.ds(0, GROUPS), 1] = jnp.ones((GROUPS, per, D), F32)
    rr[0] = jnp.zeros(rr.shape[1:], F32)
    for stage in range(len(stages)):
        for low, high, unused in (
            (0, GROUPS, pl.ds(2 * per, 2 * per)),
            (phases, phases + GROUPS, pl.ds(0, 2 * per)),
        ):
            cut = pl.ds(low, high - low)
            stat[stage][cut, unused, :] = jnp.zeros((GROUPS, 2 * per, D), F32)
            arrive = stat_recv[stage]
            arrive[cut, :, unused, :] = jnp.zeros((GROUPS, arrive.shape[1], 2 * per, D), F32)

    def rows_of(buf, l, t, start, size):
        return buf[l, pl.ds(t, per), pl.ds(start, size), :].reshape(per * size, buf.shape[-1])

    def enter(p):
        l, g = div(p, GROUPS), rem(p, GROUPS)
        base = g * per
        slot = rem(p, 2)
        for c in range(per):
            t = base + c
            mean = fin[p, 0, pl.ds(c, 1), :]
            scale = fin[p, 1, pl.ds(c, 1), :]
            xs[l, t, pl.ds(0, nodes), :] = pair((raw[l, t] - mean) * scale)
            near = jnp.concatenate([hr[1, l, t], hr[0, l, t]], 0)
            near = (near - mean) * scale
            yh[t] = near
            xs[l, t, pl.ds(nodes, 2 * RIM), :] = pair(near)
        x = rows_of(xs, l, base, 0, ext)
        side = xa[pl.ds(base, per)].reshape(per * ext, D)
        yield
        p4 = dot(x, w_in[l, pl.ds(0, 2 * D), :])
        p4 = p4 + dot(jnp.concatenate([x[:, :D], side], 1), w_in[l, pl.ds(2 * D, 2 * D), :])
        yield
        for c in range(per):
            at = c * ext
            a_buf[l, base + c] = p4[at : at + nodes, :D]
            r_buf[l, base + c, pl.ds(RIM, nodes), :] = p4[at : at + nodes, D : 2 * D]
            r_buf[l, base + c, pl.ds(0, RIM), :] = p4[at + nodes : at + nodes + RIM, D : 2 * D]
            r_buf[l, base + c, pl.ds(RIM + nodes, RIM), :] = p4[
                at + nodes + RIM : at + ext, D : 2 * D
            ]
            n_buf[slot, c] = p4[at : at + nodes, 2 * D :]
        yield

    def edges(p, s):
        l, g = div(p, GROUPS), rem(p, GROUPS)
        bias2 = 0.5 * eb2[pl.ds(l, 1), :]
        t = g * per + s
        hidden = []
        for i, o in enumerate(OFFSETS):
            half = a_buf[l, t] + r_buf[l, t, pl.ds(RIM + o, nodes), :]
            hidden.append(pair(half * (1.0 + jnp.tanh(half))))
            if i == K // 2 - 1:
                yield
        yield
        product = dot(jnp.concatenate(hidden, 0), w_e2[l])
        yield
        summed = None
        for i in range(K):
            half = halves(product[i * nodes : (i + 1) * nodes]) + bias2
            tanh = jnp.tanh(half)
            scaled = weigh[t, pl.ds(i * nodes, nodes), :] * (1.0 + tanh)
            message = scaled * half
            summed = message if summed is None else summed + message
            slope[l, t, pl.ds(i * nodes, nodes), :] = scaled + message * (1.0 - tanh)
            if i == K // 2 - 1:
                yield
        dag[rem(p, 2), s] = summed * (1.0 / K)
        yield

    def node(p):
        l, g = div(p, GROUPS), rem(p, GROUPS)
        base = g * per
        slot = rem(p, 2)
        node2 = 0.5 * nb2[pl.ds(l, 1), :]
        both = pair(dag[slot].reshape(per * nodes, D))
        agg2[l, pl.ds(base, per)] = both.reshape(per, nodes, 2 * D)
        product = dot(both, w_agg[l])
        yield
        half = n_buf[slot].reshape(per * nodes, D) + halves(product)
        act, rise = swish_parts(half)
        sn1[l, pl.ds(base, per)] = (0.5 * rise).reshape(per, nodes, D)
        both = pair(act)
        hid2[l, pl.ds(base, per)] = both.reshape(per, nodes, 2 * D)
        product = dot(both, w_n2[l])
        yield
        half = halves(product) + node2
        act, rise = swish_parts(half)
        sn2[l, pl.ds(base, per)] = (0.5 * rise).reshape(per, nodes, D)
        for c in range(per):
            t = base + c
            before = (raw[l, t] - fin[p, 0, pl.ds(c, 1), :]) * fin[p, 1, pl.ds(c, 1), :]
            new = before + act[c * nodes : (c + 1) * nodes]
            raw[l + 1, t] = new
            hs[0, 1 + l, t] = new[:RIM]
            hs[1, 1 + l, t] = new[nodes - RIM :]
            mean = jnp.sum(new, 0, keepdims=True) * (1.0 / nodes)
            gap = new - mean
            up = dst[t]
            stat[0][p, pl.ds(c, 1), :] = mean
            stat[0][p, pl.ds(per + c, 1), :] = jnp.sum(gap * gap, 0, keepdims=True)
            stat[0][p, pl.ds(2 * per + c, 1), :] = jnp.sum(up, 0, keepdims=True)
            stat[0][p, pl.ds(3 * per + c, 1), :] = jnp.sum(up * gap, 0, keepdims=True)
            if c % 2:
                yield

    def forward(p, _):
        @pl.when(p > 0)
        def _():
            weave(ORDER_NODE, edges(p, 0), edges(p, 1), node(p - 1))

        @pl.when(p == 0)
        def _():
            weave(ORDER_EDGES, edges(p, 0), edges(p, 1))

        @pl.when(p > 0)
        def _():
            stat_send(p - 1, 0)

        @pl.when((p > 0) & (p <= GROUPS))
        def _():
            ring_send(*layer_rims(p - 1), p)

        def ready():
            stat_finish(p + 1 - GROUPS)
            arrived(layer_rims(p + 1 - GROUPS)[1], rim_rsem.at[p + 2 - GROUPS])

        pl.when((p + 1 > GROUPS) & (p + 1 < phases))(ready)
        alone = (p + 1 == GROUPS) | (p + 1 == phases)

        @pl.when(jnp.logical_not(alone))
        def _():
            weave(ORDER_ENTER, edges(p, 2), edges(p, 3), enter(p + 1))

        @pl.when(alone)
        def _():
            weave(ORDER_EDGES, edges(p, 2), edges(p, 3))

        @pl.when(p + 1 == GROUPS)
        def _():
            ready()
            weave("", enter(p + 1))

        @pl.when(p > 0)
        def _():
            stat_forward(p - 1)

        return 0

    def back_node(p):
        l, g = LAYERS - 1 - div(p, GROUPS), rem(p, GROUPS)
        base = g * per
        source = phases + p
        own = GROUPS * (l + 1) + g
        back = div(p, GROUPS)
        deltas, firsts = [], []
        for c in range(per):
            t = base + c
            scale = fin[own, 1, pl.ds(c, 1), :]
            mu = fin[source, 2, pl.ds(c, 1), :]
            cross = fin[source, 3, pl.ds(c, 1), :]
            y = (raw[l + 1, t] - fin[own, 0, pl.ds(c, 1), :]) * scale
            raw[l + 1, t] = y
            up = dst[t]
            up = jnp.concatenate(
                [
                    up[:RIM] + rr[back, 1, t],
                    up[RIM : nodes - RIM],
                    up[nodes - RIM :] + rr[back, 0, t],
                ],
                0,
            )
            delta = scale * (up - mu - y * cross)
            first = delta * sn2[l, t]
            acc_bn[l] += jnp.sum(first.reshape(nodes // 8, 8, D), 0)
            deltas.append(delta)
            firsts.append(first)
        d2 = pair(jnp.concatenate(firsts, 0))
        yield
        x = rows_of(xs, l, base, 0, nodes)
        side = xa[pl.ds(base, per), pl.ds(0, nodes), :].reshape(per * nodes, D)
        size = per * nodes
        product = dot(d2, w_n2t[l])
        yield
        d1 = halves(product) * sn1[l, pl.ds(base, per)].reshape(size, D)
        d1 = pair(d1)
        product = dot(jnp.concatenate([d1, d1[:, :D]], 1), w_np[l])
        yield
        acc_n2[l] += dot_t(hid2[l, pl.ds(base, per)].reshape(size, 2 * D), d2)
        yield
        for c in range(per):
            at = c * nodes
            dst[base + c] = deltas[c] + product[at : at + nodes, :D]
            dag[rem(p, 2), c] = product[at : at + nodes, D:] * (1.0 / K)
        acc_agg[l] += dot_t(agg2[l, pl.ds(base, per)].reshape(size, 2 * D), d1)
        yield
        acc_nx[l] += dot_t(jnp.concatenate([x, side], 1), d1)
        yield

    def back_edges(p, s):
        l, g = LAYERS - 1 - div(p, GROUPS), rem(p, GROUPS)
        slot = rem(p, 2)
        t = g * per + s
        mine = e1.at[s % 2]
        hidden, deltas, rises = [], [], []
        coming = dag[slot, s]
        bias = None
        for i, o in enumerate(OFFSETS):
            half = a_buf[l, t] + r_buf[l, t, pl.ds(RIM + o, nodes), :]
            act, rise = swish_parts(half)
            rises.append(rise)
            hidden.append(pair(act))
            delta = coming * slope[l, t, pl.ds(i * nodes, nodes), :]
            bias = delta if bias is None else bias + delta
            deltas.append(pair(delta))
            if i == K // 2 - 1:
                yield
        d2 = jnp.concatenate(deltas, 0)
        acc_be[l] += jnp.sum(bias.reshape(nodes // 8, 8, D), 0)
        yield
        product = dot(d2, w_e2t[l])
        yield
        acc_e2[l] += dot_t(jnp.concatenate(hidden, 0), d2)
        yield
        near = None
        for i in range(K):
            d1 = halves(product[i * nodes : (i + 1) * nodes]) * rises[i]
            near = d1 if near is None else near + d1
            mine[i, pl.ds(RIM, nodes), :] = d1
        yield
        far = None
        left = None
        right = None
        for i, o in enumerate(OFFSETS):
            part = mine[i, pl.ds(RIM - o, nodes), :]
            far = part if far is None else far + part
            if o < 0:
                part = mine[i, pl.ds(-o, RIM), :]
                left = part if left is None else left + part
            else:
                part = mine[i, pl.ds(RIM + nodes - o, RIM), :]
                right = part if right is None else right + part
        rims = jnp.concatenate([left, right], 0)
        head, tail = split(near)
        head_f, tail_f = split(far)
        head_r, tail_r = split(rims)
        nothing = jnp.zeros((2 * RIM, D), BF16)
        dxh[slot, s, pl.ds(0, nodes), :] = jnp.concatenate([head, head_f], 1)
        dxl[slot, s, pl.ds(0, nodes), :] = jnp.concatenate([tail, tail_f], 1)
        dxh[slot, s, pl.ds(nodes, 2 * RIM), :] = jnp.concatenate([nothing, head_r], 1)
        dxl[slot, s, pl.ds(nodes, 2 * RIM), :] = jnp.concatenate([nothing, tail_r], 1)
        yield

    def leave_weights(p):
        l, g = LAYERS - 1 - div(p, GROUPS), rem(p, GROUPS)
        base = g * per
        size = per * ext
        slot = rem(p, 2)
        x = rows_of(xs, l, base, 0, ext)
        side = xa[pl.ds(base, per)].reshape(size, D)
        inputs = jnp.concatenate([x, side], 1)
        high = dxh[slot].reshape(size, 2 * D)
        low = dxl[slot].reshape(size, 2 * D)
        acc_x[l] += dot_t(
            jnp.concatenate([inputs, inputs], 0), jnp.concatenate([high, low], 0)
        )
        yield

    def leave_state(p):
        l, g = LAYERS - 1 - div(p, GROUPS), rem(p, GROUPS)
        base = g * per
        size = per * ext
        slot = rem(p, 2)
        event = phases + p
        back = div(p, GROUPS)
        own = GROUPS * l + g
        high = dxh[slot].reshape(size, 2 * D)
        low = dxl[slot].reshape(size, 2 * D)
        product = dot(high, w_ep[l]) + dot(low, w_ep[l])
        yield
        product = halves(product)
        for c in range(per):
            t, at = base + c, c * ext
            new = dst[t] + product[at : at + nodes]
            dst[t] = new
            rims = product[at + nodes : at + ext]
            rs[back, 0, t] = rims[:RIM]
            rs[back, 1, t] = rims[RIM:]
            y = (raw[l, t] - fin[own, 0, pl.ds(c, 1), :]) * fin[own, 1, pl.ds(c, 1), :]
            stat[0][event, pl.ds(2 * per + c, 1), :] = jnp.sum(new, 0, keepdims=True) + jnp.sum(
                rims, 0, keepdims=True
            )
            stat[0][event, pl.ds(3 * per + c, 1), :] = jnp.sum(
                new * y, 0, keepdims=True
            ) + jnp.sum(rims * yh[t], 0, keepdims=True)
            if c % 2:
                yield

    def backward(p, _):
        @pl.when(p > 0)
        def _():
            weave(
                ORDER_LEAVE,
                back_edges(p, 0),
                back_edges(p, 1),
                leave_weights(p - 1),
                leave_state(p - 1),
            )

        @pl.when(p == 0)
        def _():
            weave(ORDER_BACK, back_edges(p, 0), back_edges(p, 1))
            stat_forward(phases - 1)

        @pl.when(p > 0)
        def _():
            ring_send(*grad_rims(p - 1), GROUPS + p, 1)

        @pl.when((p > 0) & (p <= GROUPS))
        def _():
            stat_send(phases + p - 1, 0)

        @pl.when(p == GROUPS)
        def _():
            edge_unit(1, unit.at[1])
            sum_step(1, 0)
            sum_step(0, 1)

        @pl.when(p == phases - 1)
        def _():
            sum_step(0, 3)
            sum_step(1, 2)

        @pl.when(p + 1 < phases)
        def _():
            stat_finish(GROUPS + p + 1)

        @pl.when((p + 1 >= GROUPS) & (p + 1 < phases))
        def _():
            arrived(grad_rims(p + 1 - GROUPS)[1], rim_rsem.at[p + 2])

        @pl.when(p + 1 < phases)
        def _():
            weave(ORDER_BACK_NODE, back_edges(p, 2), back_edges(p, 3), back_node(p + 1))

        @pl.when(p + 1 == phases)
        def _():
            weave(ORDER_BACK, back_edges(p, 2), back_edges(p, 3))

        @pl.when((p > 0) & (p <= GROUPS))
        def _():
            stat_forward(phases + p - 1)

        @pl.when(p == GROUPS - 2)
        def _():
            node_unit(1, unit.at[0])
            sum_step(0, 0)

        @pl.when(p == phases - 3)
        def _():
            sum_step(0, 2)
            sum_step(1, 1)

        @pl.when(p == phases - 2)
        def _():
            node_unit(0, unit.at[2])
            sum_step(2, 0)

        return 0

    def quarter(acc, rows):
        return (
            acc[pl.ds(0, rows), pl.ds(0, D)]
            + acc[pl.ds(D, rows), pl.ds(0, D)]
            + acc[pl.ds(0, rows), pl.ds(D, D)]
            + acc[pl.ds(D, rows), pl.ds(D, D)]
        )

    def fold8(value):
        return jnp.sum(value, 0, keepdims=True)

    def node_unit(l, out):
        out[pl.ds(0, D), :] = quarter(acc_nx.at[l], D)
        out[pl.ds(D, D), :] = quarter(acc_agg.at[l], D)
        out[pl.ds(2 * D, D), :] = quarter(acc_n2.at[l], D)
        side = acc_nx[l, pl.ds(2 * D, AUX), :] + acc_nx[l, pl.ds(2 * D + AUX, AUX), :]
        out[pl.ds(UNIT_AUX, AUX), :] = halves(side)
        out[pl.ds(UNIT_BIAS, 1), :] = fold8(acc_bn[l])

    def edge_unit(l, out):
        both = acc_x[l, pl.ds(0, D), :] + acc_x[l, pl.ds(D, D), :]
        out[pl.ds(0, D), :] = both[:, :D]
        out[pl.ds(D, D), :] = both[:, D:]
        out[pl.ds(2 * D, D), :] = quarter(acc_e2.at[l], D)
        side = acc_x[l, pl.ds(2 * D, AUX), :] + acc_x[l, pl.ds(2 * D + AUX, AUX), :]
        row = lax.broadcasted_iota(jnp.int32, (AUX, D), 0)
        both = side[:, :D] - side[:, D:]
        out[pl.ds(UNIT_AUX, AUX), :] = jnp.where(
            row < TW, both, jnp.where(row == A_PLACE, both * (1.0 / HALO), side[:, :D])
        )
        out[pl.ds(UNIT_BIAS, 1), :] = fold8(acc_be[l])

    shares = links.shares
    seg_rows = unit.shape[1] // shares
    mine = pl.multiple_of(links.share_digit() * seg_rows, 8)
    mine = pl.ds(mine, seg_rows)
    steps = 2 + len(swaps)

    def sum_step(n, step):
        value = None
        if step == 1:
            arrived(unit_recv.at[n], share_rsem.at[n])
            value = unit[n, mine, :]
            for shift in range(1, shares):
                value = value + unit_recv[n, shift - 1]
        elif 1 < step < steps:
            stage = step - 2
            arrived(swap_recv[stage].at[n], swap_rsem[stage].at[n])
            value = swap[stage][n]
            for shift in range(1, swaps[stage][1]):
                value = value + swap_recv[stage][n, shift - 1]
        elif step == steps:
            arrived(unit_recv.at[n], share_rsem.at[4 + n])
        if step == 0:
            for shift in range(1, shares):
                peer, digit = links.share_peer(shift)
                cut = pl.ds(pl.multiple_of(digit * seg_rows, 8), seg_rows)
                remote(
                    unit.at[n, cut],
                    unit_recv.at[n, shift - 1],
                    share_ssem.at[0],
                    share_rsem.at[n],
                    peer,
                ).start()
        elif step < steps - 1:
            stage = step - 1
            swap[stage][n] = value
            stride, size = swaps[stage]
            for shift in range(1, size):
                remote(
                    swap[stage].at[n],
                    swap_recv[stage].at[n, shift - 1],
                    swap_ssem[stage].at[0],
                    swap_rsem[stage].at[n],
                    links.digit_peer(stride, size, shift),
                ).start()
        elif step == steps - 1:
            unit_all[n, mine, :] = value
            for shift in range(1, shares):
                remote(
                    unit_all.at[n, mine],
                    unit_all.at[n, mine],
                    share_ssem.at[1],
                    share_rsem.at[4 + n],
                    links.share_peer(shift)[0],
                ).start()

    rest = unit.shape[1] - UNIT_ROWS + 8
    for n in range(4):
        unit[n, pl.ds(UNIT_ROWS - 8, rest), :] = jnp.zeros((rest, D), F32)
    lane = lax.broadcasted_iota(jnp.int32, (RIM, D), 1)
    moved = jnp.where((lane == A_PLACE) | (lane == 2 * AUX + A_PLACE), float(nodes), 0.0)
    arrived(first[1], rim_rsem.at[0])
    for t in range(traj):
        side = jnp.concatenate(
            [
                pltpu.roll(hr[1, 0, t], HALO, 0) - moved,
                pltpu.roll(hr[0, 0, t], RIM - HALO, 0) + moved,
            ],
            0,
        )
        xa[t, pl.ds(nodes, 2 * RIM), :] = side.astype(BF16)
    weave("", enter(0))
    lax.fori_loop(0, phases, forward, 0)
    weave("", node(phases - 1))
    stat_send(phases - 1, 0)
    stat_finish(GROUPS)
    weave("", back_node(0))
    lax.fori_loop(0, phases, backward, 0)
    weave("", leave_weights(phases - 1))
    edge_unit(0, unit.at[3])
    sum_step(3, 0)
    weave("", leave_state(phases - 1))
    ring_send(*grad_rims(phases - 1), GROUPS + phases, 1)
    sum_step(2, 1)
    sum_step(1, 3)
    sum_step(3, 1)
    for g in range(GROUPS):
        arrived(grad_rims(phases - GROUPS + g)[1], rim_rsem.at[phases + 1 + g])
        for c in range(per):
            t = g * per + c
            dst[t, pl.ds(0, RIM), :] += rr[LAYERS, 1, t]
            dst[t, pl.ds(nodes - RIM, RIM), :] += rr[LAYERS, 0, t]
    for step in range(2, steps + 1):
        sum_step(2, step)
        sum_step(3, step)
    for step in range(4, steps + 1):
        sum_step(0, step)
        sum_step(1, step)

    arrived(hr, rim_ssem.at[0])
    arrived(rs, rim_ssem.at[1])
    for stage in range(len(stages)):
        arrived(stat_recv[stage].at[pl.ds(0, phases)], stat_ssem[stage].at[0])
    for stage in range(len(swaps)):
        arrived(swap_recv[stage], swap_ssem[stage].at[0])
    for way in range(2):
        arrived(unit_recv, share_ssem.at[way])


def unit_size(graph):
    share = 8 * 4 * graph
    return -(-UNIT_ROWS // share) * share


def assemble(
    raw,
    grad_mid,
    units,
    state_out,
    grad_out,
    g_ew1,
    g_eb1,
    g_ew2,
    g_eb2,
    g_nw1,
    g_nb1,
    g_nw2,
    g_nb2,
    sems,
):
    parts = sems.shape[1]
    rows = state_out.shape[0] // parts
    copies = []
    for i, (src, dst) in enumerate(((raw.at[LAYERS], state_out), (grad_mid, grad_out))):
        for part in range(parts):
            cut = pl.ds(part * rows, rows)
            copies.append(pltpu.make_async_copy(src.at[cut], dst.at[cut], sems.at[i, part]))
    for copy in copies:
        copy.start()
    for l in range(LAYERS):
        node, edge = units.at[2 * (LAYERS - 1 - l)], units.at[2 * (LAYERS - 1 - l) + 1]
        g_nw1[pl.ds(0, 2 * D), l, :] = node[pl.ds(0, 2 * D), :]
        g_nw1[pl.ds(2 * D, NPAR), l, :] = node[pl.ds(UNIT_AUX + A_THETA, NPAR), :]
        g_nb1[pl.ds(l, 1), :] = node[pl.ds(UNIT_AUX + A_ONE, 1), :]
        g_nw2[l] = node[pl.ds(2 * D, D), :]
        g_nb2[pl.ds(l, 1), :] = node[pl.ds(UNIT_BIAS, 1), :]
        g_ew1[pl.ds(0, 2 * D), l, :] = edge[pl.ds(0, 2 * D), :]
        g_ew1[pl.ds(2 * D, TW), l, :] = edge[pl.ds(UNIT_AUX, TW), :]
        g_ew1[pl.ds(2 * D + TW, 1), l, :] = edge[pl.ds(UNIT_AUX + A_PLACE, 1), :]
        g_ew1[pl.ds(2 * D + TW + 1, NPAR), l, :] = edge[pl.ds(UNIT_AUX + A_THETA, NPAR), :]
        g_eb1[pl.ds(l, 1), :] = edge[pl.ds(UNIT_AUX + A_ONE, 1), :]
        g_ew2[l] = edge[pl.ds(2 * D, D), :]
        g_eb2[pl.ds(l, 1), :] = edge[pl.ds(UNIT_BIAS, 1), :]
    for copy in copies:
        copy.wait()


def on_device(
    blk,
    graph,
    node_state,
    field_window,
    edge_offset,
    pde_id,
    pde_table,
    cotangent,
    edge_w1,
    edge_b1,
    edge_w2,
    edge_b2,
    node_w1,
    node_b1,
    node_w2,
    node_b2,
):
    traj, nodes, _ = node_state.shape
    per = traj // GROUPS
    ext = nodes + 2 * RIM
    field = jnp.transpose(field_window, (2, 0, 1)).reshape(TW * traj, nodes)
    offset = jnp.transpose(edge_offset, (2, 0, 1)).reshape(K * traj, nodes)
    table = jnp.transpose(pde_table, (1, 0))
    ew1 = jnp.transpose(edge_w1, (1, 0, 2))
    nw1 = jnp.transpose(node_w1, (1, 0, 2))
    vmem = pl.BlockSpec(memory_space=pltpu.VMEM)
    any_space = pl.BlockSpec(memory_space=pl.ANY)
    stages = digit_stages(blk, STAT_SIZES)
    swaps = digit_stages(blk // 4, (4,))
    shares = 4 * graph
    rows = unit_size(graph)
    seg = rows // shares
    events = 3 * GROUPS

    def f(*shape):
        return pltpu.VMEM(shape, F32)

    def b(*shape):
        return pltpu.VMEM(shape, BF16)

    L = LAYERS
    scratch = [
        f(TW * traj, nodes),
        pltpu.VMEM((K * traj, nodes), jnp.int32),
        pltpu.SMEM((traj,), jnp.int32),
        pltpu.SMEM((NPAR, NPDE), F32),
        f(L, -(-EDGE_IN // 8) * 8, D),
        f(L, D),
        f(L, D, D),
        f(L, D),
        f(L, -(-NODE_IN // 8) * 8, D),
        f(L, D),
        f(L, D, D),
        f(L, D),
        b(L, 4 * D, 3 * D),
        b(L, 2 * D, 2 * D),
        b(L, 2 * D, 2 * D),
        b(L, 2 * D, 2 * D),
        b(L, 2 * D, 2 * D),
        b(L, 2 * D, 2 * D),
        b(L, 3 * D, 2 * D),
        b(L, 2 * D, 2 * D),
        f(AUX, 3 * D),
        b(D, K * D),
        f(8 * traj, nodes),
        f(traj, K * nodes, D),
        f(per, AUX, nodes),
        b(L, traj, ext, 2 * D),
        b(traj, ext, D),
        f(L, traj, nodes, D),
        f(L, traj, ext, D),
        f(2, per, nodes, D),
        f(L, traj, K * nodes, D),
        b(L, traj, nodes, 2 * D),
        b(L, traj, nodes, 2 * D),
        f(L, traj, nodes, D),
        f(L, traj, nodes, D),
        f(traj, 2 * RIM, D),
        f(2, per, nodes, D),
        f(2, K, ext, D),
        b(2, per, ext, 2 * D),
        b(2, per, ext, 2 * D),
        f(L, 2 * D, 2 * D),
        f(L, 2 * D, 2 * D),
        f(L, 3 * D, 2 * D),
        f(L, 2 * D, 2 * D),
        f(L, 3 * D, 2 * D),
        f(L, 8, D),
        f(L, 8, D),
        f(events + GROUPS, 4, per, D),
        f(2, 1 + L, traj, RIM, D),
        f(2, 2, traj, RIM, D),
        f(L, 2, traj, RIM, D),
        f(L + 1, 2, traj, RIM, D),
        f(4, rows, D),
        f(4, shares - 1, seg, D),
        pltpu.SemaphoreType.DMA((16,)),
        pltpu.SemaphoreType.DMA((2,)),
        pltpu.SemaphoreType.DMA((1 + 3 * GROUPS,)),
        pltpu.SemaphoreType.DMA((2,)),
        pltpu.SemaphoreType.DMA((8,)),
    ]
    scratch += [f(events + GROUPS, 4 * per, D) for _ in stages]
    scratch += [f(events, size - 1, 4 * per, D) for _, size in stages]
    scratch += [pltpu.SemaphoreType.DMA((1,)) for _ in stages]
    scratch += [pltpu.SemaphoreType.DMA((events,)) for _ in stages]
    scratch += [f(4, seg, D) for _ in swaps]
    scratch += [f(4, size - 1, seg, D) for _, size in swaps]
    scratch += [pltpu.SemaphoreType.DMA((1,)) for _ in swaps]
    scratch += [pltpu.SemaphoreType.DMA((4,)) for _ in swaps]
    hbm = any_space
    mid = pl.pallas_call(
        functools.partial(kernel_body, blk, graph),
        out_shape=[f(L + 1, traj, nodes, D), f(traj, nodes, D), f(4, rows, D)],
        in_specs=[hbm] * 14,
        out_specs=[vmem] * 3,
        scratch_shapes=scratch,
        compiler_params=pltpu.CompilerParams(
            collective_id=0, has_side_effects=True, vmem_limit_bytes=54 * 2**20
        ),
        name="processor",
    )(
        node_state,
        field,
        offset,
        pde_id,
        table,
        cotangent,
        ew1,
        edge_b1,
        edge_w2,
        edge_b2,
        nw1,
        node_b1,
        node_w2,
        node_b2,
    )
    mid = [pltpu.with_memory_space_constraint(part, pltpu.VMEM) for part in mid]
    shapes = [
        (traj, nodes, D),
        (traj, nodes, D),
        (EDGE_IN, L, D),
        (L, D),
        (L, D, D),
        (L, D),
        (NODE_IN, L, D),
        (L, D),
        (L, D, D),
        (L, D),
    ]
    out = pl.pallas_call(
        assemble,
        out_shape=[jax.ShapeDtypeStruct(shape, F32) for shape in shapes],
        in_specs=[vmem] * 3,
        out_specs=[any_space, any_space] + [vmem] * 8,
        scratch_shapes=[pltpu.SemaphoreType.DMA((2, 8))],
        compiler_params=pltpu.CompilerParams(vmem_limit_bytes=8 * 2**20),
        name="assemble",
    )(*mid)
    out = list(out)
    out[2] = jnp.transpose(out[2], (1, 0, 2))
    out[6] = jnp.transpose(out[6], (1, 0, 2))
    return tuple(out)


def solution(mesh):
    rows = P("graph", "blk", None)
    return jax.shard_map(
        functools.partial(on_device, mesh.shape["blk"], mesh.shape["graph"]),
        mesh=mesh,
        in_specs=(rows, rows, rows, P("graph"), P(), rows) + (P(),) * 8,
        out_specs=(rows, rows) + (P(),) * 8,
        check_vma=False,
    )
```

```python
import functools

import jax
import jax.numpy as jnp
from jax import lax
from jax.experimental import pallas as pl
from jax.experimental.pallas import tpu as pltpu
from jax.sharding import PartitionSpec as P

D = 128
TW = 25
NPAR = 3
K = 6
HALO = 3
NPDE = 8
LAYERS = 2
EDGE_IN = 2 * D + TW + 1 + NPAR
NODE_IN = 2 * D + NPAR
OFFSETS = tuple(o for o in range(-HALO, HALO + 1) if o != 0)

EPSILON = 1e-05
RIM = 8
GROUPS = 4
AUX = 32
A_THETA = TW
A_ONE = TW + NPAR
A_PLACE = TW + NPAR + 1
A_SECOND = TW + NPAR + 2
UNIT_FIRST = D
UNIT_AUX = 3 * D
UNIT_ROWS = UNIT_AUX + AUX
STAT_SIZES = (2, 8)
SUMS_MID = ((3, 0, 1), (4, 1, 0), (5, 1, 1), (5, 0, 2), (7, 2, 1), (7, 1, 2))
SUMS_END = ((2, 0, 0), (6, 0, 3), (6, 2, 0))
SUMS_TURNS = ((3, 4, 2, 0), (3, 4, 1), (2, 3, 4, 1, 0))
ORDER_NODE = "1012112001020020"
ORDER_EDGES = ""
ORDER_ENTER = "002011220001111"
ORDER_LEAVE = "1020101130001133"
ORDER_BACK = ""
ORDER_BACK_NODE = "2020101222002211011"

F32 = jnp.float32
BF16 = jnp.bfloat16
MESH = pl.DeviceIdType.MESH


def dot(left, right):
    return jnp.dot(left, right, preferred_element_type=F32)


def dot_t(left, right):
    return lax.dot_general(left, right, (((0,), (0,)), ((), ())), preferred_element_type=F32)


def split(value):
    head = value.astype(BF16)
    tail = (value - head.astype(F32)).astype(BF16)
    return head, tail


def pair(value):
    head, tail = split(value)
    return jnp.concatenate([head, tail], 1)


def halves(product):
    return product[:, :D] + product[:, D:]


def doubled(weight):
    both = pair(weight)
    return jnp.concatenate([both, both], 0)


def swish_parts(half):
    t = jnp.tanh(half)
    u = 1.0 + t
    act = half * u
    return act, u + act * (1.0 - t)


def digit_stages(count, sizes):
    stages, stride, step = [], 1, 0
    while stride < count:
        size = sizes[min(step, len(sizes) - 1)]
        while count // stride % size:
            size -= 1
        stages.append((stride, size))
        stride *= size
        step += 1
    return stages


class Links:
    def __init__(self, blk, graph):
        self.blk, self.graph = blk, graph
        self.me = lax.axis_index("blk")
        self.mine = lax.axis_index("graph")
        self.stat_stages = digit_stages(blk, STAT_SIZES)
        self.share_stages = [[("blk", 1, 2)], [("blk", 2, 2), ("graph", 1, graph)]]
        self.swap_stages = [(stride * 4, size) for stride, size in digit_stages(blk // 4, (4,))]

    def ring(self, shift):
        return (self.mine, lax.rem(self.me + shift + self.blk, self.blk))

    def digit_peer(self, stride, size, shift):
        digit = lax.rem(self.me // stride, size)
        other = lax.rem(digit + shift, size)
        return (self.mine, self.me + (other - digit) * stride)

    def share_size(self, stage):
        size = 1
        for _, _, count in self.share_stages[stage]:
            size *= count
        return size

    def share_digit(self, stage):
        value = 0
        for axis, stride, size in self.share_stages[stage]:
            place = self.me if axis == "blk" else self.mine
            value = value * size + lax.rem(place // stride, size)
        return value

    def share_peer(self, stage, shift):
        other = lax.rem(self.share_digit(stage) + shift, self.share_size(stage))
        coords = {"blk": self.me, "graph": self.mine}
        rest = other
        for axis, stride, count in reversed(self.share_stages[stage]):
            place = coords[axis]
            now = lax.rem(place // stride, count)
            coords[axis] = place + (lax.rem(rest, count) - now) * stride
            rest = rest // count
        return (coords["graph"], coords["blk"]), other

    def greeted(self):
        peers = [self.ring(1), self.ring(-1)]
        for stride, size in self.stat_stages + self.swap_stages:
            peers += [self.digit_peer(stride, size, shift) for shift in range(1, size)]
        for stage in range(len(self.share_stages)):
            peers += [self.share_peer(stage, shift)[0] for shift in range(1, self.share_size(stage))]
        return peers


def div(value, by):
    return value // by if isinstance(value, int) else lax.div(value, jnp.int32(by))


def rem(value, by):
    return value % by if isinstance(value, int) else lax.rem(value, jnp.int32(by))


def weave(order, *parts):
    for name in order:
        next(parts[int(name)], None)
    for part in parts:
        for _ in part:
            pass


def remote(src, dst, send_sem, recv_sem, device):
    return pltpu.make_async_remote_copy(
        src_ref=src,
        dst_ref=dst,
        send_sem=send_sem,
        recv_sem=recv_sem,
        device_id=device,
        device_id_type=MESH,
    )


def kernel_body(
    blk,
    graph,
    state_hbm,
    field_hbm,
    offset_hbm,
    id_hbm,
    table_hbm,
    cot_hbm,
    ew1_hbm,
    eb1_hbm,
    ew2_hbm,
    eb2_hbm,
    nw1_hbm,
    nb1_hbm,
    nw2_hbm,
    nb2_hbm,
    raw,
    dst,
    unit_all,
    field_in,
    offset_in,
    id_in,
    table_in,
    ew1,
    eb1,
    ew2,
    eb2,
    nw1,
    nb1,
    nw2,
    nb2,
    w_in,
    w_e2,
    w_e2t,
    w_agg,
    w_n2,
    w_n2t,
    w_np,
    w_ep,
    w_aux,
    spread,
    counts,
    weigh,
    aux_t,
    xs,
    xa,
    a_buf,
    r_buf,
    n_buf,
    slope,
    agg2,
    hid2,
    sn1,
    sn2,
    yh,
    dag,
    e1,
    dxh,
    dxl,
    acc_n2,
    acc_agg,
    acc_nx,
    acc_e2,
    acc_x,
    acc_bn,
    acc_be,
    fin,
    hs,
    hr,
    rs,
    rr,
    unit,
    load_sem,
    rim_ssem,
    rim_rsem,
    share_ssem,
    share_rsem,
    *staged,
):
    _, traj, nodes, _ = raw.shape
    state_in = raw.at[0]
    per = traj // GROUPS
    ext = nodes + 2 * RIM
    total = float(nodes * blk)
    links = Links(blk, graph)
    stages = links.stat_stages
    phases = LAYERS * GROUPS
    swaps = links.swap_stages
    staged = list(staged)
    stat, stat_recv, stat_ssem, stat_rsem = [
        [staged.pop(0) for _ in stages] for _ in range(4)
    ]
    swap, swap_recv, swap_ssem, swap_rsem = [
        [staged.pop(0) for _ in swaps] for _ in range(4)
    ]
    unit_recv = staged

    barrier = pltpu.get_barrier_semaphore()
    greeted = links.greeted()
    for peer in greeted:
        pl.semaphore_signal(barrier, inc=1, device_id=peer, device_id_type=MESH)

    parts = [
        (offset_hbm, offset_in),
        (field_hbm, field_in),
        (id_hbm, id_in),
        (table_hbm, table_in),
        (state_hbm, raw.at[0]),
        (eb1_hbm, eb1),
        (eb2_hbm, eb2),
        (nb1_hbm, nb1),
        (nb2_hbm, nb2),
        (ew2_hbm, ew2),
        (nw2_hbm, nw2),
        (cot_hbm, dst),
    ]
    for l in range(LAYERS):
        parts.append((ew1_hbm.at[:, l, :], ew1.at[l, pl.ds(0, EDGE_IN), :]))
        parts.append((nw1_hbm.at[:, l, :], nw1.at[l, pl.ds(0, NODE_IN), :]))
    loads = [pltpu.make_async_copy(src, to, load_sem.at[i]) for i, (src, to) in enumerate(parts)]
    for load in loads:
        load.start()

    rows = lax.broadcasted_iota(jnp.int32, (D, K * D), 0)
    cols = lax.broadcasted_iota(jnp.int32, (D, K * D), 1)
    spread[...] = jnp.where(rows == 3 * AUX + cols // D, 1.0, 0.0).astype(BF16)
    aux_t[...] = jnp.zeros_like(aux_t)
    e1[...] = jnp.zeros_like(e1)
    for acc in (acc_n2, acc_agg, acc_nx, acc_e2, acc_x, acc_bn, acc_be):
        acc[...] = jnp.zeros_like(acc)
    for u in range(4):
        rest = unit.shape[1] - UNIT_ROWS
        unit[u, pl.ds(UNIT_ROWS, rest), :] = jnp.zeros((rest, D), F32)
    fin[pl.ds(0, GROUPS), 0] = jnp.zeros((GROUPS, per, D), F32)
    fin[pl.ds(0, GROUPS), 1] = jnp.ones((GROUPS, per, D), F32)
    rr[0] = jnp.zeros(rr.shape[1:], F32)
    for stage in range(len(stages)):
        for low, high, unused in (
            (0, GROUPS, pl.ds(2 * per, 2 * per)),
            (phases, phases + GROUPS, pl.ds(0, 2 * per)),
        ):
            cut = pl.ds(low, high - low)
            stat[stage][cut, unused, :] = jnp.zeros((GROUPS, 2 * per, D), F32)
            arrive = stat_recv[stage]
            arrive[cut, :, unused, :] = jnp.zeros((GROUPS, arrive.shape[1], 2 * per, D), F32)
    place = lax.broadcasted_iota(jnp.int32, (1, nodes), 1).astype(F32) - nodes / 2
    loads[0].wait()
    offs = [offset_in[pl.ds(k * traj, traj), :] for k in range(K)]
    for i, o in enumerate(OFFSETS):
        many = jnp.zeros((traj, nodes), F32)
        for k in range(K):
            many = many + jnp.where(offs[k] == o, 1.0, 0.0)
        counts[pl.ds(i * traj, traj), :] = many
    counts[pl.ds(K * traj, 2 * traj), :] = jnp.zeros((2 * traj, nodes), F32)
    for load in loads[1:5]:
        load.wait()

    near_row = lax.broadcasted_iota(jnp.int32, (RIM, D), 0)

    for t in range(traj):
        tile = aux_t.at[t]
        tile[pl.ds(0, TW), :] = field_in[pl.ds(t, TW, stride=traj), :]
        row = id_in[t]
        for q in range(NPAR):
            tile[pl.ds(A_THETA + q, 1), :] = jnp.full((1, nodes), table_in[q, row], F32)
        tile[pl.ds(A_ONE, 1), :] = jnp.ones((1, nodes), F32)
        tile[pl.ds(A_PLACE, 1), :] = place
    for t in range(traj):
        head, tail = split(aux_t[t])
        head, tail = head.astype(F32), tail.astype(F32)
        full = jnp.concatenate(
            [
                head,
                tail,
                head,
                counts[pl.ds(t, 8, stride=traj), :],
                jnp.zeros((D - 3 * AUX - 8, nodes), F32),
            ],
            0,
        )
        back = full.T
        ahead, behind = raw[0, t, pl.ds(0, RIM), :], raw[0, t, pl.ds(nodes - RIM, RIM), :]
        hs[0, 0, t] = jnp.where(near_row < HALO, ahead, pltpu.roll(back[:RIM], HALO, 0))
        hs[1, 0, t] = jnp.where(
            near_row >= RIM - HALO, behind, pltpu.roll(back[nodes - RIM :], RIM - HALO, 0)
        )
        xa[t, pl.ds(0, nodes), :] = back.astype(BF16)

    pl.semaphore_wait(barrier, len(greeted))

    def ring_send(src, dst, kind, back=0):
        for way in range(2):
            remote(
                src.at[way],
                dst.at[way],
                rim_ssem.at[back],
                rim_rsem.at[kind],
                links.ring(1 if way else -1),
            ).start()

    def arrived(dst, sem):
        pltpu.make_async_copy(dst, dst, sem).wait()

    first = hs.at[:, 0], hr.at[:, 0]
    ring_send(*first, 0)

    def layer_rims(g):
        cut = pl.ds(g * per, per)
        return hs.at[:, 1, cut], hr.at[:, 1, cut]

    def grad_rims(p):
        cut = pl.ds(rem(p, GROUPS) * per, per)
        back = div(p, GROUPS)
        return rs.at[back, :, cut], rr.at[back + 1, :, cut]


    def multiply(j, _):
        for c in range(per):
            t = j * per + c
            many = dot(xa[t, pl.ds(0, nodes), :], spread[...])
            for i in range(K):
                weigh[t, pl.ds(i * nodes, nodes), :] = many[:, i * D : (i + 1) * D]
        return 0

    lax.fori_loop(0, GROUPS, multiply, 0)
    for load in loads[5:]:
        load.wait()
    for l in range(LAYERS):
        w_self = ew1[l, pl.ds(0, D), :]
        w_far = ew1[l, pl.ds(D, D), :]
        n_self = nw1[l, pl.ds(0, D), :]
        n_agg = nw1[l, pl.ds(D, D), :]
        for i, w in enumerate((w_self, w_far, n_self)):
            head, tail = split(0.5 * w)
            cut = pl.ds(i * D, D)
            w_in[l, pl.ds(0, D), cut] = head
            w_in[l, pl.ds(D, D), cut] = head
            w_in[l, pl.ds(2 * D, D), cut] = tail
        w_field = 0.5 * ew1[l, pl.ds(2 * D, TW), :]
        w_place = (0.5 / HALO) * ew1[l, pl.ds(2 * D + TW, 1), :]
        w_theta = 0.5 * ew1[l, pl.ds(2 * D + TW + 1, NPAR), :]
        n_theta = 0.5 * nw1[l, pl.ds(2 * D, NPAR), :]
        w_aux[...] = jnp.zeros_like(w_aux)
        w_aux[pl.ds(0, TW), pl.ds(0, D)] = w_field
        w_aux[pl.ds(0, TW), pl.ds(D, D)] = -w_field
        w_aux[pl.ds(A_THETA, NPAR), pl.ds(0, D)] = w_theta
        w_aux[pl.ds(A_THETA, NPAR), pl.ds(2 * D, D)] = n_theta
        w_aux[pl.ds(A_ONE, 1), pl.ds(0, D)] = 0.5 * eb1[pl.ds(l, 1), :]
        w_aux[pl.ds(A_ONE, 1), pl.ds(2 * D, D)] = 0.5 * nb1[pl.ds(l, 1), :]
        w_aux[pl.ds(A_PLACE, 1), pl.ds(0, D)] = w_place
        w_aux[pl.ds(A_PLACE, 1), pl.ds(D, D)] = -w_place
        head, tail = split(w_aux[...])
        w_in[l, pl.ds(3 * D, AUX), :] = head
        w_in[l, pl.ds(3 * D + AUX, AUX), :] = head
        w_in[l, pl.ds(3 * D + 2 * AUX, AUX), :] = tail
        w_in[l, pl.ds(3 * D + 3 * AUX, AUX), :] = jnp.zeros((AUX, 3 * D), BF16)
        second = 0.5 * ew2[l]
        w_e2[l] = doubled(second)
        w_e2t[l] = doubled(second.T)
        w_agg[l] = doubled(0.5 * n_agg)
        w_n2[l] = doubled(0.5 * nw2[l])
        w_n2t[l] = doubled(nw2[l].T)
        head, tail = split(jnp.concatenate([n_self.T, 0.5 * n_agg.T], 1))
        w_np[l, pl.ds(0, D), :] = head
        w_np[l, pl.ds(D, D), :] = head
        w_np[l, pl.ds(2 * D, D), :] = tail
        w_ep[l, pl.ds(0, D), :] = pair(w_self.T)
        w_ep[l, pl.ds(D, D), :] = pair(w_far.T)

    kinds = (
        (0, GROUPS, pl.ds(0, 2 * per)),
        (GROUPS, phases, pl.ds(0, 4 * per)),
        (phases, phases + GROUPS, pl.ds(2 * per, 2 * per)),
    )

    def by_kind(event, action):
        for low, high, cut in kinds:
            if isinstance(event, int):
                if low <= event < high:
                    action(cut)
            else:
                pl.when((event >= low) & (event < high))(functools.partial(action, cut))

    def stat_send(event, stage):
        stride, size = stages[stage]

        def send(cut):
            for shift in range(1, size):
                remote(
                    stat[stage].at[event, cut],
                    stat_recv[stage].at[event, shift - 1, cut],
                    stat_ssem[stage].at[0],
                    stat_rsem[stage].at[event],
                    links.digit_peer(stride, size, shift),
                ).start()

        by_kind(event, send)

    def stat_merge(event, stage):
        stride, size = stages[stage]
        by_kind(
            event,
            lambda cut: arrived(stat_recv[stage].at[event, :, cut], stat_rsem[stage].at[event]),
        )
        parts = [stat[stage].at[event]] + [
            stat_recv[stage].at[event, shift - 1] for shift in range(1, size)
        ]
        m, m2, u, c = [[part[pl.ds(q * per, per), :] for part in parts] for q in range(4)]
        mean = sum(m[1:], m[0]) * (1.0 / size)
        gaps = [value - mean for value in m]
        spread2 = sum((gap * gap for gap in gaps[1:]), gaps[0] * gaps[0])
        m2_all = sum(m2[1:], m2[0]) + spread2 * float(nodes * stride)
        u_all = sum(u[1:], u[0])
        c_all = sum(c[1:], c[0])
        for gap, value in zip(gaps, u):
            c_all = c_all + gap * value
        return mean, m2_all, u_all, c_all

    def stat_forward(event):
        for stage in range(1, len(stages)):
            merged = stat_merge(event, stage - 1)
            for q, value in enumerate(merged):
                stat[stage][event, pl.ds(q * per, per), :] = value
            stat_send(event, stage)

    def stat_finish(event):
        mean, m2, u, c = stat_merge(event, len(stages) - 1)
        scale = lax.rsqrt(m2 * (1.0 / total) + EPSILON)
        at = event + GROUPS
        fin[at, 0] = mean
        fin[at, 1] = scale
        fin[at, 2] = u * (1.0 / total)
        fin[at, 3] = jnp.where(event < phases, scale, 1.0) * c * (1.0 / total)

    def rows_of(buf, l, t, start, size):
        return buf[l, pl.ds(t, per), pl.ds(start, size), :].reshape(per * size, buf.shape[-1])

    def enter(p):
        l, g = div(p, GROUPS), rem(p, GROUPS)
        base = g * per
        slot = rem(p, 2)
        for c in range(per):
            t = base + c
            mean = fin[p, 0, pl.ds(c, 1), :]
            scale = fin[p, 1, pl.ds(c, 1), :]
            xs[l, t, pl.ds(0, nodes), :] = pair((raw[l, t] - mean) * scale)
            near = jnp.concatenate([hr[1, l, t], hr[0, l, t]], 0)
            near = (near - mean) * scale
            yh[t] = near
            xs[l, t, pl.ds(nodes, 2 * RIM), :] = pair(near)
        x = rows_of(xs, l, base, 0, ext)
        side = xa[pl.ds(base, per)].reshape(per * ext, D)
        yield
        p4 = dot(x, w_in[l, pl.ds(0, 2 * D), :])
        p4 = p4 + dot(jnp.concatenate([x[:, :D], side], 1), w_in[l, pl.ds(2 * D, 2 * D), :])
        yield
        for c in range(per):
            at = c * ext
            a_buf[l, base + c] = p4[at : at + nodes, :D]
            r_buf[l, base + c, pl.ds(RIM, nodes), :] = p4[at : at + nodes, D : 2 * D]
            r_buf[l, base + c, pl.ds(0, RIM), :] = p4[at + nodes : at + nodes + RIM, D : 2 * D]
            r_buf[l, base + c, pl.ds(RIM + nodes, RIM), :] = p4[
                at + nodes + RIM : at + ext, D : 2 * D
            ]
            n_buf[slot, c] = p4[at : at + nodes, 2 * D :]
        yield

    def edges(p, s):
        l, g = div(p, GROUPS), rem(p, GROUPS)
        bias2 = 0.5 * eb2[pl.ds(l, 1), :]
        t = g * per + s
        hidden = []
        for i, o in enumerate(OFFSETS):
            half = a_buf[l, t] + r_buf[l, t, pl.ds(RIM + o, nodes), :]
            hidden.append(pair(half * (1.0 + jnp.tanh(half))))
            if i == K // 2 - 1:
                yield
        yield
        product = dot(jnp.concatenate(hidden, 0), w_e2[l])
        yield
        summed = None
        for i in range(K):
            half = halves(product[i * nodes : (i + 1) * nodes]) + bias2
            tanh = jnp.tanh(half)
            scaled = weigh[t, pl.ds(i * nodes, nodes), :] * (1.0 + tanh)
            message = scaled * half
            summed = message if summed is None else summed + message
            slope[l, t, pl.ds(i * nodes, nodes), :] = scaled + message * (1.0 - tanh)
            if i == K // 2 - 1:
                yield
        dag[rem(p, 2), s] = summed * (1.0 / K)
        yield

    def node(p):
        l, g = div(p, GROUPS), rem(p, GROUPS)
        base = g * per
        slot = rem(p, 2)
        node2 = 0.5 * nb2[pl.ds(l, 1), :]
        both = pair(dag[slot].reshape(per * nodes, D))
        agg2[l, pl.ds(base, per)] = both.reshape(per, nodes, 2 * D)
        product = dot(both, w_agg[l])
        yield
        half = n_buf[slot].reshape(per * nodes, D) + halves(product)
        act, rise = swish_parts(half)
        sn1[l, pl.ds(base, per)] = (0.5 * rise).reshape(per, nodes, D)
        both = pair(act)
        hid2[l, pl.ds(base, per)] = both.reshape(per, nodes, 2 * D)
        product = dot(both, w_n2[l])
        yield
        half = halves(product) + node2
        act, rise = swish_parts(half)
        sn2[l, pl.ds(base, per)] = (0.5 * rise).reshape(per, nodes, D)
        for c in range(per):
            t = base + c
            before = (raw[l, t] - fin[p, 0, pl.ds(c, 1), :]) * fin[p, 1, pl.ds(c, 1), :]
            new = before + act[c * nodes : (c + 1) * nodes]
            raw[l + 1, t] = new
            hs[0, 1 + l, t] = new[:RIM]
            hs[1, 1 + l, t] = new[nodes - RIM :]
            mean = jnp.sum(new, 0, keepdims=True) * (1.0 / nodes)
            gap = new - mean
            up = dst[t]
            stat[0][p, pl.ds(c, 1), :] = mean
            stat[0][p, pl.ds(per + c, 1), :] = jnp.sum(gap * gap, 0, keepdims=True)
            stat[0][p, pl.ds(2 * per + c, 1), :] = jnp.sum(up, 0, keepdims=True)
            stat[0][p, pl.ds(3 * per + c, 1), :] = jnp.sum(up * gap, 0, keepdims=True)
            if c % 2:
                yield

    def forward(p, _):
        @pl.when(p > 0)
        def _():
            weave(ORDER_NODE, edges(p, 0), edges(p, 1), node(p - 1))

        @pl.when(p == 0)
        def _():
            weave(ORDER_EDGES, edges(p, 0), edges(p, 1))

        @pl.when(p > 0)
        def _():
            stat_send(p - 1, 0)

        @pl.when((p > 0) & (p <= GROUPS))
        def _():
            ring_send(*layer_rims(p - 1), p)

        def ready():
            stat_finish(p + 1 - GROUPS)
            arrived(layer_rims(p + 1 - GROUPS)[1], rim_rsem.at[p + 2 - GROUPS])

        pl.when((p + 1 > GROUPS) & (p + 1 < phases))(ready)
        alone = (p + 1 == GROUPS) | (p + 1 == phases)

        @pl.when(jnp.logical_not(alone))
        def _():
            weave(ORDER_ENTER, edges(p, 2), edges(p, 3), enter(p + 1))

        @pl.when(alone)
        def _():
            weave(ORDER_EDGES, edges(p, 2), edges(p, 3))

        @pl.when(p + 1 == GROUPS)
        def _():
            stat_forward(p - 1)
            ready()
            weave("", enter(p + 1))

        @pl.when((p > 0) & (p + 1 != GROUPS))
        def _():
            stat_forward(p - 1)

        return 0

    def back_node(p):
        l, g = LAYERS - 1 - div(p, GROUPS), rem(p, GROUPS)
        base = g * per
        source = phases + p
        own = GROUPS * (l + 1) + g
        back = div(p, GROUPS)
        deltas, firsts = [], []
        for c in range(per):
            t = base + c
            scale = fin[own, 1, pl.ds(c, 1), :]
            mu = fin[source, 2, pl.ds(c, 1), :]
            cross = fin[source, 3, pl.ds(c, 1), :]
            y = (raw[l + 1, t] - fin[own, 0, pl.ds(c, 1), :]) * scale
            raw[l + 1, t] = y
            up = dst[t]
            up = jnp.concatenate(
                [
                    up[:RIM] + rr[back, 1, t],
                    up[RIM : nodes - RIM],
                    up[nodes - RIM :] + rr[back, 0, t],
                ],
                0,
            )
            delta = scale * (up - mu - y * cross)
            first = delta * sn2[l, t]
            acc_bn[l] += jnp.sum(first.reshape(nodes // 8, 8, D), 0)
            deltas.append(delta)
            firsts.append(first)
        d2 = pair(jnp.concatenate(firsts, 0))
        yield
        x = rows_of(xs, l, base, 0, nodes)
        side = xa[pl.ds(base, per), pl.ds(0, nodes), :].reshape(per * nodes, D)
        size = per * nodes
        product = dot(d2, w_n2t[l])
        yield
        d1 = halves(product) * sn1[l, pl.ds(base, per)].reshape(size, D)
        d1 = pair(d1)
        product = dot(jnp.concatenate([d1, d1[:, :D]], 1), w_np[l])
        yield
        acc_n2[l] += dot_t(hid2[l, pl.ds(base, per)].reshape(size, 2 * D), d2)
        yield
        for c in range(per):
            at = c * nodes
            dst[base + c] = deltas[c] + product[at : at + nodes, :D]
            dag[rem(p, 2), c] = product[at : at + nodes, D:] * (1.0 / K)
        acc_agg[l] += dot_t(agg2[l, pl.ds(base, per)].reshape(size, 2 * D), d1)
        yield
        acc_nx[l] += dot_t(jnp.concatenate([x, side], 1), d1)
        yield

    def back_edges(p, s):
        l, g = LAYERS - 1 - div(p, GROUPS), rem(p, GROUPS)
        slot = rem(p, 2)
        t = g * per + s
        mine = e1.at[s % 2]
        hidden, deltas, rises = [], [], []
        coming = dag[slot, s]
        bias = None
        for i, o in enumerate(OFFSETS):
            half = a_buf[l, t] + r_buf[l, t, pl.ds(RIM + o, nodes), :]
            act, rise = swish_parts(half)
            rises.append(rise)
            hidden.append(pair(act))
            delta = coming * slope[l, t, pl.ds(i * nodes, nodes), :]
            bias = delta if bias is None else bias + delta
            deltas.append(pair(delta))
            if i == K // 2 - 1:
                yield
        d2 = jnp.concatenate(deltas, 0)
        acc_be[l] += jnp.sum(bias.reshape(nodes // 8, 8, D), 0)
        yield
        product = dot(d2, w_e2t[l])
        yield
        acc_e2[l] += dot_t(jnp.concatenate(hidden, 0), d2)
        yield
        near = None
        for i in range(K):
            d1 = halves(product[i * nodes : (i + 1) * nodes]) * rises[i]
            near = d1 if near is None else near + d1
            mine[i, pl.ds(RIM, nodes), :] = d1
        yield
        far = None
        left = None
        right = None
        for i, o in enumerate(OFFSETS):
            part = mine[i, pl.ds(RIM - o, nodes), :]
            far = part if far is None else far + part
            if o < 0:
                part = mine[i, pl.ds(-o, RIM), :]
                left = part if left is None else left + part
            else:
                part = mine[i, pl.ds(RIM + nodes - o, RIM), :]
                right = part if right is None else right + part
        rims = jnp.concatenate([left, right], 0)
        head, tail = split(near)
        head_f, tail_f = split(far)
        head_r, tail_r = split(rims)
        nothing = jnp.zeros((2 * RIM, D), BF16)
        dxh[slot, s, pl.ds(0, nodes), :] = jnp.concatenate([head, head_f], 1)
        dxl[slot, s, pl.ds(0, nodes), :] = jnp.concatenate([tail, tail_f], 1)
        dxh[slot, s, pl.ds(nodes, 2 * RIM), :] = jnp.concatenate([nothing, head_r], 1)
        dxl[slot, s, pl.ds(nodes, 2 * RIM), :] = jnp.concatenate([nothing, tail_r], 1)
        yield

    def leave_weights(p):
        l, g = LAYERS - 1 - div(p, GROUPS), rem(p, GROUPS)
        base = g * per
        size = per * ext
        slot = rem(p, 2)
        x = rows_of(xs, l, base, 0, ext)
        side = xa[pl.ds(base, per)].reshape(size, D)
        inputs = jnp.concatenate([x, side], 1)
        high = dxh[slot].reshape(size, 2 * D)
        low = dxl[slot].reshape(size, 2 * D)
        acc_x[l] += dot_t(
            jnp.concatenate([inputs, inputs], 0), jnp.concatenate([high, low], 0)
        )
        yield

    def leave_state(p):
        l, g = LAYERS - 1 - div(p, GROUPS), rem(p, GROUPS)
        base = g * per
        size = per * ext
        slot = rem(p, 2)
        event = phases + p
        back = div(p, GROUPS)
        own = GROUPS * l + g
        high = dxh[slot].reshape(size, 2 * D)
        low = dxl[slot].reshape(size, 2 * D)
        product = dot(high, w_ep[l]) + dot(low, w_ep[l])
        yield
        product = halves(product)
        for c in range(per):
            t, at = base + c, c * ext
            new = dst[t] + product[at : at + nodes]
            dst[t] = new
            rims = product[at + nodes : at + ext]
            rs[back, 0, t] = rims[:RIM]
            rs[back, 1, t] = rims[RIM:]
            y = (raw[l, t] - fin[own, 0, pl.ds(c, 1), :]) * fin[own, 1, pl.ds(c, 1), :]
            stat[0][event, pl.ds(2 * per + c, 1), :] = jnp.sum(new, 0, keepdims=True) + jnp.sum(
                rims, 0, keepdims=True
            )
            stat[0][event, pl.ds(3 * per + c, 1), :] = jnp.sum(
                new * y, 0, keepdims=True
            ) + jnp.sum(rims * yh[t], 0, keepdims=True)
            if c % 2:
                yield

    def backward(p, _):
        @pl.when(p > 0)
        def _():
            weave(
                ORDER_LEAVE,
                back_edges(p, 0),
                back_edges(p, 1),
                leave_weights(p - 1),
                leave_state(p - 1),
            )

        @pl.when(p == 0)
        def _():
            weave(ORDER_BACK, back_edges(p, 0), back_edges(p, 1))
            stat_forward(phases - 1)

        @pl.when(p > 0)
        def _():
            ring_send(*grad_rims(p - 1), GROUPS + p, 1)

        @pl.when((p > 0) & (p <= GROUPS))
        def _():
            stat_send(phases + p - 1, 0)

        @pl.when(p == GROUPS)
        def _():
            unit_second(unit.at[1], acc_e2.at[1])
            edge_unit(1, unit.at[1])

        sum_hook(SUMS_MID, p)

        @pl.when(p + 1 < phases)
        def _():
            stat_finish(GROUPS + p + 1)

        @pl.when((p + 1 >= GROUPS) & (p + 1 < phases))
        def _():
            arrived(grad_rims(p + 1 - GROUPS)[1], rim_rsem.at[p + 2])

        @pl.when(p + 1 < phases)
        def _():
            weave(ORDER_BACK_NODE, back_edges(p, 2), back_edges(p, 3), back_node(p + 1))

        @pl.when(p + 1 == phases)
        def _():
            weave(ORDER_BACK, back_edges(p, 2), back_edges(p, 3))

        @pl.when((p > 0) & (p <= GROUPS))
        def _():
            stat_forward(phases + p - 1)

        @pl.when(p == GROUPS - 2)
        def _():
            node_unit(1, unit.at[0])

        @pl.when(p == phases - 2)
        def _():
            node_unit(0, unit.at[2])

        sum_hook(SUMS_END, p)

        return 0

    def quarter(acc, rows):
        return (
            acc[pl.ds(0, rows), pl.ds(0, D)]
            + acc[pl.ds(D, rows), pl.ds(0, D)]
            + acc[pl.ds(0, rows), pl.ds(D, D)]
            + acc[pl.ds(D, rows), pl.ds(D, D)]
        )

    def fold8(value):
        return jnp.sum(value, 0, keepdims=True)

    def unit_second(out, acc):
        out[pl.ds(0, D), :] = quarter(acc, D)

    def node_unit(l, out):
        unit_second(out, acc_n2.at[l])
        out[pl.ds(UNIT_FIRST, D), :] = quarter(acc_nx.at[l], D)
        out[pl.ds(UNIT_FIRST + D, D), :] = quarter(acc_agg.at[l], D)
        side = acc_nx[l, pl.ds(2 * D, AUX), :] + acc_nx[l, pl.ds(2 * D + AUX, AUX), :]
        out[pl.ds(UNIT_AUX, AUX), :] = halves(side)
        out[pl.ds(UNIT_AUX + A_SECOND, 1), :] = fold8(acc_bn[l])

    def edge_unit(l, out):
        both = acc_x[l, pl.ds(0, D), :] + acc_x[l, pl.ds(D, D), :]
        out[pl.ds(UNIT_FIRST, D), :] = both[:, :D]
        out[pl.ds(UNIT_FIRST + D, D), :] = both[:, D:]
        side = acc_x[l, pl.ds(2 * D, AUX), :] + acc_x[l, pl.ds(2 * D + AUX, AUX), :]
        row = lax.broadcasted_iota(jnp.int32, (AUX, D), 0)
        both = side[:, :D] - side[:, D:]
        out[pl.ds(UNIT_AUX, AUX), :] = jnp.where(
            row < TW, both, jnp.where(row == A_PLACE, both * (1.0 / HALO), side[:, :D])
        )
        out[pl.ds(UNIT_AUX + A_SECOND, 1), :] = fold8(acc_be[l])

    shares = len(links.share_stages)
    pieces = [1]
    for stage in range(shares):
        pieces.append(pieces[-1] * links.share_size(stage))
    lead, unit_rows = unit_sizes(graph)
    sums = (
        (0, 0, unit_rows),
        (1, 0, unit_rows),
        (2, 0, unit_rows),
        (3, 0, lead),
        (3, lead, unit_rows - lead),
    )
    steps = 2 * shares + len(swaps)

    def sum_step(n, step):
        u, start, rows = sums[n]

        def segment(stage, digit=None):
            place = start
            for k in range(stage):
                mine = links.share_digit(k) if digit is None or k < stage - 1 else digit
                place = place + mine * (rows // pieces[k + 1])
            return pl.ds(pl.multiple_of(place, 8), rows // pieces[stage])

        def part(stage):
            return pl.ds(start // pieces[stage], rows // pieces[stage])

        def others(stage):
            return range(1, links.share_size(stage))

        last = part(shares)
        done = step - 1
        value = None
        if 0 <= done < shares:
            into = unit_recv[done].at[u, :, part(done + 1)]
            arrived(into, share_rsem.at[done, n])
            value = unit[u, segment(done + 1), :]
            for shift in others(done):
                value = value + into[shift - 1]
        elif 0 <= done < shares + len(swaps):
            stage = done - shares
            into = swap_recv[stage].at[u, :, last]
            arrived(into, swap_rsem[stage].at[n])
            value = swap[stage][u, last, :]
            for shift in range(1, swaps[stage][1]):
                value = value + into[shift - 1]
        elif done >= 0:
            stage = steps - 1 - done
            arrived(unit_recv[stage].at[u, :, part(stage + 1)], share_rsem.at[shares + stage, n])
        if step < shares:
            if value is not None:
                unit[u, segment(step), :] = value
            for shift in others(step):
                peer, digit = links.share_peer(step, shift)
                remote(
                    unit.at[u, segment(step + 1, digit)],
                    unit_recv[step].at[u, shift - 1, part(step + 1)],
                    share_ssem.at[step],
                    share_rsem.at[step, n],
                    peer,
                ).start()
        elif step < shares + len(swaps):
            stage = step - shares
            swap[stage][u, last, :] = value
            stride, size = swaps[stage]
            for shift in range(1, size):
                remote(
                    swap[stage].at[u, last],
                    swap_recv[stage].at[u, shift - 1, last],
                    swap_ssem[stage].at[0],
                    swap_rsem[stage].at[n],
                    links.digit_peer(stride, size, shift),
                ).start()
        elif step < steps:
            if value is not None:
                unit_all[u, segment(shares), :] = value
            stage = steps - 1 - step
            for shift in others(stage):
                mine = segment(stage + 1)
                remote(
                    unit_all.at[u, mine],
                    unit_all.at[u, mine],
                    share_ssem.at[shares + stage],
                    share_rsem.at[shares + stage, n],
                    links.share_peer(stage, shift)[0],
                ).start()

    def sum_hook(table, p):
        for phase, n, step in table:
            pl.when(p == phase)(functools.partial(sum_step, n, step))

    lane = lax.broadcasted_iota(jnp.int32, (RIM, D), 1)
    moved = jnp.where((lane == A_PLACE) | (lane == 2 * AUX + A_PLACE), float(nodes), 0.0)
    arrived(first[1], rim_rsem.at[0])
    for t in range(traj):
        side = jnp.concatenate(
            [
                pltpu.roll(hr[1, 0, t], HALO, 0) - moved,
                pltpu.roll(hr[0, 0, t], RIM - HALO, 0) + moved,
            ],
            0,
        )
        xa[t, pl.ds(nodes, 2 * RIM), :] = side.astype(BF16)
    weave("", enter(0))
    lax.fori_loop(0, phases, forward, 0)
    weave("", node(phases - 1))
    stat_send(phases - 1, 0)
    stat_finish(GROUPS)
    weave("", back_node(0))
    lax.fori_loop(0, phases, backward, 0)
    unit_second(unit.at[3], acc_e2.at[0])
    sum_step(3, 0)
    weave("", leave_weights(phases - 1))
    edge_unit(0, unit.at[3])
    sum_step(4, 0)
    weave("", leave_state(phases - 1))
    ring_send(*grad_rims(phases - 1), GROUPS + phases, 1)
    done = {n: 0 for n in range(len(sums))}
    for table in (SUMS_MID, SUMS_END):
        for _, n, step in table:
            done[n] = max(done[n], step)
    for turn in range(2 * steps):
        for n in SUMS_TURNS[min(turn, len(SUMS_TURNS) - 1)]:
            if done[n] < steps:
                done[n] += 1
                sum_step(n, done[n])
        if turn:
            continue
        for g in range(GROUPS):
            arrived(grad_rims(phases - GROUPS + g)[1], rim_rsem.at[phases + 1 + g])
            for c in range(per):
                t = g * per + c
                dst[t, pl.ds(0, RIM), :] += rr[LAYERS, 1, t]
                dst[t, pl.ds(nodes - RIM, RIM), :] += rr[LAYERS, 0, t]

    arrived(hr, rim_ssem.at[0])
    arrived(rs, rim_ssem.at[1])
    for stage in range(len(stages)):
        arrived(stat_recv[stage].at[pl.ds(0, phases)], stat_ssem[stage].at[0])
    for stage in range(len(swaps)):
        arrived(swap_recv[stage], swap_ssem[stage].at[0])
    for stage in range(shares):
        for way in range(2):
            arrived(unit_recv[stage], share_ssem.at[way * shares + stage])


def unit_sizes(graph):
    share = 8 * 4 * graph
    lead = -(-UNIT_FIRST // share) * share
    return lead, lead + -(-(UNIT_ROWS - UNIT_FIRST) // share) * share


def assemble(
    raw,
    grad_mid,
    units,
    state_out,
    grad_out,
    g_ew1,
    g_eb1,
    g_ew2,
    g_eb2,
    g_nw1,
    g_nb1,
    g_nw2,
    g_nb2,
    sems,
):
    parts = sems.shape[1]
    rows = state_out.shape[0] // parts
    copies = []
    for i, (src, dst) in enumerate(((raw.at[LAYERS], state_out), (grad_mid, grad_out))):
        for part in range(parts):
            cut = pl.ds(part * rows, rows)
            copies.append(pltpu.make_async_copy(src.at[cut], dst.at[cut], sems.at[i, part]))
    for copy in copies:
        copy.start()
    for l in range(LAYERS):
        node, edge = units.at[2 * (LAYERS - 1 - l)], units.at[2 * (LAYERS - 1 - l) + 1]
        for unit, first, bias1, second, bias2 in (
            (node, g_nw1, g_nb1, g_nw2, g_nb2),
            (edge, g_ew1, g_eb1, g_ew2, g_eb2),
        ):
            first[pl.ds(0, 2 * D), l, :] = unit[pl.ds(UNIT_FIRST, 2 * D), :]
            bias1[pl.ds(l, 1), :] = unit[pl.ds(UNIT_AUX + A_ONE, 1), :]
            second[l] = unit[pl.ds(0, D), :]
            bias2[pl.ds(l, 1), :] = unit[pl.ds(UNIT_AUX + A_SECOND, 1), :]
        g_nw1[pl.ds(2 * D, NPAR), l, :] = node[pl.ds(UNIT_AUX + A_THETA, NPAR), :]
        g_ew1[pl.ds(2 * D, TW), l, :] = edge[pl.ds(UNIT_AUX, TW), :]
        g_ew1[pl.ds(2 * D + TW, 1), l, :] = edge[pl.ds(UNIT_AUX + A_PLACE, 1), :]
        g_ew1[pl.ds(2 * D + TW + 1, NPAR), l, :] = edge[pl.ds(UNIT_AUX + A_THETA, NPAR), :]
    for copy in copies:
        copy.wait()


def on_device(
    blk,
    graph,
    node_state,
    field_window,
    edge_offset,
    pde_id,
    pde_table,
    cotangent,
    edge_w1,
    edge_b1,
    edge_w2,
    edge_b2,
    node_w1,
    node_b1,
    node_w2,
    node_b2,
):
    traj, nodes, _ = node_state.shape
    per = traj // GROUPS
    ext = nodes + 2 * RIM
    field = jnp.transpose(field_window, (2, 0, 1)).reshape(TW * traj, nodes)
    offset = jnp.transpose(edge_offset, (2, 0, 1)).reshape(K * traj, nodes)
    table = jnp.transpose(pde_table, (1, 0))
    ew1 = jnp.transpose(edge_w1, (1, 0, 2))
    nw1 = jnp.transpose(node_w1, (1, 0, 2))
    vmem = pl.BlockSpec(memory_space=pltpu.VMEM)
    any_space = pl.BlockSpec(memory_space=pl.ANY)
    stages = digit_stages(blk, STAT_SIZES)
    swaps = digit_stages(blk // 4, (4,))
    shares = 4 * graph
    _, rows = unit_sizes(graph)
    seg = rows // shares
    events = 3 * GROUPS

    def f(*shape):
        return pltpu.VMEM(shape, F32)

    def b(*shape):
        return pltpu.VMEM(shape, BF16)

    L = LAYERS
    scratch = [
        f(TW * traj, nodes),
        pltpu.VMEM((K * traj, nodes), jnp.int32),
        pltpu.SMEM((traj,), jnp.int32),
        pltpu.SMEM((NPAR, NPDE), F32),
        f(L, -(-EDGE_IN // 8) * 8, D),
        f(L, D),
        f(L, D, D),
        f(L, D),
        f(L, -(-NODE_IN // 8) * 8, D),
        f(L, D),
        f(L, D, D),
        f(L, D),
        b(L, 4 * D, 3 * D),
        b(L, 2 * D, 2 * D),
        b(L, 2 * D, 2 * D),
        b(L, 2 * D, 2 * D),
        b(L, 2 * D, 2 * D),
        b(L, 2 * D, 2 * D),
        b(L, 3 * D, 2 * D),
        b(L, 2 * D, 2 * D),
        f(AUX, 3 * D),
        b(D, K * D),
        f(8 * traj, nodes),
        f(traj, K * nodes, D),
        f(traj, AUX, nodes),
        b(L, traj, ext, 2 * D),
        b(traj, ext, D),
        f(L, traj, nodes, D),
        f(L, traj, ext, D),
        f(2, per, nodes, D),
        f(L, traj, K * nodes, D),
        b(L, traj, nodes, 2 * D),
        b(L, traj, nodes, 2 * D),
        f(L, traj, nodes, D),
        f(L, traj, nodes, D),
        f(traj, 2 * RIM, D),
        f(2, per, nodes, D),
        f(2, K, ext, D),
        b(2, per, ext, 2 * D),
        b(2, per, ext, 2 * D),
        f(L, 2 * D, 2 * D),
        f(L, 2 * D, 2 * D),
        f(L, 3 * D, 2 * D),
        f(L, 2 * D, 2 * D),
        f(L, 3 * D, 2 * D),
        f(L, 8, D),
        f(L, 8, D),
        f(events + GROUPS, 4, per, D),
        f(2, 1 + L, traj, RIM, D),
        f(2, 2, traj, RIM, D),
        f(L, 2, traj, RIM, D),
        f(L + 1, 2, traj, RIM, D),
        f(4, rows, D),
        pltpu.SemaphoreType.DMA((16,)),
        pltpu.SemaphoreType.DMA((2,)),
        pltpu.SemaphoreType.DMA((1 + 3 * GROUPS,)),
        pltpu.SemaphoreType.DMA((4,)),
        pltpu.SemaphoreType.DMA((4, 5)),
    ]
    scratch += [f(events + GROUPS, 4 * per, D) for _ in stages]
    scratch += [f(events, size - 1, 4 * per, D) for _, size in stages]
    scratch += [pltpu.SemaphoreType.DMA((1,)) for _ in stages]
    scratch += [pltpu.SemaphoreType.DMA((events,)) for _ in stages]
    scratch += [f(4, seg, D) for _ in swaps]
    scratch += [f(4, size - 1, seg, D) for _, size in swaps]
    scratch += [pltpu.SemaphoreType.DMA((1,)) for _ in swaps]
    scratch += [pltpu.SemaphoreType.DMA((5,)) for _ in swaps]
    scratch += [f(4, 1, rows // 2, D), f(4, 2 * graph - 1, seg, D)]
    hbm = any_space
    mid = pl.pallas_call(
        functools.partial(kernel_body, blk, graph),
        out_shape=[f(L + 1, traj, nodes, D), f(traj, nodes, D), f(4, rows, D)],
        in_specs=[hbm] * 14,
        out_specs=[vmem] * 3,
        scratch_shapes=scratch,
        compiler_params=pltpu.CompilerParams(
            collective_id=0, has_side_effects=True, vmem_limit_bytes=54 * 2**20
        ),
        name="processor",
    )(
        node_state,
        field,
        offset,
        pde_id,
        table,
        cotangent,
        ew1,
        edge_b1,
        edge_w2,
        edge_b2,
        nw1,
        node_b1,
        node_w2,
        node_b2,
    )
    mid = [pltpu.with_memory_space_constraint(part, pltpu.VMEM) for part in mid]
    shapes = [
        (traj, nodes, D),
        (traj, nodes, D),
        (EDGE_IN, L, D),
        (L, D),
        (L, D, D),
        (L, D),
        (NODE_IN, L, D),
        (L, D),
        (L, D, D),
        (L, D),
    ]
    out = pl.pallas_call(
        assemble,
        out_shape=[jax.ShapeDtypeStruct(shape, F32) for shape in shapes],
        in_specs=[vmem] * 3,
        out_specs=[any_space, any_space] + [vmem] * 8,
        scratch_shapes=[pltpu.SemaphoreType.DMA((2, 8))],
        compiler_params=pltpu.CompilerParams(vmem_limit_bytes=8 * 2**20),
        name="assemble",
    )(*mid)
    out = list(out)
    out[2] = jnp.transpose(out[2], (1, 0, 2))
    out[6] = jnp.transpose(out[6], (1, 0, 2))
    return tuple(out)


def solution(mesh):
    rows = P("graph", "blk", None)
    return jax.shard_map(
        functools.partial(on_device, mesh.shape["blk"], mesh.shape["graph"]),
        mesh=mesh,
        in_specs=(rows, rows, rows, P("graph"), P(), rows) + (P(),) * 8,
        out_specs=(rows, rows) + (P(),) * 8,
        check_vma=False,
    )
```

```python
import functools

import jax
import jax.numpy as jnp
from jax import lax
from jax.experimental import pallas as pl
from jax.experimental.pallas import tpu as pltpu
from jax.sharding import PartitionSpec as P

D = 128
TW = 25
NPAR = 3
K = 6
HALO = 3
NPDE = 8
LAYERS = 2
EDGE_IN = 2 * D + TW + 1 + NPAR
NODE_IN = 2 * D + NPAR
OFFSETS = tuple(o for o in range(-HALO, HALO + 1) if o != 0)

EPSILON = 1e-05
RIM = 8
GROUPS = 4
AUX = 32
A_THETA = TW
A_ONE = TW + NPAR
A_PLACE = TW + NPAR + 1
A_SECOND = TW + NPAR + 2
UNIT_FIRST = D
UNIT_AUX = 3 * D
UNIT_ROWS = UNIT_AUX + AUX
STAT_SIZES = (2, 8)
SUMS_MID = ((3, 0, 1), (4, 1, 0), (5, 1, 1), (5, 0, 2), (7, 2, 1), (7, 1, 2))
SUMS_END = ((2, 0, 0), (6, 0, 3), (6, 2, 0))
SUMS_TURNS = ((3, 4, 2, 0), (3, 4, 1), (2, 3, 4, 1, 0))
ORDER_NODE = "0011000122210012011020"
ORDER_EDGES = ""
ORDER_ENTER = "02002011202000111112"
ORDER_LEAVE = "10000300021013111131"
ORDER_BACK = ""
ORDER_BACK_NODE = "0200201222201222011110110"

F32 = jnp.float32
BF16 = jnp.bfloat16
MESH = pl.DeviceIdType.MESH


def dot(left, right):
    return jnp.dot(left, right, preferred_element_type=F32)


def dot_t(left, right):
    return lax.dot_general(left, right, (((0,), (0,)), ((), ())), preferred_element_type=F32)


def split(value):
    head = value.astype(BF16)
    tail = (value - head.astype(F32)).astype(BF16)
    return head, tail


def pair(value):
    head, tail = split(value)
    return jnp.concatenate([head, tail], 1)


def halves(product):
    return product[:, :D] + product[:, D:]


def doubled(weight):
    both = pair(weight)
    return jnp.concatenate([both, both], 0)


def swish_parts(half):
    t = jnp.tanh(half)
    u = 1.0 + t
    act = half * u
    return act, u + act * (1.0 - t)


def digit_stages(count, sizes):
    stages, stride, step = [], 1, 0
    while stride < count:
        size = sizes[min(step, len(sizes) - 1)]
        while count // stride % size:
            size -= 1
        stages.append((stride, size))
        stride *= size
        step += 1
    return stages


class Links:
    def __init__(self, blk, graph):
        self.blk, self.graph = blk, graph
        self.me = lax.axis_index("blk")
        self.mine = lax.axis_index("graph")
        self.stat_stages = digit_stages(blk, STAT_SIZES)
        self.share_stages = [[("blk", 1, 2)], [("blk", 2, 2), ("graph", 1, graph)]]
        self.swap_stages = [(stride * 4, size) for stride, size in digit_stages(blk // 4, (4,))]

    def ring(self, shift):
        return (self.mine, lax.rem(self.me + shift + self.blk, self.blk))

    def digit_peer(self, stride, size, shift):
        digit = lax.rem(self.me // stride, size)
        other = lax.rem(digit + shift, size)
        return (self.mine, self.me + (other - digit) * stride)

    def share_size(self, stage):
        size = 1
        for _, _, count in self.share_stages[stage]:
            size *= count
        return size

    def share_digit(self, stage):
        value = 0
        for axis, stride, size in self.share_stages[stage]:
            place = self.me if axis == "blk" else self.mine
            value = value * size + lax.rem(place // stride, size)
        return value

    def share_peer(self, stage, shift):
        other = lax.rem(self.share_digit(stage) + shift, self.share_size(stage))
        coords = {"blk": self.me, "graph": self.mine}
        rest = other
        for axis, stride, count in reversed(self.share_stages[stage]):
            place = coords[axis]
            now = lax.rem(place // stride, count)
            coords[axis] = place + (lax.rem(rest, count) - now) * stride
            rest = rest // count
        return (coords["graph"], coords["blk"]), other

    def greeted(self):
        peers = [self.ring(1), self.ring(-1)]
        for stride, size in self.stat_stages + self.swap_stages:
            peers += [self.digit_peer(stride, size, shift) for shift in range(1, size)]
        for stage in range(len(self.share_stages)):
            peers += [self.share_peer(stage, shift)[0] for shift in range(1, self.share_size(stage))]
        return peers


def div(value, by):
    return value // by if isinstance(value, int) else lax.div(value, jnp.int32(by))


def rem(value, by):
    return value % by if isinstance(value, int) else lax.rem(value, jnp.int32(by))


def weave(order, *parts):
    for name in order:
        next(parts[int(name)], None)
    for part in parts:
        for _ in part:
            pass


def remote(src, dst, send_sem, recv_sem, device):
    return pltpu.make_async_remote_copy(
        src_ref=src,
        dst_ref=dst,
        send_sem=send_sem,
        recv_sem=recv_sem,
        device_id=device,
        device_id_type=MESH,
    )


def kernel_body(
    blk,
    graph,
    state_hbm,
    field_hbm,
    offset_hbm,
    id_hbm,
    table_hbm,
    cot_hbm,
    ew1_hbm,
    eb1_hbm,
    ew2_hbm,
    eb2_hbm,
    nw1_hbm,
    nb1_hbm,
    nw2_hbm,
    nb2_hbm,
    raw,
    dst,
    unit_all,
    field_in,
    offset_in,
    id_in,
    table_in,
    ew1,
    eb1,
    ew2,
    eb2,
    nw1,
    nb1,
    nw2,
    nb2,
    w_in,
    w_e2,
    w_e2t,
    w_agg,
    w_n2,
    w_n2t,
    w_np,
    w_ep,
    w_aux,
    spread,
    counts,
    weigh,
    aux_t,
    xs,
    xa,
    a_buf,
    r_buf,
    n_buf,
    slope,
    agg2,
    hid2,
    sn1,
    sn2,
    yh,
    dag,
    e1,
    dxh,
    dxl,
    acc_n2,
    acc_agg,
    acc_nx,
    acc_e2,
    acc_x,
    acc_bn,
    acc_be,
    fin,
    hs,
    hr,
    rs,
    rr,
    unit,
    load_sem,
    rim_ssem,
    rim_rsem,
    share_ssem,
    share_rsem,
    *staged,
):
    _, traj, nodes, _ = raw.shape
    state_in = raw.at[0]
    per = traj // GROUPS
    ext = nodes + 2 * RIM
    total = float(nodes * blk)
    links = Links(blk, graph)
    stages = links.stat_stages
    phases = LAYERS * GROUPS
    swaps = links.swap_stages
    staged = list(staged)
    stat, stat_recv, stat_ssem, stat_rsem = [
        [staged.pop(0) for _ in stages] for _ in range(4)
    ]
    swap, swap_recv, swap_ssem, swap_rsem = [
        [staged.pop(0) for _ in swaps] for _ in range(4)
    ]
    unit_recv = staged

    parts = [
        (offset_hbm, offset_in),
        (field_hbm, field_in),
        (id_hbm, id_in),
        (table_hbm, table_in),
        (state_hbm, raw.at[0]),
        (eb1_hbm, eb1),
        (eb2_hbm, eb2),
        (nb1_hbm, nb1),
        (nb2_hbm, nb2),
        (ew2_hbm, ew2),
        (nw2_hbm, nw2),
        (cot_hbm, dst),
    ]
    for l in range(LAYERS):
        parts.append((ew1_hbm.at[:, l, :], ew1.at[l, pl.ds(0, EDGE_IN), :]))
        parts.append((nw1_hbm.at[:, l, :], nw1.at[l, pl.ds(0, NODE_IN), :]))
    loads = [pltpu.make_async_copy(src, to, load_sem.at[i]) for i, (src, to) in enumerate(parts)]
    for load in loads:
        load.start()

    barrier = pltpu.get_barrier_semaphore()
    greeted = links.greeted()
    for peer in greeted:
        pl.semaphore_signal(barrier, inc=1, device_id=peer, device_id_type=MESH)

    rows = lax.broadcasted_iota(jnp.int32, (D, K * D), 0)
    cols = lax.broadcasted_iota(jnp.int32, (D, K * D), 1)
    spread[...] = jnp.where(rows == 3 * AUX + cols // D, 1.0, 0.0).astype(BF16)
    aux_t[...] = jnp.zeros_like(aux_t)
    e1[...] = jnp.zeros_like(e1)
    for acc in (acc_n2, acc_agg, acc_nx, acc_e2, acc_x, acc_bn, acc_be):
        acc[...] = jnp.zeros_like(acc)
    for u in range(4):
        rest = unit.shape[1] - UNIT_ROWS
        unit[u, pl.ds(UNIT_ROWS, rest), :] = jnp.zeros((rest, D), F32)
    fin[pl.ds(0, GROUPS), 0] = jnp.zeros((GROUPS, per, D), F32)
    fin[pl.ds(0, GROUPS), 1] = jnp.ones((GROUPS, per, D), F32)
    rr[0] = jnp.zeros(rr.shape[1:], F32)
    for stage in range(len(stages)):
        for low, high, unused in (
            (0, GROUPS, pl.ds(2 * per, 2 * per)),
            (phases, phases + GROUPS, pl.ds(0, 2 * per)),
        ):
            cut = pl.ds(low, high - low)
            stat[stage][cut, unused, :] = jnp.zeros((GROUPS, 2 * per, D), F32)
            arrive = stat_recv[stage]
            arrive[cut, :, unused, :] = jnp.zeros((GROUPS, arrive.shape[1], 2 * per, D), F32)
    place = lax.broadcasted_iota(jnp.int32, (1, nodes), 1).astype(F32) - nodes / 2
    loads[0].wait()
    offs = [offset_in[pl.ds(k * traj, traj), :] for k in range(K)]
    for i, o in enumerate(OFFSETS):
        many = jnp.zeros((traj, nodes), F32)
        for k in range(K):
            many = many + jnp.where(offs[k] == o, 1.0, 0.0)
        counts[pl.ds(i * traj, traj), :] = many
    counts[pl.ds(K * traj, 2 * traj), :] = jnp.zeros((2 * traj, nodes), F32)
    for load in loads[1:5]:
        load.wait()

    near_row = lax.broadcasted_iota(jnp.int32, (RIM, D), 0)

    for t in range(traj):
        tile = aux_t.at[t]
        tile[pl.ds(0, TW), :] = field_in[pl.ds(t, TW, stride=traj), :]
        row = id_in[t]
        for q in range(NPAR):
            tile[pl.ds(A_THETA + q, 1), :] = jnp.full((1, nodes), table_in[q, row], F32)
        tile[pl.ds(A_ONE, 1), :] = jnp.ones((1, nodes), F32)
        tile[pl.ds(A_PLACE, 1), :] = place
    for t in range(traj):
        head, tail = split(aux_t[t])
        head, tail = head.astype(F32), tail.astype(F32)
        full = jnp.concatenate(
            [
                head,
                tail,
                head,
                counts[pl.ds(t, 8, stride=traj), :],
                jnp.zeros((D - 3 * AUX - 8, nodes), F32),
            ],
            0,
        )
        back = full.T
        ahead, behind = raw[0, t, pl.ds(0, RIM), :], raw[0, t, pl.ds(nodes - RIM, RIM), :]
        hs[0, 0, t] = jnp.where(near_row < HALO, ahead, pltpu.roll(back[:RIM], HALO, 0))
        hs[1, 0, t] = jnp.where(
            near_row >= RIM - HALO, behind, pltpu.roll(back[nodes - RIM :], RIM - HALO, 0)
        )
        xa[t, pl.ds(0, nodes), :] = back.astype(BF16)

    pl.semaphore_wait(barrier, len(greeted))

    def ring_send(src, dst, kind, back=0):
        for way in range(2):
            remote(
                src.at[way],
                dst.at[way],
                rim_ssem.at[back],
                rim_rsem.at[kind],
                links.ring(1 if way else -1),
            ).start()

    def arrived(dst, sem):
        pltpu.make_async_copy(dst, dst, sem).wait()

    first = hs.at[:, 0], hr.at[:, 0]
    ring_send(*first, 0)

    def layer_rims(g):
        cut = pl.ds(g * per, per)
        return hs.at[:, 1, cut], hr.at[:, 1, cut]

    def grad_rims(p):
        cut = pl.ds(rem(p, GROUPS) * per, per)
        back = div(p, GROUPS)
        return rs.at[back, :, cut], rr.at[back + 1, :, cut]


    def multiply(j, _):
        for c in range(per):
            t = j * per + c
            many = dot(xa[t, pl.ds(0, nodes), :], spread[...])
            for i in range(K):
                weigh[t, pl.ds(i * nodes, nodes), :] = many[:, i * D : (i + 1) * D]
        return 0

    lax.fori_loop(0, GROUPS, multiply, 0)
    for load in loads[5:]:
        load.wait()
    for l in range(LAYERS):
        w_self = ew1[l, pl.ds(0, D), :]
        w_far = ew1[l, pl.ds(D, D), :]
        n_self = nw1[l, pl.ds(0, D), :]
        n_agg = nw1[l, pl.ds(D, D), :]
        for i, w in enumerate((w_self, w_far, n_self)):
            head, tail = split(0.5 * w)
            cut = pl.ds(i * D, D)
            w_in[l, pl.ds(0, D), cut] = head
            w_in[l, pl.ds(D, D), cut] = head
            w_in[l, pl.ds(2 * D, D), cut] = tail
        w_field = 0.5 * ew1[l, pl.ds(2 * D, TW), :]
        w_place = (0.5 / HALO) * ew1[l, pl.ds(2 * D + TW, 1), :]
        w_theta = 0.5 * ew1[l, pl.ds(2 * D + TW + 1, NPAR), :]
        n_theta = 0.5 * nw1[l, pl.ds(2 * D, NPAR), :]
        w_aux[...] = jnp.zeros_like(w_aux)
        w_aux[pl.ds(0, TW), pl.ds(0, D)] = w_field
        w_aux[pl.ds(0, TW), pl.ds(D, D)] = -w_field
        w_aux[pl.ds(A_THETA, NPAR), pl.ds(0, D)] = w_theta
        w_aux[pl.ds(A_THETA, NPAR), pl.ds(2 * D, D)] = n_theta
        w_aux[pl.ds(A_ONE, 1), pl.ds(0, D)] = 0.5 * eb1[pl.ds(l, 1), :]
        w_aux[pl.ds(A_ONE, 1), pl.ds(2 * D, D)] = 0.5 * nb1[pl.ds(l, 1), :]
        w_aux[pl.ds(A_PLACE, 1), pl.ds(0, D)] = w_place
        w_aux[pl.ds(A_PLACE, 1), pl.ds(D, D)] = -w_place
        head, tail = split(w_aux[...])
        w_in[l, pl.ds(3 * D, AUX), :] = head
        w_in[l, pl.ds(3 * D + AUX, AUX), :] = head
        w_in[l, pl.ds(3 * D + 2 * AUX, AUX), :] = tail
        w_in[l, pl.ds(3 * D + 3 * AUX, AUX), :] = jnp.zeros((AUX, 3 * D), BF16)
        second = 0.5 * ew2[l]
        w_e2[l] = doubled(second)
        w_agg[l] = doubled(0.5 * n_agg)
        w_n2[l] = doubled(0.5 * nw2[l])

    def back_weights():
        for l in range(LAYERS):
            w_e2t[l] = doubled(0.5 * ew2[l].T)
            w_n2t[l] = doubled(nw2[l].T)
            n_self = nw1[l, pl.ds(0, D), :]
            n_agg = nw1[l, pl.ds(D, D), :]
            head, tail = split(jnp.concatenate([n_self.T, 0.5 * n_agg.T], 1))
            w_np[l, pl.ds(0, D), :] = head
            w_np[l, pl.ds(D, D), :] = head
            w_np[l, pl.ds(2 * D, D), :] = tail
            w_ep[l, pl.ds(0, D), :] = pair(ew1[l, pl.ds(0, D), :].T)
            w_ep[l, pl.ds(D, D), :] = pair(ew1[l, pl.ds(D, D), :].T)

    kinds = (
        (0, GROUPS, pl.ds(0, 2 * per)),
        (GROUPS, phases, pl.ds(0, 4 * per)),
        (phases, phases + GROUPS, pl.ds(2 * per, 2 * per)),
    )

    def by_kind(event, action):
        for low, high, cut in kinds:
            if isinstance(event, int):
                if low <= event < high:
                    action(cut)
            else:
                pl.when((event >= low) & (event < high))(functools.partial(action, cut))

    def stat_send(event, stage):
        stride, size = stages[stage]

        def send(cut):
            for shift in range(1, size):
                remote(
                    stat[stage].at[event, cut],
                    stat_recv[stage].at[event, shift - 1, cut],
                    stat_ssem[stage].at[0],
                    stat_rsem[stage].at[event],
                    links.digit_peer(stride, size, shift),
                ).start()

        by_kind(event, send)

    def stat_merge(event, stage):
        stride, size = stages[stage]
        by_kind(
            event,
            lambda cut: arrived(stat_recv[stage].at[event, :, cut], stat_rsem[stage].at[event]),
        )
        parts = [stat[stage].at[event]] + [
            stat_recv[stage].at[event, shift - 1] for shift in range(1, size)
        ]
        m, m2, u, c = [[part[pl.ds(q * per, per), :] for part in parts] for q in range(4)]
        mean = sum(m[1:], m[0]) * (1.0 / size)
        gaps = [value - mean for value in m]
        spread2 = sum((gap * gap for gap in gaps[1:]), gaps[0] * gaps[0])
        m2_all = sum(m2[1:], m2[0]) + spread2 * float(nodes * stride)
        u_all = sum(u[1:], u[0])
        c_all = sum(c[1:], c[0])
        for gap, value in zip(gaps, u):
            c_all = c_all + gap * value
        return mean, m2_all, u_all, c_all

    def stat_forward(event):
        for stage in range(1, len(stages)):
            merged = stat_merge(event, stage - 1)
            for q, value in enumerate(merged):
                stat[stage][event, pl.ds(q * per, per), :] = value
            stat_send(event, stage)

    def stat_finish(event):
        mean, m2, u, c = stat_merge(event, len(stages) - 1)
        scale = lax.rsqrt(m2 * (1.0 / total) + EPSILON)
        at = event + GROUPS
        fin[at, 0] = mean
        fin[at, 1] = scale
        fin[at, 2] = u * (1.0 / total)
        fin[at, 3] = jnp.where(event < phases, scale, 1.0) * c * (1.0 / total)

    def rows_of(buf, l, t, start, size):
        return buf[l, pl.ds(t, per), pl.ds(start, size), :].reshape(per * size, buf.shape[-1])

    def enter(p):
        l, g = div(p, GROUPS), rem(p, GROUPS)
        base = g * per
        slot = rem(p, GROUPS)
        for c in range(per):
            t = base + c
            mean = fin[p, 0, pl.ds(c, 1), :]
            scale = fin[p, 1, pl.ds(c, 1), :]
            xs[l, t, pl.ds(0, nodes), :] = pair((raw[l, t] - mean) * scale)
            near = jnp.concatenate([hr[1, l, t], hr[0, l, t]], 0)
            near = (near - mean) * scale
            yh[t] = near
            xs[l, t, pl.ds(nodes, 2 * RIM), :] = pair(near)
            if c == per // 2 - 1:
                yield
        x = rows_of(xs, l, base, 0, ext)
        side = xa[pl.ds(base, per)].reshape(per * ext, D)
        yield
        p4 = dot(x, w_in[l, pl.ds(0, 2 * D), :])
        p4 = p4 + dot(jnp.concatenate([x[:, :D], side], 1), w_in[l, pl.ds(2 * D, 2 * D), :])
        yield
        for c in range(per):
            at = c * ext
            a_buf[l, base + c] = p4[at : at + nodes, :D]
            r_buf[l, base + c, pl.ds(RIM, nodes), :] = p4[at : at + nodes, D : 2 * D]
            r_buf[l, base + c, pl.ds(0, RIM), :] = p4[at + nodes : at + nodes + RIM, D : 2 * D]
            r_buf[l, base + c, pl.ds(RIM + nodes, RIM), :] = p4[
                at + nodes + RIM : at + ext, D : 2 * D
            ]
            n_buf[slot, c] = p4[at : at + nodes, 2 * D :]
            if c % 2:
                yield

    def first_main(g):
        base = g * per
        for c in range(per):
            xs[0, base + c, pl.ds(0, nodes), :] = pair(raw[0, base + c])
        x = rows_of(xs, 0, base, 0, nodes)
        side = xa[pl.ds(base, per), pl.ds(0, nodes), :].reshape(per * nodes, D)
        product = dot(x, w_in[0, pl.ds(0, 2 * D), :])
        product = product + dot(
            jnp.concatenate([x[:, :D], side], 1), w_in[0, pl.ds(2 * D, 2 * D), :]
        )
        for c in range(per):
            part = product[c * nodes : (c + 1) * nodes]
            a_buf[0, base + c] = part[:, :D]
            r_buf[0, base + c, pl.ds(RIM, nodes), :] = part[:, D : 2 * D]
            n_buf[g, c] = part[:, 2 * D :]

    def first_rims():
        lane = lax.broadcasted_iota(jnp.int32, (RIM, D), 1)
        moved = jnp.where((lane == A_PLACE) | (lane == 2 * AUX + A_PLACE), float(nodes), 0.0)
        near = []
        for t in range(traj):
            side = jnp.concatenate(
                [
                    pltpu.roll(hr[1, 0, t], HALO, 0) - moved,
                    pltpu.roll(hr[0, 0, t], RIM - HALO, 0) + moved,
                ],
                0,
            ).astype(BF16)
            xa[t, pl.ds(nodes, 2 * RIM), :] = side
            head, tail = split(jnp.concatenate([hr[1, 0, t], hr[0, 0, t]], 0))
            xs[0, t, pl.ds(nodes, 2 * RIM), :] = jnp.concatenate([head, tail], 1)
            near.append(jnp.concatenate([head, tail, head, side], 1))
        product = dot(jnp.concatenate(near, 0), w_in[0, :, pl.ds(D, D)])
        for t in range(traj):
            at = t * 2 * RIM
            r_buf[0, t, pl.ds(0, RIM), :] = product[at : at + RIM]
            r_buf[0, t, pl.ds(RIM + nodes, RIM), :] = product[at + RIM : at + 2 * RIM]

    def edges(p, s):
        l, g = div(p, GROUPS), rem(p, GROUPS)
        bias2 = 0.5 * eb2[pl.ds(l, 1), :]
        t = g * per + s
        hidden = []
        for i, o in enumerate(OFFSETS):
            half = a_buf[l, t] + r_buf[l, t, pl.ds(RIM + o, nodes), :]
            hidden.append(pair(half * (1.0 + jnp.tanh(half))))
            if i % 2:
                yield
        product = dot(jnp.concatenate(hidden, 0), w_e2[l])
        yield
        summed = None
        for i in range(K):
            half = halves(product[i * nodes : (i + 1) * nodes]) + bias2
            tanh = jnp.tanh(half)
            scaled = weigh[t, pl.ds(i * nodes, nodes), :] * (1.0 + tanh)
            message = scaled * half
            summed = message if summed is None else summed + message
            slope[l, t, pl.ds(i * nodes, nodes), :] = scaled + message * (1.0 - tanh)
            if i % 2 and i < K - 1:
                yield
        dag[rem(p, 2), s] = summed * (1.0 / K)
        yield

    def node(p):
        l, g = div(p, GROUPS), rem(p, GROUPS)
        base = g * per
        slot = rem(p, 2)
        here = rem(p, GROUPS)
        node2 = 0.5 * nb2[pl.ds(l, 1), :]
        both = pair(dag[slot].reshape(per * nodes, D))
        agg2[l, pl.ds(base, per)] = both.reshape(per, nodes, 2 * D)
        product = dot(both, w_agg[l])
        yield
        half = n_buf[here].reshape(per * nodes, D) + halves(product)
        act, rise = swish_parts(half)
        sn1[l, pl.ds(base, per)] = (0.5 * rise).reshape(per, nodes, D)
        both = pair(act)
        hid2[l, pl.ds(base, per)] = both.reshape(per, nodes, 2 * D)
        product = dot(both, w_n2[l])
        yield
        half = halves(product) + node2
        act, rise = swish_parts(half)
        sn2[l, pl.ds(base, per)] = (0.5 * rise).reshape(per, nodes, D)
        for c in range(per):
            t = base + c
            before = (raw[l, t] - fin[p, 0, pl.ds(c, 1), :]) * fin[p, 1, pl.ds(c, 1), :]
            new = before + act[c * nodes : (c + 1) * nodes]
            raw[l + 1, t] = new
            hs[0, 1 + l, t] = new[:RIM]
            hs[1, 1 + l, t] = new[nodes - RIM :]
            mean = jnp.sum(new, 0, keepdims=True) * (1.0 / nodes)
            gap = new - mean
            up = dst[t]
            stat[0][p, pl.ds(c, 1), :] = mean
            stat[0][p, pl.ds(per + c, 1), :] = jnp.sum(gap * gap, 0, keepdims=True)
            stat[0][p, pl.ds(2 * per + c, 1), :] = jnp.sum(up, 0, keepdims=True)
            stat[0][p, pl.ds(3 * per + c, 1), :] = jnp.sum(up * gap, 0, keepdims=True)
            if c % 2:
                yield

    def forward(p, _):
        border = p == GROUPS

        @pl.when((p > 0) & jnp.logical_not(border))
        def _():
            weave(ORDER_NODE, edges(p, 0), edges(p, 1), node(p - 1))

        @pl.when((p == 0) | border)
        def _():
            weave(ORDER_EDGES, edges(p, 0), edges(p, 1))

        @pl.when((p > 0) & jnp.logical_not(border))
        def _():
            stat_send(p - 1, 0)

        @pl.when((p > 0) & (p < GROUPS))
        def _():
            ring_send(*layer_rims(p - 1), p)

        @pl.when(border)
        def _():
            stat_forward(p - 1)

        def ready():
            stat_finish(p + 1 - GROUPS)
            arrived(layer_rims(p + 1 - GROUPS)[1], rim_rsem.at[p + 2 - GROUPS])

        pl.when((p + 1 > GROUPS) & (p + 1 < phases))(ready)
        alone = (p + 1 <= GROUPS) | (p + 1 == phases)

        @pl.when(jnp.logical_not(alone))
        def _():
            weave(ORDER_ENTER, edges(p, 2), edges(p, 3), enter(p + 1))

        @pl.when(alone)
        def _():
            weave(ORDER_EDGES, edges(p, 2), edges(p, 3))

        @pl.when(p + 1 == GROUPS)
        def _():
            weave("", node(p))
            stat_send(p, 0)
            ring_send(*layer_rims(p), p + 1)
            stat_forward(p - 1)
            ready()
            weave("", enter(p + 1))

        @pl.when((p > 0) & (p + 1 != GROUPS) & jnp.logical_not(border))
        def _():
            stat_forward(p - 1)

        return 0

    def back_node(p):
        l, g = LAYERS - 1 - div(p, GROUPS), rem(p, GROUPS)
        base = g * per
        source = phases + p
        own = GROUPS * (l + 1) + g
        back = div(p, GROUPS)
        deltas, firsts = [], []
        for c in range(per):
            t = base + c
            scale = fin[own, 1, pl.ds(c, 1), :]
            mu = fin[source, 2, pl.ds(c, 1), :]
            cross = fin[source, 3, pl.ds(c, 1), :]
            y = (raw[l + 1, t] - fin[own, 0, pl.ds(c, 1), :]) * scale
            raw[l + 1, t] = y
            up = dst[t]
            up = jnp.concatenate(
                [
                    up[:RIM] + rr[back, 1, t],
                    up[RIM : nodes - RIM],
                    up[nodes - RIM :] + rr[back, 0, t],
                ],
                0,
            )
            delta = scale * (up - mu - y * cross)
            first = delta * sn2[l, t]
            acc_bn[l] += jnp.sum(first.reshape(nodes // 8, 8, D), 0)
            deltas.append(delta)
            firsts.append(first)
            if c == per // 2 - 1:
                yield
        d2 = pair(jnp.concatenate(firsts, 0))
        yield
        x = rows_of(xs, l, base, 0, nodes)
        side = xa[pl.ds(base, per), pl.ds(0, nodes), :].reshape(per * nodes, D)
        size = per * nodes
        product = dot(d2, w_n2t[l])
        yield
        d1 = halves(product) * sn1[l, pl.ds(base, per)].reshape(size, D)
        d1 = pair(d1)
        product = dot(jnp.concatenate([d1, d1[:, :D]], 1), w_np[l])
        yield
        acc_n2[l] += dot_t(hid2[l, pl.ds(base, per)].reshape(size, 2 * D), d2)
        yield
        for c in range(per):
            at = c * nodes
            dst[base + c] = deltas[c] + product[at : at + nodes, :D]
            dag[rem(p, 2), c] = product[at : at + nodes, D:] * (1.0 / K)
        acc_agg[l] += dot_t(agg2[l, pl.ds(base, per)].reshape(size, 2 * D), d1)
        yield
        acc_nx[l] += dot_t(jnp.concatenate([x, side[:, : 2 * AUX]], 1), d1)
        yield

    def back_edges(p, s):
        l, g = LAYERS - 1 - div(p, GROUPS), rem(p, GROUPS)
        slot = rem(p, 2)
        t = g * per + s
        mine = e1.at[s % 2]
        hidden, deltas, rises = [], [], []
        coming = dag[slot, s]
        bias = None
        for i, o in enumerate(OFFSETS):
            half = a_buf[l, t] + r_buf[l, t, pl.ds(RIM + o, nodes), :]
            act, rise = swish_parts(half)
            rises.append(rise)
            hidden.append(pair(act))
            delta = coming * slope[l, t, pl.ds(i * nodes, nodes), :]
            bias = delta if bias is None else bias + delta
            deltas.append(pair(delta))
            if i % 2 and i < K - 1:
                yield
        d2 = jnp.concatenate(deltas, 0)
        acc_be[l] += jnp.sum(bias.reshape(nodes // 8, 8, D), 0)
        yield
        product = dot(d2, w_e2t[l])
        yield
        acc_e2[l] += dot_t(jnp.concatenate(hidden, 0), d2)
        yield
        near = None
        for i in range(K):
            d1 = halves(product[i * nodes : (i + 1) * nodes]) * rises[i]
            near = d1 if near is None else near + d1
            mine[i, pl.ds(RIM, nodes), :] = d1
            if i == K // 2 - 1:
                yield
        yield
        far = None
        left = None
        right = None
        for i, o in enumerate(OFFSETS):
            part = mine[i, pl.ds(RIM - o, nodes), :]
            far = part if far is None else far + part
            if o < 0:
                part = mine[i, pl.ds(-o, RIM), :]
                left = part if left is None else left + part
            else:
                part = mine[i, pl.ds(RIM + nodes - o, RIM), :]
                right = part if right is None else right + part
        rims = jnp.concatenate([left, right], 0)
        head, tail = split(near)
        head_f, tail_f = split(far)
        head_r, tail_r = split(rims)
        nothing = jnp.zeros((2 * RIM, D), BF16)
        dxh[slot, s, pl.ds(0, nodes), :] = jnp.concatenate([head, head_f], 1)
        dxl[slot, s, pl.ds(0, nodes), :] = jnp.concatenate([tail, tail_f], 1)
        dxh[slot, s, pl.ds(nodes, 2 * RIM), :] = jnp.concatenate([nothing, head_r], 1)
        dxl[slot, s, pl.ds(nodes, 2 * RIM), :] = jnp.concatenate([nothing, tail_r], 1)
        yield

    def leave_weights(p):
        l, g = LAYERS - 1 - div(p, GROUPS), rem(p, GROUPS)
        base = g * per
        size = per * ext
        slot = rem(p, 2)
        x = rows_of(xs, l, base, 0, ext)
        side = xa[pl.ds(base, per)].reshape(size, D)
        inputs = jnp.concatenate([x, side[:, : 2 * AUX]], 1)
        high = dxh[slot].reshape(size, 2 * D)
        low = dxl[slot].reshape(size, 2 * D)
        acc_x[l] += dot_t(
            jnp.concatenate([inputs, inputs], 0), jnp.concatenate([high, low], 0)
        )
        yield

    def leave_state(p):
        l, g = LAYERS - 1 - div(p, GROUPS), rem(p, GROUPS)
        base = g * per
        size = per * ext
        slot = rem(p, 2)
        event = phases + p
        back = div(p, GROUPS)
        own = GROUPS * l + g
        high = dxh[slot].reshape(size, 2 * D)
        low = dxl[slot].reshape(size, 2 * D)
        product = dot(high, w_ep[l]) + dot(low, w_ep[l])
        yield
        product = halves(product)
        for c in range(per):
            t, at = base + c, c * ext
            new = dst[t] + product[at : at + nodes]
            dst[t] = new
            rims = product[at + nodes : at + ext]
            rs[back, 0, t] = rims[:RIM]
            rs[back, 1, t] = rims[RIM:]
            y = (raw[l, t] - fin[own, 0, pl.ds(c, 1), :]) * fin[own, 1, pl.ds(c, 1), :]
            stat[0][event, pl.ds(2 * per + c, 1), :] = jnp.sum(new, 0, keepdims=True) + jnp.sum(
                rims, 0, keepdims=True
            )
            stat[0][event, pl.ds(3 * per + c, 1), :] = jnp.sum(
                new * y, 0, keepdims=True
            ) + jnp.sum(rims * yh[t], 0, keepdims=True)
            if c % 2:
                yield

    def backward(p, _):
        @pl.when(p > 0)
        def _():
            weave(
                ORDER_LEAVE,
                back_edges(p, 0),
                back_edges(p, 1),
                leave_weights(p - 1),
                leave_state(p - 1),
            )

        @pl.when(p == 0)
        def _():
            weave(ORDER_BACK, back_edges(p, 0), back_edges(p, 1))
            stat_forward(phases - 1)

        @pl.when(p > 0)
        def _():
            ring_send(*grad_rims(p - 1), GROUPS + p, 1)

        @pl.when((p > 0) & (p <= GROUPS))
        def _():
            stat_send(phases + p - 1, 0)

        @pl.when(p == GROUPS)
        def _():
            unit_second(unit.at[1], acc_e2.at[1])
            edge_unit(1, unit.at[1])

        sum_hook(SUMS_MID, p)

        def ready():
            stat_finish(GROUPS + p + 1)

        def rims_ready():
            arrived(grad_rims(p + 1 - GROUPS)[1], rim_rsem.at[p + 2])

        alone = (p + 1 == GROUPS) | (p + 1 == phases)
        pl.when(jnp.logical_not(alone))(ready)
        pl.when((p + 1 > GROUPS) & (p + 1 < phases))(rims_ready)

        @pl.when(jnp.logical_not(alone))
        def _():
            weave(ORDER_BACK_NODE, back_edges(p, 2), back_edges(p, 3), back_node(p + 1))

        @pl.when(alone)
        def _():
            weave(ORDER_BACK, back_edges(p, 2), back_edges(p, 3))

        @pl.when((p > 0) & (p <= GROUPS))
        def _():
            stat_forward(phases + p - 1)

        @pl.when(p + 1 == GROUPS)
        def _():
            ready()
            rims_ready()
            weave("", back_node(p + 1))

        @pl.when(p == GROUPS - 2)
        def _():
            node_unit(1, unit.at[0])

        @pl.when(p == phases - 2)
        def _():
            node_unit(0, unit.at[2])

        sum_hook(SUMS_END, p)

        return 0

    def quarter(acc, rows):
        return (
            acc[pl.ds(0, rows), pl.ds(0, D)]
            + acc[pl.ds(D, rows), pl.ds(0, D)]
            + acc[pl.ds(0, rows), pl.ds(D, D)]
            + acc[pl.ds(D, rows), pl.ds(D, D)]
        )

    def fold8(value):
        return jnp.sum(value, 0, keepdims=True)

    def unit_second(out, acc):
        out[pl.ds(0, D), :] = quarter(acc, D)

    def node_unit(l, out):
        unit_second(out, acc_n2.at[l])
        out[pl.ds(UNIT_FIRST, D), :] = quarter(acc_nx.at[l], D)
        out[pl.ds(UNIT_FIRST + D, D), :] = quarter(acc_agg.at[l], D)
        side = acc_nx[l, pl.ds(2 * D, AUX), :] + acc_nx[l, pl.ds(2 * D + AUX, AUX), :]
        out[pl.ds(UNIT_AUX, AUX), :] = halves(side)
        out[pl.ds(UNIT_AUX + A_SECOND, 1), :] = fold8(acc_bn[l])

    def edge_unit(l, out):
        both = acc_x[l, pl.ds(0, D), :] + acc_x[l, pl.ds(D, D), :]
        out[pl.ds(UNIT_FIRST, D), :] = both[:, :D]
        out[pl.ds(UNIT_FIRST + D, D), :] = both[:, D:]
        side = acc_x[l, pl.ds(2 * D, AUX), :] + acc_x[l, pl.ds(2 * D + AUX, AUX), :]
        row = lax.broadcasted_iota(jnp.int32, (AUX, D), 0)
        both = side[:, :D] - side[:, D:]
        out[pl.ds(UNIT_AUX, AUX), :] = jnp.where(
            row < TW, both, jnp.where(row == A_PLACE, both * (1.0 / HALO), side[:, :D])
        )
        out[pl.ds(UNIT_AUX + A_SECOND, 1), :] = fold8(acc_be[l])

    shares = len(links.share_stages)
    pieces = [1]
    for stage in range(shares):
        pieces.append(pieces[-1] * links.share_size(stage))
    lead, unit_rows = unit_sizes(graph)
    sums = (
        (0, 0, unit_rows),
        (1, 0, unit_rows),
        (2, 0, unit_rows),
        (3, 0, lead),
        (3, lead, unit_rows - lead),
    )
    steps = 2 * shares + len(swaps)

    def sum_step(n, step):
        u, start, rows = sums[n]

        def segment(stage, digit=None):
            place = start
            for k in range(stage):
                mine = links.share_digit(k) if digit is None or k < stage - 1 else digit
                place = place + mine * (rows // pieces[k + 1])
            return pl.ds(pl.multiple_of(place, 8), rows // pieces[stage])

        def part(stage):
            return pl.ds(start // pieces[stage], rows // pieces[stage])

        def others(stage):
            return range(1, links.share_size(stage))

        last = part(shares)
        done = step - 1
        value = None
        if 0 <= done < shares:
            into = unit_recv[done].at[u, :, part(done + 1)]
            arrived(into, share_rsem.at[done, n])
            value = unit[u, segment(done + 1), :]
            for shift in others(done):
                value = value + into[shift - 1]
        elif 0 <= done < shares + len(swaps):
            stage = done - shares
            into = swap_recv[stage].at[u, :, last]
            arrived(into, swap_rsem[stage].at[n])
            value = swap[stage][u, last, :]
            for shift in range(1, swaps[stage][1]):
                value = value + into[shift - 1]
        elif done >= 0:
            stage = steps - 1 - done
            arrived(unit_recv[stage].at[u, :, part(stage + 1)], share_rsem.at[shares + stage, n])
        if step < shares:
            if value is not None:
                unit[u, segment(step), :] = value
            for shift in others(step):
                peer, digit = links.share_peer(step, shift)
                remote(
                    unit.at[u, segment(step + 1, digit)],
                    unit_recv[step].at[u, shift - 1, part(step + 1)],
                    share_ssem.at[step],
                    share_rsem.at[step, n],
                    peer,
                ).start()
        elif step < shares + len(swaps):
            stage = step - shares
            swap[stage][u, last, :] = value
            stride, size = swaps[stage]
            for shift in range(1, size):
                remote(
                    swap[stage].at[u, last],
                    swap_recv[stage].at[u, shift - 1, last],
                    swap_ssem[stage].at[0],
                    swap_rsem[stage].at[n],
                    links.digit_peer(stride, size, shift),
                ).start()
        elif step < steps:
            if value is not None:
                unit_all[u, segment(shares), :] = value
            stage = steps - 1 - step
            for shift in others(stage):
                mine = segment(stage + 1)
                remote(
                    unit_all.at[u, mine],
                    unit_all.at[u, mine],
                    share_ssem.at[shares + stage],
                    share_rsem.at[shares + stage, n],
                    links.share_peer(stage, shift)[0],
                ).start()

    def sum_hook(table, p):
        for phase, n, step in table:
            pl.when(p == phase)(functools.partial(sum_step, n, step))

    for g in range(GROUPS):
        first_main(g)
    arrived(first[1], rim_rsem.at[0])
    first_rims()
    lax.fori_loop(0, phases, forward, 0)
    weave("", node(phases - 1))
    stat_send(phases - 1, 0)
    back_weights()
    stat_finish(GROUPS)
    weave("", back_node(0))
    lax.fori_loop(0, phases, backward, 0)
    unit_second(unit.at[3], acc_e2.at[0])
    sum_step(3, 0)
    weave("", leave_weights(phases - 1))
    edge_unit(0, unit.at[3])
    sum_step(4, 0)
    weave("", leave_state(phases - 1))
    ring_send(*grad_rims(phases - 1), GROUPS + phases, 1)
    done = {n: 0 for n in range(len(sums))}
    for table in (SUMS_MID, SUMS_END):
        for _, n, step in table:
            done[n] = max(done[n], step)
    for turn in range(2 * steps):
        for n in SUMS_TURNS[min(turn, len(SUMS_TURNS) - 1)]:
            if done[n] < steps:
                done[n] += 1
                sum_step(n, done[n])
        if turn:
            continue
        for g in range(GROUPS):
            arrived(grad_rims(phases - GROUPS + g)[1], rim_rsem.at[phases + 1 + g])
            for c in range(per):
                t = g * per + c
                dst[t, pl.ds(0, RIM), :] += rr[LAYERS, 1, t]
                dst[t, pl.ds(nodes - RIM, RIM), :] += rr[LAYERS, 0, t]

    arrived(hr, rim_ssem.at[0])
    arrived(rs, rim_ssem.at[1])
    for stage in range(len(stages)):
        arrived(stat_recv[stage].at[pl.ds(0, phases)], stat_ssem[stage].at[0])
    for stage in range(len(swaps)):
        arrived(swap_recv[stage], swap_ssem[stage].at[0])
    for stage in range(shares):
        for way in range(2):
            arrived(unit_recv[stage], share_ssem.at[way * shares + stage])


def unit_sizes(graph):
    share = 8 * 4 * graph
    lead = -(-UNIT_FIRST // share) * share
    return lead, lead + -(-(UNIT_ROWS - UNIT_FIRST) // share) * share


def assemble(
    raw,
    grad_mid,
    units,
    state_out,
    grad_out,
    g_ew1,
    g_eb1,
    g_ew2,
    g_eb2,
    g_nw1,
    g_nb1,
    g_nw2,
    g_nb2,
    sems,
):
    parts = sems.shape[1]
    rows = state_out.shape[0] // parts
    copies = []
    for i, (src, dst) in enumerate(((raw.at[LAYERS], state_out), (grad_mid, grad_out))):
        for part in range(parts):
            cut = pl.ds(part * rows, rows)
            copies.append(pltpu.make_async_copy(src.at[cut], dst.at[cut], sems.at[i, part]))
    for copy in copies:
        copy.start()
    for l in range(LAYERS):
        node, edge = units.at[2 * (LAYERS - 1 - l)], units.at[2 * (LAYERS - 1 - l) + 1]
        for unit, first, bias1, second, bias2 in (
            (node, g_nw1, g_nb1, g_nw2, g_nb2),
            (edge, g_ew1, g_eb1, g_ew2, g_eb2),
        ):
            first[pl.ds(0, 2 * D), l, :] = unit[pl.ds(UNIT_FIRST, 2 * D), :]
            bias1[pl.ds(l, 1), :] = unit[pl.ds(UNIT_AUX + A_ONE, 1), :]
            second[l] = unit[pl.ds(0, D), :]
            bias2[pl.ds(l, 1), :] = unit[pl.ds(UNIT_AUX + A_SECOND, 1), :]
        g_nw1[pl.ds(2 * D, NPAR), l, :] = node[pl.ds(UNIT_AUX + A_THETA, NPAR), :]
        g_ew1[pl.ds(2 * D, TW), l, :] = edge[pl.ds(UNIT_AUX, TW), :]
        g_ew1[pl.ds(2 * D + TW, 1), l, :] = edge[pl.ds(UNIT_AUX + A_PLACE, 1), :]
        g_ew1[pl.ds(2 * D + TW + 1, NPAR), l, :] = edge[pl.ds(UNIT_AUX + A_THETA, NPAR), :]
    for copy in copies:
        copy.wait()


def on_device(
    blk,
    graph,
    node_state,
    field_window,
    edge_offset,
    pde_id,
    pde_table,
    cotangent,
    edge_w1,
    edge_b1,
    edge_w2,
    edge_b2,
    node_w1,
    node_b1,
    node_w2,
    node_b2,
):
    traj, nodes, _ = node_state.shape
    per = traj // GROUPS
    ext = nodes + 2 * RIM
    field = jnp.transpose(field_window, (2, 0, 1)).reshape(TW * traj, nodes)
    offset = jnp.transpose(edge_offset, (2, 0, 1)).reshape(K * traj, nodes)
    table = jnp.transpose(pde_table, (1, 0))
    ew1 = jnp.transpose(edge_w1, (1, 0, 2))
    nw1 = jnp.transpose(node_w1, (1, 0, 2))
    vmem = pl.BlockSpec(memory_space=pltpu.VMEM)
    any_space = pl.BlockSpec(memory_space=pl.ANY)
    stages = digit_stages(blk, STAT_SIZES)
    swaps = digit_stages(blk // 4, (4,))
    shares = 4 * graph
    _, rows = unit_sizes(graph)
    seg = rows // shares
    events = 3 * GROUPS

    def f(*shape):
        return pltpu.VMEM(shape, F32)

    def b(*shape):
        return pltpu.VMEM(shape, BF16)

    L = LAYERS
    scratch = [
        f(TW * traj, nodes),
        pltpu.VMEM((K * traj, nodes), jnp.int32),
        pltpu.SMEM((traj,), jnp.int32),
        pltpu.SMEM((NPAR, NPDE), F32),
        f(L, -(-EDGE_IN // 8) * 8, D),
        f(L, D),
        f(L, D, D),
        f(L, D),
        f(L, -(-NODE_IN // 8) * 8, D),
        f(L, D),
        f(L, D, D),
        f(L, D),
        b(L, 4 * D, 3 * D),
        b(L, 2 * D, 2 * D),
        b(L, 2 * D, 2 * D),
        b(L, 2 * D, 2 * D),
        b(L, 2 * D, 2 * D),
        b(L, 2 * D, 2 * D),
        b(L, 3 * D, 2 * D),
        b(L, 2 * D, 2 * D),
        f(AUX, 3 * D),
        b(D, K * D),
        f(8 * traj, nodes),
        f(traj, K * nodes, D),
        f(traj, AUX, nodes),
        b(L, traj, ext, 2 * D),
        b(traj, ext, D),
        f(L, traj, nodes, D),
        f(L, traj, ext, D),
        f(GROUPS, per, nodes, D),
        f(L, traj, K * nodes, D),
        b(L, traj, nodes, 2 * D),
        b(L, traj, nodes, 2 * D),
        f(L, traj, nodes, D),
        f(L, traj, nodes, D),
        f(traj, 2 * RIM, D),
        f(2, per, nodes, D),
        f(2, K, ext, D),
        b(2, per, ext, 2 * D),
        b(2, per, ext, 2 * D),
        f(L, 2 * D, 2 * D),
        f(L, 2 * D, 2 * D),
        f(L, 2 * D + 2 * AUX, 2 * D),
        f(L, 2 * D, 2 * D),
        f(L, 2 * D + 2 * AUX, 2 * D),
        f(L, 8, D),
        f(L, 8, D),
        f(events + GROUPS, 4, per, D),
        f(2, 1 + L, traj, RIM, D),
        f(2, 2, traj, RIM, D),
        f(L, 2, traj, RIM, D),
        f(L + 1, 2, traj, RIM, D),
        f(4, rows, D),
        pltpu.SemaphoreType.DMA((16,)),
        pltpu.SemaphoreType.DMA((2,)),
        pltpu.SemaphoreType.DMA((1 + 3 * GROUPS,)),
        pltpu.SemaphoreType.DMA((4,)),
        pltpu.SemaphoreType.DMA((4, 5)),
    ]
    scratch += [f(events + GROUPS, 4 * per, D) for _ in stages]
    scratch += [f(events, size - 1, 4 * per, D) for _, size in stages]
    scratch += [pltpu.SemaphoreType.DMA((1,)) for _ in stages]
    scratch += [pltpu.SemaphoreType.DMA((events,)) for _ in stages]
    scratch += [f(4, seg, D) for _ in swaps]
    scratch += [f(4, size - 1, seg, D) for _, size in swaps]
    scratch += [pltpu.SemaphoreType.DMA((1,)) for _ in swaps]
    scratch += [pltpu.SemaphoreType.DMA((5,)) for _ in swaps]
    scratch += [f(4, 1, rows // 2, D), f(4, 2 * graph - 1, seg, D)]
    hbm = any_space
    mid = pl.pallas_call(
        functools.partial(kernel_body, blk, graph),
        out_shape=[f(L + 1, traj, nodes, D), f(traj, nodes, D), f(4, rows, D)],
        in_specs=[hbm] * 14,
        out_specs=[vmem] * 3,
        scratch_shapes=scratch,
        compiler_params=pltpu.CompilerParams(
            collective_id=0, has_side_effects=True, vmem_limit_bytes=54 * 2**20
        ),
        name="processor",
    )(
        node_state,
        field,
        offset,
        pde_id,
        table,
        cotangent,
        ew1,
        edge_b1,
        edge_w2,
        edge_b2,
        nw1,
        node_b1,
        node_w2,
        node_b2,
    )
    mid = [pltpu.with_memory_space_constraint(part, pltpu.VMEM) for part in mid]
    shapes = [
        (traj, nodes, D),
        (traj, nodes, D),
        (EDGE_IN, L, D),
        (L, D),
        (L, D, D),
        (L, D),
        (NODE_IN, L, D),
        (L, D),
        (L, D, D),
        (L, D),
    ]
    out = pl.pallas_call(
        assemble,
        out_shape=[jax.ShapeDtypeStruct(shape, F32) for shape in shapes],
        in_specs=[vmem] * 3,
        out_specs=[any_space, any_space] + [vmem] * 8,
        scratch_shapes=[pltpu.SemaphoreType.DMA((2, 8))],
        compiler_params=pltpu.CompilerParams(vmem_limit_bytes=8 * 2**20),
        name="assemble",
    )(*mid)
    out = list(out)
    out[2] = jnp.transpose(out[2], (1, 0, 2))
    out[6] = jnp.transpose(out[6], (1, 0, 2))
    return tuple(out)


def solution(mesh):
    rows = P("graph", "blk", None)
    return jax.shard_map(
        functools.partial(on_device, mesh.shape["blk"], mesh.shape["graph"]),
        mesh=mesh,
        in_specs=(rows, rows, rows, P("graph"), P(), rows) + (P(),) * 8,
        out_specs=(rows, rows) + (P(),) * 8,
        check_vma=False,
    )
```

```python
import functools

import jax
import jax.numpy as jnp
from jax import lax
from jax.experimental import pallas as pl
from jax.experimental.pallas import tpu as pltpu
from jax.sharding import PartitionSpec as P

D = 128
TW = 25
NPAR = 3
K = 6
HALO = 3
NPDE = 8
LAYERS = 2
EDGE_IN = 2 * D + TW + 1 + NPAR
NODE_IN = 2 * D + NPAR
OFFSETS = tuple(o for o in range(-HALO, HALO + 1) if o != 0)

EPSILON = 1e-05
RIM = 8
GROUPS = 4
AUX = 32
A_THETA = TW
A_ONE = TW + NPAR
A_PLACE = TW + NPAR + 1
A_SECOND = TW + NPAR + 2
UNIT_FIRST = D
UNIT_AUX = 3 * D
UNIT_ROWS = UNIT_AUX + AUX
STAT_SIZES = (2, 8)
SUMS_MID = ((3, 0, 1), (4, 1, 0), (5, 1, 1), (5, 0, 2), (7, 2, 1), (7, 1, 2))
SUMS_END = ((2, 0, 0), (6, 0, 3), (6, 2, 0))
SUMS_TURNS = ((3, 4, 2, 0), (3, 4, 1), (2, 3, 4, 1, 0))
ORDER_NODE = "0011000122210012011020"
ORDER_EDGES = "00001000111111"
ORDER_ENTER = "02002011202000111112"
ORDER_LEAVE = "00003000211013111131"
ORDER_BACK = "1010001110001101"
ORDER_BACK_NODE = "0201102202221122200111010"

F32 = jnp.float32
BF16 = jnp.bfloat16
MESH = pl.DeviceIdType.MESH


def dot(left, right):
    return jnp.dot(left, right, preferred_element_type=F32)


def dot_t(left, right):
    return lax.dot_general(left, right, (((0,), (0,)), ((), ())), preferred_element_type=F32)


def split(value):
    head = value.astype(BF16)
    tail = (value - head.astype(F32)).astype(BF16)
    return head, tail


def pair(value):
    head, tail = split(value)
    return jnp.concatenate([head, tail], 1)


def halves(product):
    return product[:, :D] + product[:, D:]


def doubled(weight):
    both = pair(weight)
    return jnp.concatenate([both, both], 0)


def swish_parts(half):
    t = jnp.tanh(half)
    u = 1.0 + t
    act = half * u
    return act, u + act * (1.0 - t)


def digit_stages(count, sizes):
    stages, stride, step = [], 1, 0
    while stride < count:
        size = sizes[min(step, len(sizes) - 1)]
        while count // stride % size:
            size -= 1
        stages.append((stride, size))
        stride *= size
        step += 1
    return stages


class Links:
    def __init__(self, blk, graph):
        self.blk, self.graph = blk, graph
        self.me = lax.axis_index("blk")
        self.mine = lax.axis_index("graph")
        self.stat_stages = digit_stages(blk, STAT_SIZES)
        self.share_stages = [[("blk", 1, 2)], [("blk", 2, 2), ("graph", 1, graph)]]
        self.swap_stages = [(stride * 4, size) for stride, size in digit_stages(blk // 4, (4,))]

    def ring(self, shift):
        return (self.mine, lax.rem(self.me + shift + self.blk, self.blk))

    def digit_peer(self, stride, size, shift):
        digit = lax.rem(self.me // stride, size)
        other = lax.rem(digit + shift, size)
        return (self.mine, self.me + (other - digit) * stride)

    def share_size(self, stage):
        size = 1
        for _, _, count in self.share_stages[stage]:
            size *= count
        return size

    def share_digit(self, stage):
        value = 0
        for axis, stride, size in self.share_stages[stage]:
            place = self.me if axis == "blk" else self.mine
            value = value * size + lax.rem(place // stride, size)
        return value

    def share_peer(self, stage, shift):
        other = lax.rem(self.share_digit(stage) + shift, self.share_size(stage))
        coords = {"blk": self.me, "graph": self.mine}
        rest = other
        for axis, stride, count in reversed(self.share_stages[stage]):
            place = coords[axis]
            now = lax.rem(place // stride, count)
            coords[axis] = place + (lax.rem(rest, count) - now) * stride
            rest = rest // count
        return (coords["graph"], coords["blk"]), other

    def greeted(self):
        peers = [self.ring(1), self.ring(-1)]
        for stride, size in self.stat_stages + self.swap_stages:
            peers += [self.digit_peer(stride, size, shift) for shift in range(1, size)]
        for stage in range(len(self.share_stages)):
            peers += [self.share_peer(stage, shift)[0] for shift in range(1, self.share_size(stage))]
        return peers


def div(value, by):
    return value // by if isinstance(value, int) else lax.div(value, jnp.int32(by))


def rem(value, by):
    return value % by if isinstance(value, int) else lax.rem(value, jnp.int32(by))


def negated(condition):
    return not condition if isinstance(condition, bool) else jnp.logical_not(condition)


def weave(order, *parts):
    for name in order:
        next(parts[int(name)], None)
    for part in parts:
        for _ in part:
            pass


def remote(src, dst, send_sem, recv_sem, device):
    return pltpu.make_async_remote_copy(
        src_ref=src,
        dst_ref=dst,
        send_sem=send_sem,
        recv_sem=recv_sem,
        device_id=device,
        device_id_type=MESH,
    )


def kernel_body(
    blk,
    graph,
    state_hbm,
    field_hbm,
    offset_hbm,
    id_hbm,
    table_hbm,
    cot_hbm,
    ew1_hbm,
    eb1_hbm,
    ew2_hbm,
    eb2_hbm,
    nw1_hbm,
    nb1_hbm,
    nw2_hbm,
    nb2_hbm,
    raw,
    dst,
    unit_all,
    field_in,
    offset_in,
    id_in,
    table_in,
    ew1,
    eb1,
    ew2,
    eb2,
    nw1,
    nb1,
    nw2,
    nb2,
    w_in,
    w_e2,
    w_e2t,
    w_agg,
    w_n2,
    w_n2t,
    w_np,
    w_ep,
    w_aux,
    spread,
    counts,
    weigh,
    aux_t,
    xs,
    xa,
    a_buf,
    r_buf,
    n_buf,
    slope,
    agg2,
    hid2,
    sn1,
    sn2,
    yh,
    dag,
    e1,
    dxh,
    dxl,
    acc_n2,
    acc_agg,
    acc_nx,
    acc_e2,
    acc_x,
    acc_bn,
    acc_be,
    fin,
    hs,
    hr,
    rs,
    rr,
    unit,
    load_sem,
    rim_ssem,
    rim_rsem,
    share_ssem,
    share_rsem,
    *staged,
):
    _, traj, nodes, _ = raw.shape
    state_in = raw.at[0]
    per = traj // GROUPS
    ext = nodes + 2 * RIM
    total = float(nodes * blk)
    links = Links(blk, graph)
    stages = links.stat_stages
    phases = LAYERS * GROUPS
    swaps = links.swap_stages
    staged = list(staged)
    stat, stat_recv, stat_ssem, stat_rsem = [
        [staged.pop(0) for _ in stages] for _ in range(4)
    ]
    swap, swap_recv, swap_ssem, swap_rsem = [
        [staged.pop(0) for _ in swaps] for _ in range(4)
    ]
    unit_recv = staged

    parts = [
        (offset_hbm, offset_in),
        (field_hbm, field_in),
        (id_hbm, id_in),
        (table_hbm, table_in),
        (state_hbm, raw.at[0]),
        (eb1_hbm, eb1),
        (eb2_hbm, eb2),
        (nb1_hbm, nb1),
        (nb2_hbm, nb2),
        (ew2_hbm, ew2),
        (nw2_hbm, nw2),
        (cot_hbm, dst),
    ]
    for l in range(LAYERS):
        parts.append((ew1_hbm.at[:, l, :], ew1.at[l, pl.ds(0, EDGE_IN), :]))
        parts.append((nw1_hbm.at[:, l, :], nw1.at[l, pl.ds(0, NODE_IN), :]))
    loads = [pltpu.make_async_copy(src, to, load_sem.at[i]) for i, (src, to) in enumerate(parts)]
    for load in loads:
        load.start()

    barrier = pltpu.get_barrier_semaphore()
    greeted = links.greeted()
    for peer in greeted:
        pl.semaphore_signal(barrier, inc=1, device_id=peer, device_id_type=MESH)

    rows = lax.broadcasted_iota(jnp.int32, (D, K * D), 0)
    cols = lax.broadcasted_iota(jnp.int32, (D, K * D), 1)
    spread[...] = jnp.where(rows == 3 * AUX + cols // D, 1.0, 0.0).astype(BF16)
    aux_t[...] = jnp.zeros_like(aux_t)
    e1[...] = jnp.zeros_like(e1)
    for acc in (acc_n2, acc_agg, acc_nx, acc_e2, acc_x, acc_bn, acc_be):
        acc[...] = jnp.zeros_like(acc)
    for u in range(4):
        rest = unit.shape[1] - UNIT_ROWS
        unit[u, pl.ds(UNIT_ROWS, rest), :] = jnp.zeros((rest, D), F32)
    fin[pl.ds(0, GROUPS), 0] = jnp.zeros((GROUPS, per, D), F32)
    fin[pl.ds(0, GROUPS), 1] = jnp.ones((GROUPS, per, D), F32)
    rr[0] = jnp.zeros(rr.shape[1:], F32)
    for stage in range(len(stages)):
        for low, high, unused in (
            (0, GROUPS, pl.ds(2 * per, 2 * per)),
            (phases, phases + GROUPS, pl.ds(0, 2 * per)),
        ):
            cut = pl.ds(low, high - low)
            stat[stage][cut, unused, :] = jnp.zeros((GROUPS, 2 * per, D), F32)
            arrive = stat_recv[stage]
            arrive[cut, :, unused, :] = jnp.zeros((GROUPS, arrive.shape[1], 2 * per, D), F32)
    place = lax.broadcasted_iota(jnp.int32, (1, nodes), 1).astype(F32) - nodes / 2
    loads[0].wait()
    offs = [offset_in[pl.ds(k * traj, traj), :] for k in range(K)]
    for i, o in enumerate(OFFSETS):
        many = jnp.zeros((traj, nodes), F32)
        for k in range(K):
            many = many + jnp.where(offs[k] == o, 1.0, 0.0)
        counts[pl.ds(i * traj, traj), :] = many
    counts[pl.ds(K * traj, 2 * traj), :] = jnp.zeros((2 * traj, nodes), F32)
    for load in loads[1:5]:
        load.wait()

    near_row = lax.broadcasted_iota(jnp.int32, (RIM, D), 0)

    for t in range(traj):
        tile = aux_t.at[t]
        tile[pl.ds(0, TW), :] = field_in[pl.ds(t, TW, stride=traj), :]
        row = id_in[t]
        for q in range(NPAR):
            tile[pl.ds(A_THETA + q, 1), :] = jnp.full((1, nodes), table_in[q, row], F32)
        tile[pl.ds(A_ONE, 1), :] = jnp.ones((1, nodes), F32)
        tile[pl.ds(A_PLACE, 1), :] = place
    for t in range(traj):
        head, tail = split(aux_t[t])
        head, tail = head.astype(F32), tail.astype(F32)
        full = jnp.concatenate(
            [
                head,
                tail,
                head,
                counts[pl.ds(t, 8, stride=traj), :],
                jnp.zeros((D - 3 * AUX - 8, nodes), F32),
            ],
            0,
        )
        back = full.T
        ahead, behind = raw[0, t, pl.ds(0, RIM), :], raw[0, t, pl.ds(nodes - RIM, RIM), :]
        hs[0, 0, t] = jnp.where(near_row < HALO, ahead, pltpu.roll(back[:RIM], HALO, 0))
        hs[1, 0, t] = jnp.where(
            near_row >= RIM - HALO, behind, pltpu.roll(back[nodes - RIM :], RIM - HALO, 0)
        )
        xa[t, pl.ds(0, nodes), :] = back.astype(BF16)

    pl.semaphore_wait(barrier, len(greeted))

    def ring_send(src, dst, kind, back=0):
        for way in range(2):
            remote(
                src.at[way],
                dst.at[way],
                rim_ssem.at[back],
                rim_rsem.at[kind],
                links.ring(1 if way else -1),
            ).start()

    def arrived(dst, sem):
        pltpu.make_async_copy(dst, dst, sem).wait()

    first = hs.at[:, 0], hr.at[:, 0]
    ring_send(*first, 0)

    def layer_rims(g):
        cut = pl.ds(g * per, per)
        return hs.at[:, 1, cut], hr.at[:, 1, cut]

    def grad_rims(p):
        cut = pl.ds(rem(p, GROUPS) * per, per)
        back = div(p, GROUPS)
        return rs.at[back, :, cut], rr.at[back + 1, :, cut]


    def multiply(j, _):
        for c in range(per):
            t = j * per + c
            many = dot(xa[t, pl.ds(0, nodes), :], spread[...])
            for i in range(K):
                weigh[t, pl.ds(i * nodes, nodes), :] = many[:, i * D : (i + 1) * D]
        return 0

    lax.fori_loop(0, GROUPS, multiply, 0)
    for load in loads[5:]:
        load.wait()
    for l in range(LAYERS):
        w_self = ew1[l, pl.ds(0, D), :]
        w_far = ew1[l, pl.ds(D, D), :]
        n_self = nw1[l, pl.ds(0, D), :]
        n_agg = nw1[l, pl.ds(D, D), :]
        for i, w in enumerate((w_self, w_far, n_self)):
            head, tail = split(0.5 * w)
            cut = pl.ds(i * D, D)
            w_in[l, pl.ds(0, D), cut] = head
            w_in[l, pl.ds(D, D), cut] = head
            w_in[l, pl.ds(2 * D, D), cut] = tail
        w_field = 0.5 * ew1[l, pl.ds(2 * D, TW), :]
        w_place = (0.5 / HALO) * ew1[l, pl.ds(2 * D + TW, 1), :]
        w_theta = 0.5 * ew1[l, pl.ds(2 * D + TW + 1, NPAR), :]
        n_theta = 0.5 * nw1[l, pl.ds(2 * D, NPAR), :]
        w_aux[...] = jnp.zeros_like(w_aux)
        w_aux[pl.ds(0, TW), pl.ds(0, D)] = w_field
        w_aux[pl.ds(0, TW), pl.ds(D, D)] = -w_field
        w_aux[pl.ds(A_THETA, NPAR), pl.ds(0, D)] = w_theta
        w_aux[pl.ds(A_THETA, NPAR), pl.ds(2 * D, D)] = n_theta
        w_aux[pl.ds(A_ONE, 1), pl.ds(0, D)] = 0.5 * eb1[pl.ds(l, 1), :]
        w_aux[pl.ds(A_ONE, 1), pl.ds(2 * D, D)] = 0.5 * nb1[pl.ds(l, 1), :]
        w_aux[pl.ds(A_PLACE, 1), pl.ds(0, D)] = w_place
        w_aux[pl.ds(A_PLACE, 1), pl.ds(D, D)] = -w_place
        head, tail = split(w_aux[...])
        w_in[l, pl.ds(3 * D, AUX), :] = head
        w_in[l, pl.ds(3 * D + AUX, AUX), :] = head
        w_in[l, pl.ds(3 * D + 2 * AUX, AUX), :] = tail
        w_in[l, pl.ds(3 * D + 3 * AUX, AUX), :] = jnp.zeros((AUX, 3 * D), BF16)
        second = 0.5 * ew2[l]
        w_e2[l] = doubled(second)
        w_agg[l] = doubled(0.5 * n_agg)
        w_n2[l] = doubled(0.5 * nw2[l])

    def back_weights():
        for l in range(LAYERS):
            w_e2t[l] = doubled(0.5 * ew2[l].T)
            w_n2t[l] = doubled(nw2[l].T)
            n_self = nw1[l, pl.ds(0, D), :]
            n_agg = nw1[l, pl.ds(D, D), :]
            head, tail = split(jnp.concatenate([n_self.T, 0.5 * n_agg.T], 1))
            w_np[l, pl.ds(0, D), :] = head
            w_np[l, pl.ds(D, D), :] = head
            w_np[l, pl.ds(2 * D, D), :] = tail
            w_ep[l, pl.ds(0, D), :] = pair(ew1[l, pl.ds(0, D), :].T)
            w_ep[l, pl.ds(D, D), :] = pair(ew1[l, pl.ds(D, D), :].T)

    kinds = (
        (0, GROUPS, pl.ds(0, 2 * per)),
        (GROUPS, phases, pl.ds(0, 4 * per)),
        (phases, phases + GROUPS, pl.ds(2 * per, 2 * per)),
    )

    def by_kind(event, action):
        for low, high, cut in kinds:
            if isinstance(event, int):
                if low <= event < high:
                    action(cut)
            else:
                pl.when((event >= low) & (event < high))(functools.partial(action, cut))

    def stat_send(event, stage):
        stride, size = stages[stage]

        def send(cut):
            for shift in range(1, size):
                remote(
                    stat[stage].at[event, cut],
                    stat_recv[stage].at[event, shift - 1, cut],
                    stat_ssem[stage].at[0],
                    stat_rsem[stage].at[event],
                    links.digit_peer(stride, size, shift),
                ).start()

        by_kind(event, send)

    def stat_merge(event, stage):
        stride, size = stages[stage]
        by_kind(
            event,
            lambda cut: arrived(stat_recv[stage].at[event, :, cut], stat_rsem[stage].at[event]),
        )
        parts = [stat[stage].at[event]] + [
            stat_recv[stage].at[event, shift - 1] for shift in range(1, size)
        ]
        m, m2, u, c = [[part[pl.ds(q * per, per), :] for part in parts] for q in range(4)]
        mean = sum(m[1:], m[0]) * (1.0 / size)
        gaps = [value - mean for value in m]
        spread2 = sum((gap * gap for gap in gaps[1:]), gaps[0] * gaps[0])
        m2_all = sum(m2[1:], m2[0]) + spread2 * float(nodes * stride)
        u_all = sum(u[1:], u[0])
        c_all = sum(c[1:], c[0])
        for gap, value in zip(gaps, u):
            c_all = c_all + gap * value
        return mean, m2_all, u_all, c_all

    def stat_forward(event):
        for stage in range(1, len(stages)):
            merged = stat_merge(event, stage - 1)
            for q, value in enumerate(merged):
                stat[stage][event, pl.ds(q * per, per), :] = value
            stat_send(event, stage)

    def stat_finish(event):
        mean, m2, u, c = stat_merge(event, len(stages) - 1)
        scale = lax.rsqrt(m2 * (1.0 / total) + EPSILON)
        at = event + GROUPS
        fin[at, 0] = mean
        fin[at, 1] = scale
        fin[at, 2] = u * (1.0 / total)
        fin[at, 3] = jnp.where(event < phases, scale, 1.0) * c * (1.0 / total)

    def rows_of(buf, l, t, start, size):
        return buf[l, pl.ds(t, per), pl.ds(start, size), :].reshape(per * size, buf.shape[-1])

    def enter(p):
        l, g = div(p, GROUPS), rem(p, GROUPS)
        base = g * per
        slot = rem(p, GROUPS)
        for c in range(per):
            t = base + c
            mean = fin[p, 0, pl.ds(c, 1), :]
            scale = fin[p, 1, pl.ds(c, 1), :]
            xs[l, t, pl.ds(0, nodes), :] = pair((raw[l, t] - mean) * scale)
            near = jnp.concatenate([hr[1, l, t], hr[0, l, t]], 0)
            near = (near - mean) * scale
            yh[t] = near
            xs[l, t, pl.ds(nodes, 2 * RIM), :] = pair(near)
            if c == per // 2 - 1:
                yield
        x = rows_of(xs, l, base, 0, ext)
        side = xa[pl.ds(base, per)].reshape(per * ext, D)
        yield
        p4 = dot(x, w_in[l, pl.ds(0, 2 * D), :])
        p4 = p4 + dot(jnp.concatenate([x[:, :D], side], 1), w_in[l, pl.ds(2 * D, 2 * D), :])
        yield
        for c in range(per):
            at = c * ext
            a_buf[l, base + c] = p4[at : at + nodes, :D]
            r_buf[l, base + c, pl.ds(RIM, nodes), :] = p4[at : at + nodes, D : 2 * D]
            r_buf[l, base + c, pl.ds(0, RIM), :] = p4[at + nodes : at + nodes + RIM, D : 2 * D]
            r_buf[l, base + c, pl.ds(RIM + nodes, RIM), :] = p4[
                at + nodes + RIM : at + ext, D : 2 * D
            ]
            n_buf[slot, c] = p4[at : at + nodes, 2 * D :]
            if c % 2:
                yield

    def first_main(g):
        base = g * per
        for c in range(per):
            xs[0, base + c, pl.ds(0, nodes), :] = pair(raw[0, base + c])
        x = rows_of(xs, 0, base, 0, nodes)
        side = xa[pl.ds(base, per), pl.ds(0, nodes), :].reshape(per * nodes, D)
        product = dot(x, w_in[0, pl.ds(0, 2 * D), :])
        product = product + dot(
            jnp.concatenate([x[:, :D], side], 1), w_in[0, pl.ds(2 * D, 2 * D), :]
        )
        for c in range(per):
            part = product[c * nodes : (c + 1) * nodes]
            a_buf[0, base + c] = part[:, :D]
            r_buf[0, base + c, pl.ds(RIM, nodes), :] = part[:, D : 2 * D]
            n_buf[g, c] = part[:, 2 * D :]

    def first_rims():
        lane = lax.broadcasted_iota(jnp.int32, (RIM, D), 1)
        moved = jnp.where((lane == A_PLACE) | (lane == 2 * AUX + A_PLACE), float(nodes), 0.0)
        near = []
        for t in range(traj):
            side = jnp.concatenate(
                [
                    pltpu.roll(hr[1, 0, t], HALO, 0) - moved,
                    pltpu.roll(hr[0, 0, t], RIM - HALO, 0) + moved,
                ],
                0,
            ).astype(BF16)
            xa[t, pl.ds(nodes, 2 * RIM), :] = side
            head, tail = split(jnp.concatenate([hr[1, 0, t], hr[0, 0, t]], 0))
            xs[0, t, pl.ds(nodes, 2 * RIM), :] = jnp.concatenate([head, tail], 1)
            near.append(jnp.concatenate([head, tail, head, side], 1))
        product = dot(jnp.concatenate(near, 0), w_in[0, :, pl.ds(D, D)])
        for t in range(traj):
            at = t * 2 * RIM
            r_buf[0, t, pl.ds(0, RIM), :] = product[at : at + RIM]
            r_buf[0, t, pl.ds(RIM + nodes, RIM), :] = product[at + RIM : at + 2 * RIM]

    def edges(p, s):
        l, g = div(p, GROUPS), rem(p, GROUPS)
        bias2 = 0.5 * eb2[pl.ds(l, 1), :]
        t = g * per + s
        hidden = []
        for i, o in enumerate(OFFSETS):
            half = a_buf[l, t] + r_buf[l, t, pl.ds(RIM + o, nodes), :]
            hidden.append(pair(half * (1.0 + jnp.tanh(half))))
            if i % 2:
                yield
        product = dot(jnp.concatenate(hidden, 0), w_e2[l])
        yield
        summed = None
        for i in range(K):
            half = halves(product[i * nodes : (i + 1) * nodes]) + bias2
            tanh = jnp.tanh(half)
            scaled = weigh[t, pl.ds(i * nodes, nodes), :] * (1.0 + tanh)
            message = scaled * half
            summed = message if summed is None else summed + message
            slope[l, t, pl.ds(i * nodes, nodes), :] = scaled + message * (1.0 - tanh)
            if i % 2 and i < K - 1:
                yield
        dag[rem(p, 2), s] = summed * (1.0 / K)
        yield

    def node(p):
        l, g = div(p, GROUPS), rem(p, GROUPS)
        base = g * per
        slot = rem(p, 2)
        here = rem(p, GROUPS)
        node2 = 0.5 * nb2[pl.ds(l, 1), :]
        both = pair(dag[slot].reshape(per * nodes, D))
        agg2[l, pl.ds(base, per)] = both.reshape(per, nodes, 2 * D)
        product = dot(both, w_agg[l])
        yield
        half = n_buf[here].reshape(per * nodes, D) + halves(product)
        act, rise = swish_parts(half)
        sn1[l, pl.ds(base, per)] = (0.5 * rise).reshape(per, nodes, D)
        both = pair(act)
        hid2[l, pl.ds(base, per)] = both.reshape(per, nodes, 2 * D)
        product = dot(both, w_n2[l])
        yield
        half = halves(product) + node2
        act, rise = swish_parts(half)
        sn2[l, pl.ds(base, per)] = (0.5 * rise).reshape(per, nodes, D)
        for c in range(per):
            t = base + c
            before = (raw[l, t] - fin[p, 0, pl.ds(c, 1), :]) * fin[p, 1, pl.ds(c, 1), :]
            new = before + act[c * nodes : (c + 1) * nodes]
            raw[l + 1, t] = new
            hs[0, 1 + l, t] = new[:RIM]
            hs[1, 1 + l, t] = new[nodes - RIM :]
            mean = jnp.sum(new, 0, keepdims=True) * (1.0 / nodes)
            gap = new - mean
            up = dst[t]
            stat[0][p, pl.ds(c, 1), :] = mean
            stat[0][p, pl.ds(per + c, 1), :] = jnp.sum(gap * gap, 0, keepdims=True)
            stat[0][p, pl.ds(2 * per + c, 1), :] = jnp.sum(up, 0, keepdims=True)
            stat[0][p, pl.ds(3 * per + c, 1), :] = jnp.sum(up * gap, 0, keepdims=True)
            if c % 2:
                yield

    def forward(p, _):
        border = p == GROUPS

        @pl.when((p > 0) & negated(border))
        def _():
            weave(ORDER_NODE, edges(p, 0), edges(p, 1), node(p - 1))

        @pl.when((p == 0) | border)
        def _():
            weave(ORDER_EDGES, edges(p, 0), edges(p, 1))

        @pl.when((p > 0) & negated(border))
        def _():
            stat_send(p - 1, 0)

        @pl.when((p > 0) & (p < GROUPS))
        def _():
            ring_send(*layer_rims(p - 1), p)

        @pl.when(border)
        def _():
            stat_forward(p - 1)

        def ready():
            stat_finish(p + 1 - GROUPS)
            arrived(layer_rims(p + 1 - GROUPS)[1], rim_rsem.at[p + 2 - GROUPS])

        pl.when((p + 1 > GROUPS) & (p + 1 < phases))(ready)
        alone = (p + 1 <= GROUPS) | (p + 1 == phases)

        @pl.when(negated(alone))
        def _():
            weave(ORDER_ENTER, edges(p, 2), edges(p, 3), enter(p + 1))

        @pl.when(alone)
        def _():
            weave(ORDER_EDGES, edges(p, 2), edges(p, 3))

        @pl.when(p + 1 == GROUPS)
        def _():
            weave("", node(p))
            stat_send(p, 0)
            ring_send(*layer_rims(p), p + 1)
            stat_forward(p - 1)
            ready()
            weave("", enter(p + 1))

        @pl.when((p > 0) & (p + 1 != GROUPS) & negated(border))
        def _():
            stat_forward(p - 1)

        return 0

    def back_node(p):
        l, g = LAYERS - 1 - div(p, GROUPS), rem(p, GROUPS)
        base = g * per
        source = phases + p
        own = GROUPS * (l + 1) + g
        back = div(p, GROUPS)
        deltas, firsts = [], []
        for c in range(per):
            t = base + c
            scale = fin[own, 1, pl.ds(c, 1), :]
            mu = fin[source, 2, pl.ds(c, 1), :]
            cross = fin[source, 3, pl.ds(c, 1), :]
            y = (raw[l + 1, t] - fin[own, 0, pl.ds(c, 1), :]) * scale
            raw[l + 1, t] = y
            up = dst[t]
            up = jnp.concatenate(
                [
                    up[:RIM] + rr[back, 1, t],
                    up[RIM : nodes - RIM],
                    up[nodes - RIM :] + rr[back, 0, t],
                ],
                0,
            )
            delta = scale * (up - mu - y * cross)
            first = delta * sn2[l, t]
            acc_bn[l] += jnp.sum(first.reshape(nodes // 8, 8, D), 0)
            deltas.append(delta)
            firsts.append(first)
            if c == per // 2 - 1:
                yield
        d2 = pair(jnp.concatenate(firsts, 0))
        yield
        x = rows_of(xs, l, base, 0, nodes)
        side = xa[pl.ds(base, per), pl.ds(0, nodes), :].reshape(per * nodes, D)
        size = per * nodes
        product = dot(d2, w_n2t[l])
        yield
        d1 = halves(product) * sn1[l, pl.ds(base, per)].reshape(size, D)
        d1 = pair(d1)
        product = dot(jnp.concatenate([d1, d1[:, :D]], 1), w_np[l])
        yield
        acc_n2[l] += dot_t(hid2[l, pl.ds(base, per)].reshape(size, 2 * D), d2)
        yield
        for c in range(per):
            at = c * nodes
            dst[base + c] = deltas[c] + product[at : at + nodes, :D]
            dag[rem(p, 2), c] = product[at : at + nodes, D:] * (1.0 / K)
        acc_agg[l] += dot_t(agg2[l, pl.ds(base, per)].reshape(size, 2 * D), d1)
        yield
        acc_nx[l] += dot_t(jnp.concatenate([x, side[:, : 2 * AUX]], 1), d1)
        yield

    def back_edges(p, s):
        l, g = LAYERS - 1 - div(p, GROUPS), rem(p, GROUPS)
        slot = rem(p, 2)
        t = g * per + s
        mine = e1.at[s % 2]
        hidden, deltas, rises = [], [], []
        coming = dag[slot, s]
        bias = None
        for i, o in enumerate(OFFSETS):
            half = a_buf[l, t] + r_buf[l, t, pl.ds(RIM + o, nodes), :]
            act, rise = swish_parts(half)
            rises.append(rise)
            hidden.append(pair(act))
            delta = coming * slope[l, t, pl.ds(i * nodes, nodes), :]
            bias = delta if bias is None else bias + delta
            deltas.append(pair(delta))
            if i % 2 and i < K - 1:
                yield
        d2 = jnp.concatenate(deltas, 0)
        acc_be[l] += jnp.sum(bias.reshape(nodes // 8, 8, D), 0)
        yield
        product = dot(d2, w_e2t[l])
        yield
        acc_e2[l] += dot_t(jnp.concatenate(hidden, 0), d2)
        yield
        near = None
        for i in range(K):
            d1 = halves(product[i * nodes : (i + 1) * nodes]) * rises[i]
            near = d1 if near is None else near + d1
            mine[i, pl.ds(RIM, nodes), :] = d1
            if i == K // 2 - 1:
                yield
        yield
        far = None
        left = None
        right = None
        for i, o in enumerate(OFFSETS):
            part = mine[i, pl.ds(RIM - o, nodes), :]
            far = part if far is None else far + part
            if o < 0:
                part = mine[i, pl.ds(-o, RIM), :]
                left = part if left is None else left + part
            else:
                part = mine[i, pl.ds(RIM + nodes - o, RIM), :]
                right = part if right is None else right + part
        rims = jnp.concatenate([left, right], 0)
        head, tail = split(near)
        head_f, tail_f = split(far)
        head_r, tail_r = split(rims)
        nothing = jnp.zeros((2 * RIM, D), BF16)
        dxh[slot, s, pl.ds(0, nodes), :] = jnp.concatenate([head, head_f], 1)
        dxl[slot, s, pl.ds(0, nodes), :] = jnp.concatenate([tail, tail_f], 1)
        dxh[slot, s, pl.ds(nodes, 2 * RIM), :] = jnp.concatenate([nothing, head_r], 1)
        dxl[slot, s, pl.ds(nodes, 2 * RIM), :] = jnp.concatenate([nothing, tail_r], 1)
        yield

    def leave_weights(p):
        l, g = LAYERS - 1 - div(p, GROUPS), rem(p, GROUPS)
        base = g * per
        size = per * ext
        slot = rem(p, 2)
        x = rows_of(xs, l, base, 0, ext)
        side = xa[pl.ds(base, per)].reshape(size, D)
        inputs = jnp.concatenate([x, side[:, : 2 * AUX]], 1)
        high = dxh[slot].reshape(size, 2 * D)
        low = dxl[slot].reshape(size, 2 * D)
        acc_x[l] += dot_t(
            jnp.concatenate([inputs, inputs], 0), jnp.concatenate([high, low], 0)
        )
        yield

    def leave_state(p):
        l, g = LAYERS - 1 - div(p, GROUPS), rem(p, GROUPS)
        base = g * per
        size = per * ext
        slot = rem(p, 2)
        event = phases + p
        back = div(p, GROUPS)
        own = GROUPS * l + g
        high = dxh[slot].reshape(size, 2 * D)
        low = dxl[slot].reshape(size, 2 * D)
        product = dot(high, w_ep[l]) + dot(low, w_ep[l])
        yield
        product = halves(product)
        for c in range(per):
            t, at = base + c, c * ext
            new = dst[t] + product[at : at + nodes]
            dst[t] = new
            rims = product[at + nodes : at + ext]
            rs[back, 0, t] = rims[:RIM]
            rs[back, 1, t] = rims[RIM:]
            y = (raw[l, t] - fin[own, 0, pl.ds(c, 1), :]) * fin[own, 1, pl.ds(c, 1), :]
            stat[0][event, pl.ds(2 * per + c, 1), :] = jnp.sum(new, 0, keepdims=True) + jnp.sum(
                rims, 0, keepdims=True
            )
            stat[0][event, pl.ds(3 * per + c, 1), :] = jnp.sum(
                new * y, 0, keepdims=True
            ) + jnp.sum(rims * yh[t], 0, keepdims=True)
            if c % 2:
                yield

    def backward(p, _):
        @pl.when(p > 0)
        def _():
            weave(
                ORDER_LEAVE,
                back_edges(p, 0),
                back_edges(p, 1),
                leave_weights(p - 1),
                leave_state(p - 1),
            )

        @pl.when(p == 0)
        def _():
            weave(ORDER_BACK, back_edges(p, 0), back_edges(p, 1))
            stat_forward(phases - 1)

        @pl.when(p > 0)
        def _():
            ring_send(*grad_rims(p - 1), GROUPS + p, 1)

        @pl.when((p > 0) & (p <= GROUPS))
        def _():
            stat_send(phases + p - 1, 0)

        @pl.when(p == GROUPS)
        def _():
            unit_second(unit.at[1], acc_e2.at[1])
            edge_unit(1, unit.at[1])

        sum_hook(SUMS_MID, p)

        def ready():
            stat_finish(GROUPS + p + 1)

        def rims_ready():
            arrived(grad_rims(p + 1 - GROUPS)[1], rim_rsem.at[p + 2])

        alone = (p + 1 == GROUPS) | (p + 1 == phases)
        pl.when(negated(alone))(ready)
        pl.when((p + 1 > GROUPS) & (p + 1 < phases))(rims_ready)

        @pl.when(negated(alone))
        def _():
            weave(ORDER_BACK_NODE, back_edges(p, 2), back_edges(p, 3), back_node(p + 1))

        @pl.when(alone)
        def _():
            weave(ORDER_BACK, back_edges(p, 2), back_edges(p, 3))

        @pl.when((p > 0) & (p <= GROUPS))
        def _():
            stat_forward(phases + p - 1)

        @pl.when(p + 1 == GROUPS)
        def _():
            ready()
            rims_ready()
            weave("", back_node(p + 1))

        @pl.when(p == GROUPS - 2)
        def _():
            node_unit(1, unit.at[0])

        @pl.when(p == phases - 2)
        def _():
            node_unit(0, unit.at[2])

        sum_hook(SUMS_END, p)

        return 0

    def quarter(acc, rows):
        return (
            acc[pl.ds(0, rows), pl.ds(0, D)]
            + acc[pl.ds(D, rows), pl.ds(0, D)]
            + acc[pl.ds(0, rows), pl.ds(D, D)]
            + acc[pl.ds(D, rows), pl.ds(D, D)]
        )

    def fold8(value):
        return jnp.sum(value, 0, keepdims=True)

    def unit_second(out, acc):
        out[pl.ds(0, D), :] = quarter(acc, D)

    def node_unit(l, out):
        unit_second(out, acc_n2.at[l])
        out[pl.ds(UNIT_FIRST, D), :] = quarter(acc_nx.at[l], D)
        out[pl.ds(UNIT_FIRST + D, D), :] = quarter(acc_agg.at[l], D)
        side = acc_nx[l, pl.ds(2 * D, AUX), :] + acc_nx[l, pl.ds(2 * D + AUX, AUX), :]
        out[pl.ds(UNIT_AUX, AUX), :] = halves(side)
        out[pl.ds(UNIT_AUX + A_SECOND, 1), :] = fold8(acc_bn[l])

    def edge_unit(l, out):
        both = acc_x[l, pl.ds(0, D), :] + acc_x[l, pl.ds(D, D), :]
        out[pl.ds(UNIT_FIRST, D), :] = both[:, :D]
        out[pl.ds(UNIT_FIRST + D, D), :] = both[:, D:]
        side = acc_x[l, pl.ds(2 * D, AUX), :] + acc_x[l, pl.ds(2 * D + AUX, AUX), :]
        row = lax.broadcasted_iota(jnp.int32, (AUX, D), 0)
        both = side[:, :D] - side[:, D:]
        out[pl.ds(UNIT_AUX, AUX), :] = jnp.where(
            row < TW, both, jnp.where(row == A_PLACE, both * (1.0 / HALO), side[:, :D])
        )
        out[pl.ds(UNIT_AUX + A_SECOND, 1), :] = fold8(acc_be[l])

    shares = len(links.share_stages)
    pieces = [1]
    for stage in range(shares):
        pieces.append(pieces[-1] * links.share_size(stage))
    lead, unit_rows = unit_sizes(graph)
    sums = (
        (0, 0, unit_rows),
        (1, 0, unit_rows),
        (2, 0, unit_rows),
        (3, 0, lead),
        (3, lead, unit_rows - lead),
    )
    steps = 2 * shares + len(swaps)

    def sum_step(n, step):
        u, start, rows = sums[n]

        def segment(stage, digit=None):
            place = start
            for k in range(stage):
                mine = links.share_digit(k) if digit is None or k < stage - 1 else digit
                place = place + mine * (rows // pieces[k + 1])
            return pl.ds(pl.multiple_of(place, 8), rows // pieces[stage])

        def part(stage):
            return pl.ds(start // pieces[stage], rows // pieces[stage])

        def others(stage):
            return range(1, links.share_size(stage))

        last = part(shares)
        done = step - 1
        value = None
        if 0 <= done < shares:
            into = unit_recv[done].at[u, :, part(done + 1)]
            arrived(into, share_rsem.at[done, n])
            value = unit[u, segment(done + 1), :]
            for shift in others(done):
                value = value + into[shift - 1]
        elif 0 <= done < shares + len(swaps):
            stage = done - shares
            into = swap_recv[stage].at[u, :, last]
            arrived(into, swap_rsem[stage].at[n])
            value = swap[stage][u, last, :]
            for shift in range(1, swaps[stage][1]):
                value = value + into[shift - 1]
        elif done >= 0:
            stage = steps - 1 - done
            arrived(unit_recv[stage].at[u, :, part(stage + 1)], share_rsem.at[shares + stage, n])
        if step < shares:
            if value is not None:
                unit[u, segment(step), :] = value
            for shift in others(step):
                peer, digit = links.share_peer(step, shift)
                remote(
                    unit.at[u, segment(step + 1, digit)],
                    unit_recv[step].at[u, shift - 1, part(step + 1)],
                    share_ssem.at[step],
                    share_rsem.at[step, n],
                    peer,
                ).start()
        elif step < shares + len(swaps):
            stage = step - shares
            swap[stage][u, last, :] = value
            stride, size = swaps[stage]
            for shift in range(1, size):
                remote(
                    swap[stage].at[u, last],
                    swap_recv[stage].at[u, shift - 1, last],
                    swap_ssem[stage].at[0],
                    swap_rsem[stage].at[n],
                    links.digit_peer(stride, size, shift),
                ).start()
        elif step < steps:
            if value is not None:
                unit_all[u, segment(shares), :] = value
            stage = steps - 1 - step
            for shift in others(stage):
                mine = segment(stage + 1)
                remote(
                    unit_all.at[u, mine],
                    unit_all.at[u, mine],
                    share_ssem.at[shares + stage],
                    share_rsem.at[shares + stage, n],
                    links.share_peer(stage, shift)[0],
                ).start()

    def sum_hook(table, p):
        for phase, n, step in table:
            pl.when(p == phase)(functools.partial(sum_step, n, step))

    for g in range(GROUPS):
        first_main(g)
    arrived(first[1], rim_rsem.at[0])
    first_rims()
    for p in range(phases):
        forward(p, 0)
    weave("", node(phases - 1))
    stat_send(phases - 1, 0)
    back_weights()
    stat_finish(GROUPS)
    weave("", back_node(0))
    for p in range(phases):
        backward(p, 0)
    unit_second(unit.at[3], acc_e2.at[0])
    sum_step(3, 0)
    weave("", leave_weights(phases - 1))
    edge_unit(0, unit.at[3])
    sum_step(4, 0)
    weave("", leave_state(phases - 1))
    ring_send(*grad_rims(phases - 1), GROUPS + phases, 1)
    done = {n: 0 for n in range(len(sums))}
    for table in (SUMS_MID, SUMS_END):
        for _, n, step in table:
            done[n] = max(done[n], step)
    for turn in range(2 * steps):
        for n in SUMS_TURNS[min(turn, len(SUMS_TURNS) - 1)]:
            if done[n] < steps:
                done[n] += 1
                sum_step(n, done[n])
        if turn:
            continue
        for g in range(GROUPS):
            arrived(grad_rims(phases - GROUPS + g)[1], rim_rsem.at[phases + 1 + g])
            for c in range(per):
                t = g * per + c
                dst[t, pl.ds(0, RIM), :] += rr[LAYERS, 1, t]
                dst[t, pl.ds(nodes - RIM, RIM), :] += rr[LAYERS, 0, t]

    arrived(hr, rim_ssem.at[0])
    arrived(rs, rim_ssem.at[1])
    for stage in range(len(stages)):
        arrived(stat_recv[stage].at[pl.ds(0, phases)], stat_ssem[stage].at[0])
    for stage in range(len(swaps)):
        arrived(swap_recv[stage], swap_ssem[stage].at[0])
    for stage in range(shares):
        for way in range(2):
            arrived(unit_recv[stage], share_ssem.at[way * shares + stage])


def unit_sizes(graph):
    share = 8 * 4 * graph
    lead = -(-UNIT_FIRST // share) * share
    return lead, lead + -(-(UNIT_ROWS - UNIT_FIRST) // share) * share


def assemble(
    raw,
    grad_mid,
    units,
    state_out,
    grad_out,
    g_ew1,
    g_eb1,
    g_ew2,
    g_eb2,
    g_nw1,
    g_nb1,
    g_nw2,
    g_nb2,
    sems,
):
    parts = sems.shape[1]
    rows = state_out.shape[0] // parts
    copies = []
    for i, (src, dst) in enumerate(((raw.at[LAYERS], state_out), (grad_mid, grad_out))):
        for part in range(parts):
            cut = pl.ds(part * rows, rows)
            copies.append(pltpu.make_async_copy(src.at[cut], dst.at[cut], sems.at[i, part]))
    for copy in copies:
        copy.start()
    for l in range(LAYERS):
        node, edge = units.at[2 * (LAYERS - 1 - l)], units.at[2 * (LAYERS - 1 - l) + 1]
        for unit, first, bias1, second, bias2 in (
            (node, g_nw1, g_nb1, g_nw2, g_nb2),
            (edge, g_ew1, g_eb1, g_ew2, g_eb2),
        ):
            first[pl.ds(0, 2 * D), l, :] = unit[pl.ds(UNIT_FIRST, 2 * D), :]
            bias1[pl.ds(l, 1), :] = unit[pl.ds(UNIT_AUX + A_ONE, 1), :]
            second[l] = unit[pl.ds(0, D), :]
            bias2[pl.ds(l, 1), :] = unit[pl.ds(UNIT_AUX + A_SECOND, 1), :]
        g_nw1[pl.ds(2 * D, NPAR), l, :] = node[pl.ds(UNIT_AUX + A_THETA, NPAR), :]
        g_ew1[pl.ds(2 * D, TW), l, :] = edge[pl.ds(UNIT_AUX, TW), :]
        g_ew1[pl.ds(2 * D + TW, 1), l, :] = edge[pl.ds(UNIT_AUX + A_PLACE, 1), :]
        g_ew1[pl.ds(2 * D + TW + 1, NPAR), l, :] = edge[pl.ds(UNIT_AUX + A_THETA, NPAR), :]
    for copy in copies:
        copy.wait()


def on_device(
    blk,
    graph,
    node_state,
    field_window,
    edge_offset,
    pde_id,
    pde_table,
    cotangent,
    edge_w1,
    edge_b1,
    edge_w2,
    edge_b2,
    node_w1,
    node_b1,
    node_w2,
    node_b2,
):
    traj, nodes, _ = node_state.shape
    per = traj // GROUPS
    ext = nodes + 2 * RIM
    field = jnp.transpose(field_window, (2, 0, 1)).reshape(TW * traj, nodes)
    offset = jnp.transpose(edge_offset, (2, 0, 1)).reshape(K * traj, nodes)
    table = jnp.transpose(pde_table, (1, 0))
    ew1 = jnp.transpose(edge_w1, (1, 0, 2))
    nw1 = jnp.transpose(node_w1, (1, 0, 2))
    vmem = pl.BlockSpec(memory_space=pltpu.VMEM)
    any_space = pl.BlockSpec(memory_space=pl.ANY)
    stages = digit_stages(blk, STAT_SIZES)
    swaps = digit_stages(blk // 4, (4,))
    shares = 4 * graph
    _, rows = unit_sizes(graph)
    seg = rows // shares
    events = 3 * GROUPS

    def f(*shape):
        return pltpu.VMEM(shape, F32)

    def b(*shape):
        return pltpu.VMEM(shape, BF16)

    L = LAYERS
    scratch = [
        f(TW * traj, nodes),
        pltpu.VMEM((K * traj, nodes), jnp.int32),
        pltpu.SMEM((traj,), jnp.int32),
        pltpu.SMEM((NPAR, NPDE), F32),
        f(L, -(-EDGE_IN // 8) * 8, D),
        f(L, D),
        f(L, D, D),
        f(L, D),
        f(L, -(-NODE_IN // 8) * 8, D),
        f(L, D),
        f(L, D, D),
        f(L, D),
        b(L, 4 * D, 3 * D),
        b(L, 2 * D, 2 * D),
        b(L, 2 * D, 2 * D),
        b(L, 2 * D, 2 * D),
        b(L, 2 * D, 2 * D),
        b(L, 2 * D, 2 * D),
        b(L, 3 * D, 2 * D),
        b(L, 2 * D, 2 * D),
        f(AUX, 3 * D),
        b(D, K * D),
        f(8 * traj, nodes),
        f(traj, K * nodes, D),
        f(traj, AUX, nodes),
        b(L, traj, ext, 2 * D),
        b(traj, ext, D),
        f(L, traj, nodes, D),
        f(L, traj, ext, D),
        f(GROUPS, per, nodes, D),
        f(L, traj, K * nodes, D),
        b(L, traj, nodes, 2 * D),
        b(L, traj, nodes, 2 * D),
        f(L, traj, nodes, D),
        f(L, traj, nodes, D),
        f(traj, 2 * RIM, D),
        f(2, per, nodes, D),
        f(2, K, ext, D),
        b(2, per, ext, 2 * D),
        b(2, per, ext, 2 * D),
        f(L, 2 * D, 2 * D),
        f(L, 2 * D, 2 * D),
        f(L, 2 * D + 2 * AUX, 2 * D),
        f(L, 2 * D, 2 * D),
        f(L, 2 * D + 2 * AUX, 2 * D),
        f(L, 8, D),
        f(L, 8, D),
        f(events + GROUPS, 4, per, D),
        f(2, 1 + L, traj, RIM, D),
        f(2, 2, traj, RIM, D),
        f(L, 2, traj, RIM, D),
        f(L + 1, 2, traj, RIM, D),
        f(4, rows, D),
        pltpu.SemaphoreType.DMA((16,)),
        pltpu.SemaphoreType.DMA((2,)),
        pltpu.SemaphoreType.DMA((1 + 3 * GROUPS,)),
        pltpu.SemaphoreType.DMA((4,)),
        pltpu.SemaphoreType.DMA((4, 5)),
    ]
    scratch += [f(events + GROUPS, 4 * per, D) for _ in stages]
    scratch += [f(events, size - 1, 4 * per, D) for _, size in stages]
    scratch += [pltpu.SemaphoreType.DMA((1,)) for _ in stages]
    scratch += [pltpu.SemaphoreType.DMA((events,)) for _ in stages]
    scratch += [f(4, seg, D) for _ in swaps]
    scratch += [f(4, size - 1, seg, D) for _, size in swaps]
    scratch += [pltpu.SemaphoreType.DMA((1,)) for _ in swaps]
    scratch += [pltpu.SemaphoreType.DMA((5,)) for _ in swaps]
    scratch += [f(4, 1, rows // 2, D), f(4, 2 * graph - 1, seg, D)]
    hbm = any_space
    mid = pl.pallas_call(
        functools.partial(kernel_body, blk, graph),
        out_shape=[f(L + 1, traj, nodes, D), f(traj, nodes, D), f(4, rows, D)],
        in_specs=[hbm] * 14,
        out_specs=[vmem] * 3,
        scratch_shapes=scratch,
        compiler_params=pltpu.CompilerParams(
            collective_id=0, has_side_effects=True, vmem_limit_bytes=54 * 2**20
        ),
        name="processor",
    )(
        node_state,
        field,
        offset,
        pde_id,
        table,
        cotangent,
        ew1,
        edge_b1,
        edge_w2,
        edge_b2,
        nw1,
        node_b1,
        node_w2,
        node_b2,
    )
    mid = [pltpu.with_memory_space_constraint(part, pltpu.VMEM) for part in mid]
    shapes = [
        (traj, nodes, D),
        (traj, nodes, D),
        (EDGE_IN, L, D),
        (L, D),
        (L, D, D),
        (L, D),
        (NODE_IN, L, D),
        (L, D),
        (L, D, D),
        (L, D),
    ]
    out = pl.pallas_call(
        assemble,
        out_shape=[jax.ShapeDtypeStruct(shape, F32) for shape in shapes],
        in_specs=[vmem] * 3,
        out_specs=[any_space, any_space] + [vmem] * 8,
        scratch_shapes=[pltpu.SemaphoreType.DMA((2, 8))],
        compiler_params=pltpu.CompilerParams(vmem_limit_bytes=8 * 2**20),
        name="assemble",
    )(*mid)
    out = list(out)
    out[2] = jnp.transpose(out[2], (1, 0, 2))
    out[6] = jnp.transpose(out[6], (1, 0, 2))
    return tuple(out)


def solution(mesh):
    rows = P("graph", "blk", None)
    return jax.shard_map(
        functools.partial(on_device, mesh.shape["blk"], mesh.shape["graph"]),
        mesh=mesh,
        in_specs=(rows, rows, rows, P("graph"), P(), rows) + (P(),) * 8,
        out_specs=(rows, rows) + (P(),) * 8,
        check_vma=False,
    )
```

```python
import functools

import jax
import jax.numpy as jnp
from jax import lax
from jax.experimental import pallas as pl
from jax.experimental.pallas import tpu as pltpu
from jax.sharding import PartitionSpec as P

D = 128
TW = 25
NPAR = 3
K = 6
HALO = 3
NPDE = 8
LAYERS = 2
EDGE_IN = 2 * D + TW + 1 + NPAR
NODE_IN = 2 * D + NPAR
OFFSETS = tuple(o for o in range(-HALO, HALO + 1) if o != 0)

EPSILON = 1e-05
RIM = 8
GROUPS = 4
AUX = 32
A_THETA = TW
A_ONE = TW + NPAR
A_PLACE = TW + NPAR + 1
A_SECOND = TW + NPAR + 2
UNIT_FIRST = D
UNIT_AUX = 3 * D
UNIT_ROWS = UNIT_AUX + AUX
STAT_SIZES = (2, 8)
HAND_ON = 12
SUMS_MID = ((3, 0, 1), (4, 1, 0), (5, 1, 1), (5, 0, 2), (7, 2, 1), (7, 1, 2))
SUMS_END = ((2, 0, 0), (6, 0, 3), (6, 2, 0))
SUMS_TURNS = ((3, 4, 2, 0), (3, 4, 1), (2, 3, 4, 1, 0))
ORDER_NODE = "0011000122210012011020"
ORDER_EDGES = "00001000111111"
ORDER_ENTER = "02002011202000111112"
ORDER_LEAVE = "00003000211013111131"
ORDER_BACK = "1010001110001101"
ORDER_BACK_NODE = "0201102202221122200111010"

F32 = jnp.float32
BF16 = jnp.bfloat16
MESH = pl.DeviceIdType.MESH


def dot(left, right):
    return jnp.dot(left, right, preferred_element_type=F32)


def dot_t(left, right):
    return lax.dot_general(left, right, (((0,), (0,)), ((), ())), preferred_element_type=F32)


def split(value):
    head = value.astype(BF16)
    tail = (value - head.astype(F32)).astype(BF16)
    return head, tail


def pair(value):
    head, tail = split(value)
    return jnp.concatenate([head, tail], 1)


def halves(product):
    return product[:, :D] + product[:, D:]


def doubled(weight):
    both = pair(weight)
    return jnp.concatenate([both, both], 0)


def swish_parts(half):
    t = jnp.tanh(half)
    u = 1.0 + t
    act = half * u
    return act, u + act * (1.0 - t)


def digit_stages(count, sizes):
    stages, stride, step = [], 1, 0
    while stride < count:
        size = sizes[min(step, len(sizes) - 1)]
        while count // stride % size:
            size -= 1
        stages.append((stride, size))
        stride *= size
        step += 1
    return stages


class Links:
    def __init__(self, blk, graph):
        self.blk, self.graph = blk, graph
        self.me = lax.axis_index("blk")
        self.mine = lax.axis_index("graph")
        self.stat_stages = digit_stages(blk, STAT_SIZES)
        self.share_stages = [[("blk", 1, 2)], [("blk", 2, 2), ("graph", 1, graph)]]
        self.swap_stages = [(stride * 4, size) for stride, size in digit_stages(blk // 4, (4,))]

    def ring(self, shift):
        return (self.mine, lax.rem(self.me + shift + self.blk, self.blk))

    def digit_peer(self, stride, size, shift):
        digit = lax.rem(self.me // stride, size)
        other = lax.rem(digit + shift, size)
        return (self.mine, self.me + (other - digit) * stride)

    def share_size(self, stage):
        size = 1
        for _, _, count in self.share_stages[stage]:
            size *= count
        return size

    def share_digit(self, stage):
        value = 0
        for axis, stride, size in self.share_stages[stage]:
            place = self.me if axis == "blk" else self.mine
            value = value * size + lax.rem(place // stride, size)
        return value

    def share_peer(self, stage, shift):
        other = lax.rem(self.share_digit(stage) + shift, self.share_size(stage))
        coords = {"blk": self.me, "graph": self.mine}
        rest = other
        for axis, stride, count in reversed(self.share_stages[stage]):
            place = coords[axis]
            now = lax.rem(place // stride, count)
            coords[axis] = place + (lax.rem(rest, count) - now) * stride
            rest = rest // count
        return (coords["graph"], coords["blk"]), other

    def greeted(self):
        peers = [self.ring(1), self.ring(-1)]
        for stride, size in self.stat_stages + self.swap_stages:
            peers += [self.digit_peer(stride, size, shift) for shift in range(1, size)]
        for stage in range(len(self.share_stages)):
            peers += [self.share_peer(stage, shift)[0] for shift in range(1, self.share_size(stage))]
        return peers


def div(value, by):
    return value // by if isinstance(value, int) else lax.div(value, jnp.int32(by))


def rem(value, by):
    return value % by if isinstance(value, int) else lax.rem(value, jnp.int32(by))


def negated(condition):
    return not condition if isinstance(condition, bool) else jnp.logical_not(condition)


def weave(order, *parts):
    for name in order:
        next(parts[int(name)], None)
    for part in parts:
        for _ in part:
            pass


def remote(src, dst, send_sem, recv_sem, device):
    return pltpu.make_async_remote_copy(
        src_ref=src,
        dst_ref=dst,
        send_sem=send_sem,
        recv_sem=recv_sem,
        device_id=device,
        device_id_type=MESH,
    )


def kernel_body(
    blk,
    graph,
    state_hbm,
    field_hbm,
    offset_hbm,
    id_hbm,
    table_hbm,
    cot_hbm,
    ew1_hbm,
    eb1_hbm,
    ew2_hbm,
    eb2_hbm,
    nw1_hbm,
    nb1_hbm,
    nw2_hbm,
    nb2_hbm,
    raw,
    dst,
    unit_all,
    field_in,
    offset_in,
    id_in,
    table_in,
    ew1,
    eb1,
    ew2,
    eb2,
    nw1,
    nb1,
    nw2,
    nb2,
    w_in,
    w_e2,
    w_e2t,
    w_agg,
    w_n2,
    w_n2t,
    w_np,
    w_ep,
    w_aux,
    spread,
    counts,
    weigh,
    aux_t,
    xs,
    xa,
    a_buf,
    r_buf,
    n_buf,
    slope,
    agg2,
    hid2,
    sn1,
    sn2,
    yh,
    dag,
    e1,
    dxh,
    dxl,
    acc_n2,
    acc_agg,
    acc_nx,
    acc_e2,
    acc_x,
    acc_bn,
    acc_be,
    fin,
    hs,
    hr,
    rs,
    rr,
    unit,
    load_sem,
    rim_ssem,
    rim_rsem,
    share_ssem,
    share_rsem,
    *staged,
):
    _, traj, nodes, _ = raw.shape
    state_in = raw.at[0]
    per = traj // GROUPS
    ext = nodes + 2 * RIM
    total = float(nodes * blk)
    links = Links(blk, graph)
    stages = links.stat_stages
    phases = LAYERS * GROUPS
    swaps = links.swap_stages
    staged = list(staged)
    stat, stat_recv, stat_ssem, stat_rsem = [
        [staged.pop(0) for _ in stages] for _ in range(4)
    ]
    swap, swap_recv, swap_ssem, swap_rsem = [
        [staged.pop(0) for _ in swaps] for _ in range(4)
    ]
    unit_recv = staged

    parts = [
        (offset_hbm, offset_in),
        (field_hbm, field_in),
        (id_hbm, id_in),
        (table_hbm, table_in),
        (state_hbm, raw.at[0]),
        (eb1_hbm, eb1),
        (eb2_hbm, eb2),
        (nb1_hbm, nb1),
        (nb2_hbm, nb2),
        (ew2_hbm, ew2),
        (nw2_hbm, nw2),
        (cot_hbm, dst),
    ]
    for l in range(LAYERS):
        parts.append((ew1_hbm.at[:, l, :], ew1.at[l, pl.ds(0, EDGE_IN), :]))
        parts.append((nw1_hbm.at[:, l, :], nw1.at[l, pl.ds(0, NODE_IN), :]))
    loads = [pltpu.make_async_copy(src, to, load_sem.at[i]) for i, (src, to) in enumerate(parts)]
    for load in loads:
        load.start()

    barrier = pltpu.get_barrier_semaphore()
    greeted = links.greeted()
    for peer in greeted:
        pl.semaphore_signal(barrier, inc=1, device_id=peer, device_id_type=MESH)

    rows = lax.broadcasted_iota(jnp.int32, (D, K * D), 0)
    cols = lax.broadcasted_iota(jnp.int32, (D, K * D), 1)
    spread[...] = jnp.where(rows == 3 * AUX + cols // D, 1.0, 0.0).astype(BF16)
    aux_t[...] = jnp.zeros_like(aux_t)
    e1[...] = jnp.zeros_like(e1)
    for acc in (acc_n2, acc_agg, acc_nx, acc_e2, acc_x, acc_bn, acc_be):
        acc[...] = jnp.zeros_like(acc)
    for u in range(4):
        rest = unit.shape[1] - UNIT_ROWS
        unit[u, pl.ds(UNIT_ROWS, rest), :] = jnp.zeros((rest, D), F32)
    place = lax.broadcasted_iota(jnp.int32, (1, nodes), 1).astype(F32) - nodes / 2
    loads[0].wait()
    offs = [offset_in[pl.ds(k * traj, traj), :] for k in range(K)]
    for i, o in enumerate(OFFSETS):
        many = jnp.zeros((traj, nodes), F32)
        for k in range(K):
            many = many + jnp.where(offs[k] == o, 1.0, 0.0)
        counts[pl.ds(i * traj, traj), :] = many
    counts[pl.ds(K * traj, 2 * traj), :] = jnp.zeros((2 * traj, nodes), F32)
    for load in loads[1:5]:
        load.wait()

    near_row = lax.broadcasted_iota(jnp.int32, (RIM, D), 0)

    for t in range(traj):
        tile = aux_t.at[t]
        tile[pl.ds(0, TW), :] = field_in[pl.ds(t, TW, stride=traj), :]
        row = id_in[t]
        for q in range(NPAR):
            tile[pl.ds(A_THETA + q, 1), :] = jnp.full((1, nodes), table_in[q, row], F32)
        tile[pl.ds(A_ONE, 1), :] = jnp.ones((1, nodes), F32)
        tile[pl.ds(A_PLACE, 1), :] = place
    for t in range(traj):
        head, tail = split(aux_t[t])
        head, tail = head.astype(F32), tail.astype(F32)
        full = jnp.concatenate(
            [
                head,
                tail,
                head,
                counts[pl.ds(t, 8, stride=traj), :],
                jnp.zeros((D - 3 * AUX - 8, nodes), F32),
            ],
            0,
        )
        back = full.T
        ahead, behind = raw[0, t, pl.ds(0, RIM), :], raw[0, t, pl.ds(nodes - RIM, RIM), :]
        hs[0, 0, t] = jnp.where(near_row < HALO, ahead, pltpu.roll(back[:RIM], HALO, 0))
        hs[1, 0, t] = jnp.where(
            near_row >= RIM - HALO, behind, pltpu.roll(back[nodes - RIM :], RIM - HALO, 0)
        )
        xa[t, pl.ds(0, nodes), :] = back.astype(BF16)

    pl.semaphore_wait(barrier, len(greeted))

    def ring_send(src, dst, kind, back=0):
        for way in range(2):
            remote(
                src.at[way],
                dst.at[way],
                rim_ssem.at[back],
                rim_rsem.at[kind],
                links.ring(1 if way else -1),
            ).start()

    def arrived(dst, sem):
        pltpu.make_async_copy(dst, dst, sem).wait()

    first = hs.at[:, 0], hr.at[:, 0]
    ring_send(*first, 0)

    def layer_rims(g):
        cut = pl.ds(g * per, per)
        return hs.at[:, 1, cut], hr.at[:, 1, cut]

    def grad_rims(p):
        cut = pl.ds(rem(p, GROUPS) * per, per)
        back = div(p, GROUPS)
        return rs.at[back, :, cut], rr.at[back + 1, :, cut]


    def multiply(j, _):
        for c in range(per):
            t = j * per + c
            many = dot(xa[t, pl.ds(0, nodes), :], spread[...])
            for i in range(K):
                weigh[t, pl.ds(i * nodes, nodes), :] = many[:, i * D : (i + 1) * D]
        return 0

    lax.fori_loop(0, GROUPS, multiply, 0)
    for load in loads[5:]:
        load.wait()
    for l in range(LAYERS):
        w_self = ew1[l, pl.ds(0, D), :]
        w_far = ew1[l, pl.ds(D, D), :]
        n_self = nw1[l, pl.ds(0, D), :]
        n_agg = nw1[l, pl.ds(D, D), :]
        for i, w in enumerate((w_self, w_far, n_self)):
            head, tail = split(0.5 * w)
            cut = pl.ds(i * D, D)
            w_in[l, pl.ds(0, D), cut] = head
            w_in[l, pl.ds(D, D), cut] = head
            w_in[l, pl.ds(2 * D, D), cut] = tail
        w_field = 0.5 * ew1[l, pl.ds(2 * D, TW), :]
        w_place = (0.5 / HALO) * ew1[l, pl.ds(2 * D + TW, 1), :]
        w_theta = 0.5 * ew1[l, pl.ds(2 * D + TW + 1, NPAR), :]
        n_theta = 0.5 * nw1[l, pl.ds(2 * D, NPAR), :]
        w_aux[...] = jnp.zeros_like(w_aux)
        w_aux[pl.ds(0, TW), pl.ds(0, D)] = w_field
        w_aux[pl.ds(0, TW), pl.ds(D, D)] = -w_field
        w_aux[pl.ds(A_THETA, NPAR), pl.ds(0, D)] = w_theta
        w_aux[pl.ds(A_THETA, NPAR), pl.ds(2 * D, D)] = n_theta
        w_aux[pl.ds(A_ONE, 1), pl.ds(0, D)] = 0.5 * eb1[pl.ds(l, 1), :]
        w_aux[pl.ds(A_ONE, 1), pl.ds(2 * D, D)] = 0.5 * nb1[pl.ds(l, 1), :]
        w_aux[pl.ds(A_PLACE, 1), pl.ds(0, D)] = w_place
        w_aux[pl.ds(A_PLACE, 1), pl.ds(D, D)] = -w_place
        head, tail = split(w_aux[...])
        w_in[l, pl.ds(3 * D, AUX), :] = head
        w_in[l, pl.ds(3 * D + AUX, AUX), :] = head
        w_in[l, pl.ds(3 * D + 2 * AUX, AUX), :] = tail
        w_in[l, pl.ds(3 * D + 3 * AUX, AUX), :] = jnp.zeros((AUX, 3 * D), BF16)
        second = 0.5 * ew2[l]
        w_e2[l] = doubled(second)
        w_agg[l] = doubled(0.5 * n_agg)
        w_n2[l] = doubled(0.5 * nw2[l])

    def back_weights():
        for l in range(LAYERS):
            w_e2t[l] = doubled(0.5 * ew2[l].T)
            w_n2t[l] = doubled(nw2[l].T)
            n_self = nw1[l, pl.ds(0, D), :]
            n_agg = nw1[l, pl.ds(D, D), :]
            head, tail = split(jnp.concatenate([n_self.T, 0.5 * n_agg.T], 1))
            w_np[l, pl.ds(0, D), :] = head
            w_np[l, pl.ds(D, D), :] = head
            w_np[l, pl.ds(2 * D, D), :] = tail
            w_ep[l, pl.ds(0, D), :] = pair(ew1[l, pl.ds(0, D), :].T)
            w_ep[l, pl.ds(D, D), :] = pair(ew1[l, pl.ds(D, D), :].T)

    kinds = (
        (0, GROUPS, pl.ds(0, 2 * per)),
        (GROUPS, phases, pl.ds(0, 4 * per)),
        (phases, phases + GROUPS, pl.ds(2 * per, 2 * per)),
    )

    def by_kind(event, action):
        for low, high, cut in kinds:
            if isinstance(event, int):
                if low <= event < high:
                    action(cut)
            else:
                pl.when((event >= low) & (event < high))(functools.partial(action, cut))

    def stat_send(event, stage):
        stride, size = stages[stage]

        def send(cut):
            for shift in range(1, size):
                remote(
                    stat[stage].at[event, cut],
                    stat_recv[stage].at[event, shift - 1, cut],
                    stat_ssem[stage].at[0],
                    stat_rsem[stage].at[event],
                    links.digit_peer(stride, size, shift),
                ).start()

        by_kind(event, send)

    def stat_merge(event, stage):
        stride, size = stages[stage]
        by_kind(
            event,
            lambda cut: arrived(stat_recv[stage].at[event, :, cut], stat_rsem[stage].at[event]),
        )
        parts = [stat[stage].at[event]] + [
            stat_recv[stage].at[event, shift - 1] for shift in range(1, size)
        ]
        forward_rows, gradient_rows = event < phases, event >= GROUPS

        def row(q):
            return [part[pl.ds(q * per, per), :] for part in parts]

        mean = m2_all = u_all = c_all = None
        if gradient_rows:
            u, c = row(2), row(3)
            u_all = sum(u[1:], u[0])
            c_all = sum(c[1:], c[0])
        if forward_rows:
            m, m2 = row(0), row(1)
            mean = sum(m[1:], m[0]) * (1.0 / size)
            gaps = [value - mean for value in m]
            spread2 = sum((gap * gap for gap in gaps[1:]), gaps[0] * gaps[0])
            m2_all = sum(m2[1:], m2[0]) + spread2 * float(nodes * stride)
            if gradient_rows:
                for gap, value in zip(gaps, u):
                    c_all = c_all + gap * value
        return mean, m2_all, u_all, c_all

    def stat_forward(event):
        for stage in range(1, len(stages)):
            merged = stat_merge(event, stage - 1)
            for q, value in enumerate(merged):
                if value is not None:
                    stat[stage][event, pl.ds(q * per, per), :] = value
            stat_send(event, stage)

    def stat_finish(event):
        mean, m2, u, c = stat_merge(event, len(stages) - 1)
        at = event + GROUPS
        if mean is not None:
            scale = lax.rsqrt(m2 * (1.0 / total) + EPSILON)
            fin[at, 0] = mean
            fin[at, 1] = scale
        if u is not None:
            fin[at, 2] = u * (1.0 / total)
            fin[at, 3] = c * (1.0 / total) if mean is None else scale * c * (1.0 / total)

    def rows_of(buf, l, t, start, size):
        return buf[l, pl.ds(t, per), pl.ds(start, size), :].reshape(per * size, buf.shape[-1])

    def enter(p):
        l, g = div(p, GROUPS), rem(p, GROUPS)
        base = g * per
        slot = rem(p, GROUPS)
        for c in range(per):
            t = base + c
            mean = fin[p, 0, pl.ds(c, 1), :]
            scale = fin[p, 1, pl.ds(c, 1), :]
            xs[l, t, pl.ds(0, nodes), :] = pair((raw[l, t] - mean) * scale)
            near = jnp.concatenate([hr[1, l, t], hr[0, l, t]], 0)
            near = (near - mean) * scale
            yh[t] = near
            xs[l, t, pl.ds(nodes, 2 * RIM), :] = pair(near)
            if c == per // 2 - 1:
                yield
        x = rows_of(xs, l, base, 0, ext)
        side = xa[pl.ds(base, per)].reshape(per * ext, D)
        yield
        p4 = dot(x, w_in[l, pl.ds(0, 2 * D), :])
        p4 = p4 + dot(jnp.concatenate([x[:, :D], side], 1), w_in[l, pl.ds(2 * D, 2 * D), :])
        yield
        for c in range(per):
            at = c * ext
            a_buf[l, base + c] = p4[at : at + nodes, :D]
            r_buf[l, base + c, pl.ds(RIM, nodes), :] = p4[at : at + nodes, D : 2 * D]
            r_buf[l, base + c, pl.ds(0, RIM), :] = p4[at + nodes : at + nodes + RIM, D : 2 * D]
            r_buf[l, base + c, pl.ds(RIM + nodes, RIM), :] = p4[
                at + nodes + RIM : at + ext, D : 2 * D
            ]
            n_buf[slot, c] = p4[at : at + nodes, 2 * D :]
            if c % 2:
                yield

    def first_main(g):
        base = g * per
        for c in range(per):
            xs[0, base + c, pl.ds(0, nodes), :] = pair(raw[0, base + c])
        x = rows_of(xs, 0, base, 0, nodes)
        side = xa[pl.ds(base, per), pl.ds(0, nodes), :].reshape(per * nodes, D)
        product = dot(x, w_in[0, pl.ds(0, 2 * D), :])
        product = product + dot(
            jnp.concatenate([x[:, :D], side], 1), w_in[0, pl.ds(2 * D, 2 * D), :]
        )
        for c in range(per):
            part = product[c * nodes : (c + 1) * nodes]
            a_buf[0, base + c] = part[:, :D]
            r_buf[0, base + c, pl.ds(RIM, nodes), :] = part[:, D : 2 * D]
            n_buf[g, c] = part[:, 2 * D :]

    def first_rims():
        lane = lax.broadcasted_iota(jnp.int32, (RIM, D), 1)
        moved = jnp.where((lane == A_PLACE) | (lane == 2 * AUX + A_PLACE), float(nodes), 0.0)
        near = []
        for t in range(traj):
            side = jnp.concatenate(
                [
                    pltpu.roll(hr[1, 0, t], HALO, 0) - moved,
                    pltpu.roll(hr[0, 0, t], RIM - HALO, 0) + moved,
                ],
                0,
            ).astype(BF16)
            xa[t, pl.ds(nodes, 2 * RIM), :] = side
            head, tail = split(jnp.concatenate([hr[1, 0, t], hr[0, 0, t]], 0))
            xs[0, t, pl.ds(nodes, 2 * RIM), :] = jnp.concatenate([head, tail], 1)
            near.append(jnp.concatenate([head, tail, head, side], 1))
        product = dot(jnp.concatenate(near, 0), w_in[0, :, pl.ds(D, D)])
        for t in range(traj):
            at = t * 2 * RIM
            r_buf[0, t, pl.ds(0, RIM), :] = product[at : at + RIM]
            r_buf[0, t, pl.ds(RIM + nodes, RIM), :] = product[at + RIM : at + 2 * RIM]

    def edges(p, s):
        l, g = div(p, GROUPS), rem(p, GROUPS)
        bias2 = 0.5 * eb2[pl.ds(l, 1), :]
        t = g * per + s
        hidden = []
        for i, o in enumerate(OFFSETS):
            half = a_buf[l, t] + r_buf[l, t, pl.ds(RIM + o, nodes), :]
            hidden.append(pair(half * (1.0 + jnp.tanh(half))))
            if i % 2:
                yield
        product = dot(jnp.concatenate(hidden, 0), w_e2[l])
        yield
        summed = None
        for i in range(K):
            half = halves(product[i * nodes : (i + 1) * nodes]) + bias2
            tanh = jnp.tanh(half)
            scaled = weigh[t, pl.ds(i * nodes, nodes), :] * (1.0 + tanh)
            message = scaled * half
            summed = message if summed is None else summed + message
            slope[l, t, pl.ds(i * nodes, nodes), :] = scaled + message * (1.0 - tanh)
            if i % 2 and i < K - 1:
                yield
        dag[rem(p, 2), s] = summed * (1.0 / K)
        yield

    def node(p):
        l, g = div(p, GROUPS), rem(p, GROUPS)
        base = g * per
        slot = rem(p, 2)
        here = rem(p, GROUPS)
        node2 = 0.5 * nb2[pl.ds(l, 1), :]
        both = pair(dag[slot].reshape(per * nodes, D))
        agg2[l, pl.ds(base, per)] = both.reshape(per, nodes, 2 * D)
        product = dot(both, w_agg[l])
        yield
        half = n_buf[here].reshape(per * nodes, D) + halves(product)
        act, rise = swish_parts(half)
        sn1[l, pl.ds(base, per)] = (0.5 * rise).reshape(per, nodes, D)
        both = pair(act)
        hid2[l, pl.ds(base, per)] = both.reshape(per, nodes, 2 * D)
        product = dot(both, w_n2[l])
        yield
        half = halves(product) + node2
        act, rise = swish_parts(half)
        sn2[l, pl.ds(base, per)] = (0.5 * rise).reshape(per, nodes, D)
        for c in range(per):
            t = base + c
            before = raw[l, t]
            if l > 0:
                before = (before - fin[p, 0, pl.ds(c, 1), :]) * fin[p, 1, pl.ds(c, 1), :]
            new = before + act[c * nodes : (c + 1) * nodes]
            raw[l + 1, t] = new
            mean = jnp.sum(new, 0, keepdims=True) * (1.0 / nodes)
            gap = new - mean
            stat[0][p, pl.ds(c, 1), :] = mean
            stat[0][p, pl.ds(per + c, 1), :] = jnp.sum(gap * gap, 0, keepdims=True)
            if l < LAYERS - 1:
                hs[0, 1, t] = new[:RIM]
                hs[1, 1, t] = new[nodes - RIM :]
            else:
                up = dst[t]
                stat[0][p, pl.ds(2 * per + c, 1), :] = jnp.sum(up, 0, keepdims=True)
                stat[0][p, pl.ds(3 * per + c, 1), :] = jnp.sum(up * gap, 0, keepdims=True)
            if c % 2:
                yield

    def hand_on(event):
        if event is not None:
            stat_forward(event)
        yield

    def forward(p, _):
        border = p == GROUPS

        @pl.when((p > 0) & negated(border))
        def _():
            weave(
                ORDER_NODE[:HAND_ON] + "3" + ORDER_NODE[HAND_ON:],
                edges(p, 0),
                edges(p, 1),
                node(p - 1),
                hand_on(p - 2 if 1 < p < GROUPS else None),
            )

        @pl.when((p == 0) | border)
        def _():
            weave(ORDER_EDGES, edges(p, 0), edges(p, 1))

        @pl.when((p > 0) & negated(border))
        def _():
            stat_send(p - 1, 0)

        @pl.when((p > 0) & (p < GROUPS))
        def _():
            ring_send(*layer_rims(p - 1), p)

        @pl.when(border)
        def _():
            stat_forward(p - 1)

        def ready():
            stat_finish(p + 1 - GROUPS)
            arrived(layer_rims(p + 1 - GROUPS)[1], rim_rsem.at[p + 2 - GROUPS])

        pl.when((p + 1 > GROUPS) & (p + 1 < phases))(ready)
        alone = (p + 1 <= GROUPS) | (p + 1 == phases)

        @pl.when(negated(alone))
        def _():
            weave(ORDER_ENTER, edges(p, 2), edges(p, 3), enter(p + 1))

        @pl.when(alone)
        def _():
            weave(ORDER_EDGES, edges(p, 2), edges(p, 3))

        @pl.when(p + 1 == GROUPS)
        def _():
            weave("", node(p))
            stat_send(p, 0)
            ring_send(*layer_rims(p), p + 1)
            stat_forward(p - 1)
            ready()
            weave("", enter(p + 1))

        @pl.when(p > GROUPS)
        def _():
            stat_forward(p - 1)

        return 0

    def back_node(p):
        l, g = LAYERS - 1 - div(p, GROUPS), rem(p, GROUPS)
        base = g * per
        source = phases + p
        own = GROUPS * (l + 1) + g
        back = div(p, GROUPS)
        deltas, firsts = [], []
        for c in range(per):
            t = base + c
            scale = fin[own, 1, pl.ds(c, 1), :]
            mu = fin[source, 2, pl.ds(c, 1), :]
            cross = fin[source, 3, pl.ds(c, 1), :]
            y = (raw[l + 1, t] - fin[own, 0, pl.ds(c, 1), :]) * scale
            up = dst[t]
            if l == LAYERS - 1:
                raw[l + 1, t] = y
            else:
                up = jnp.concatenate(
                    [
                        up[:RIM] + rr[back, 1, t],
                        up[RIM : nodes - RIM],
                        up[nodes - RIM :] + rr[back, 0, t],
                    ],
                    0,
                )
            delta = scale * (up - mu - y * cross)
            first = delta * sn2[l, t]
            acc_bn[l] += jnp.sum(first.reshape(nodes // 8, 8, D), 0)
            deltas.append(delta)
            firsts.append(first)
            if c == per // 2 - 1:
                yield
        d2 = pair(jnp.concatenate(firsts, 0))
        yield
        x = rows_of(xs, l, base, 0, nodes)
        side = xa[pl.ds(base, per), pl.ds(0, nodes), :].reshape(per * nodes, D)
        size = per * nodes
        product = dot(d2, w_n2t[l])
        yield
        d1 = halves(product) * sn1[l, pl.ds(base, per)].reshape(size, D)
        d1 = pair(d1)
        product = dot(jnp.concatenate([d1, d1[:, :D]], 1), w_np[l])
        yield
        acc_n2[l] += dot_t(hid2[l, pl.ds(base, per)].reshape(size, 2 * D), d2)
        yield
        for c in range(per):
            at = c * nodes
            dst[base + c] = deltas[c] + product[at : at + nodes, :D]
            dag[rem(p, 2), c] = product[at : at + nodes, D:] * (1.0 / K)
        acc_agg[l] += dot_t(agg2[l, pl.ds(base, per)].reshape(size, 2 * D), d1)
        yield
        acc_nx[l] += dot_t(jnp.concatenate([x, side[:, : 2 * AUX]], 1), d1)
        yield

    def back_edges(p, s):
        l, g = LAYERS - 1 - div(p, GROUPS), rem(p, GROUPS)
        slot = rem(p, 2)
        t = g * per + s
        mine = e1.at[s % 2]
        hidden, deltas, rises = [], [], []
        coming = dag[slot, s]
        bias = None
        for i, o in enumerate(OFFSETS):
            half = a_buf[l, t] + r_buf[l, t, pl.ds(RIM + o, nodes), :]
            act, rise = swish_parts(half)
            rises.append(rise)
            hidden.append(pair(act))
            delta = coming * slope[l, t, pl.ds(i * nodes, nodes), :]
            bias = delta if bias is None else bias + delta
            deltas.append(pair(delta))
            if i % 2 and i < K - 1:
                yield
        d2 = jnp.concatenate(deltas, 0)
        acc_be[l] += jnp.sum(bias.reshape(nodes // 8, 8, D), 0)
        yield
        product = dot(d2, w_e2t[l])
        yield
        acc_e2[l] += dot_t(jnp.concatenate(hidden, 0), d2)
        yield
        near = None
        for i in range(K):
            d1 = halves(product[i * nodes : (i + 1) * nodes]) * rises[i]
            near = d1 if near is None else near + d1
            mine[i, pl.ds(RIM, nodes), :] = d1
            if i == K // 2 - 1:
                yield
        yield
        far = None
        left = None
        right = None
        for i, o in enumerate(OFFSETS):
            part = mine[i, pl.ds(RIM - o, nodes), :]
            far = part if far is None else far + part
            if o < 0:
                part = mine[i, pl.ds(-o, RIM), :]
                left = part if left is None else left + part
            else:
                part = mine[i, pl.ds(RIM + nodes - o, RIM), :]
                right = part if right is None else right + part
        rims = jnp.concatenate([left, right], 0)
        head, tail = split(near)
        head_f, tail_f = split(far)
        head_r, tail_r = split(rims)
        nothing = jnp.zeros((2 * RIM, D), BF16)
        dxh[slot, s, pl.ds(0, nodes), :] = jnp.concatenate([head, head_f], 1)
        dxl[slot, s, pl.ds(0, nodes), :] = jnp.concatenate([tail, tail_f], 1)
        dxh[slot, s, pl.ds(nodes, 2 * RIM), :] = jnp.concatenate([nothing, head_r], 1)
        dxl[slot, s, pl.ds(nodes, 2 * RIM), :] = jnp.concatenate([nothing, tail_r], 1)
        yield

    def leave_weights(p):
        l, g = LAYERS - 1 - div(p, GROUPS), rem(p, GROUPS)
        base = g * per
        size = per * ext
        slot = rem(p, 2)
        x = rows_of(xs, l, base, 0, ext)
        side = xa[pl.ds(base, per)].reshape(size, D)
        inputs = jnp.concatenate([x, side[:, : 2 * AUX]], 1)
        high = dxh[slot].reshape(size, 2 * D)
        low = dxl[slot].reshape(size, 2 * D)
        acc_x[l] += dot_t(
            jnp.concatenate([inputs, inputs], 0), jnp.concatenate([high, low], 0)
        )
        yield

    def leave_state(p):
        l, g = LAYERS - 1 - div(p, GROUPS), rem(p, GROUPS)
        base = g * per
        size = per * ext
        slot = rem(p, 2)
        event = phases + p
        back = div(p, GROUPS)
        own = GROUPS * l + g
        high = dxh[slot].reshape(size, 2 * D)
        low = dxl[slot].reshape(size, 2 * D)
        product = dot(high, w_ep[l]) + dot(low, w_ep[l])
        yield
        product = halves(product)
        for c in range(per):
            t, at = base + c, c * ext
            new = dst[t] + product[at : at + nodes]
            dst[t] = new
            rims = product[at + nodes : at + ext]
            rs[back, 0, t] = rims[:RIM]
            rs[back, 1, t] = rims[RIM:]
            if l > 0:
                y = (raw[l, t] - fin[own, 0, pl.ds(c, 1), :]) * fin[own, 1, pl.ds(c, 1), :]
                stat[0][event, pl.ds(2 * per + c, 1), :] = jnp.sum(
                    new, 0, keepdims=True
                ) + jnp.sum(rims, 0, keepdims=True)
                stat[0][event, pl.ds(3 * per + c, 1), :] = jnp.sum(
                    new * y, 0, keepdims=True
                ) + jnp.sum(rims * yh[t], 0, keepdims=True)
            if c % 2:
                yield

    def backward(p, _):
        @pl.when(p > 0)
        def _():
            weave(
                ORDER_LEAVE,
                back_edges(p, 0),
                back_edges(p, 1),
                leave_weights(p - 1),
                leave_state(p - 1),
            )

        @pl.when(p == 0)
        def _():
            weave(ORDER_BACK, back_edges(p, 0), back_edges(p, 1))
            stat_forward(phases - 1)

        @pl.when(p > 0)
        def _():
            ring_send(*grad_rims(p - 1), GROUPS + p, 1)

        @pl.when((p > 0) & (p <= GROUPS))
        def _():
            stat_send(phases + p - 1, 0)

        @pl.when(p == GROUPS)
        def _():
            unit_second(unit.at[1], acc_e2.at[1])
            edge_unit(1, unit.at[1])

        sum_hook(SUMS_MID, p)

        def ready():
            stat_finish(GROUPS + p + 1)

        def rims_ready():
            arrived(grad_rims(p + 1 - GROUPS)[1], rim_rsem.at[p + 2])

        alone = (p + 1 == GROUPS) | (p + 1 == phases)
        pl.when(negated(alone))(ready)
        pl.when((p + 1 > GROUPS) & (p + 1 < phases))(rims_ready)

        @pl.when(negated(alone))
        def _():
            weave(ORDER_BACK_NODE, back_edges(p, 2), back_edges(p, 3), back_node(p + 1))

        @pl.when(alone)
        def _():
            weave(ORDER_BACK, back_edges(p, 2), back_edges(p, 3))

        @pl.when((p > 0) & (p <= GROUPS))
        def _():
            stat_forward(phases + p - 1)

        @pl.when(p + 1 == GROUPS)
        def _():
            ready()
            rims_ready()
            weave("", back_node(p + 1))

        @pl.when(p == GROUPS - 2)
        def _():
            node_unit(1, unit.at[0])

        @pl.when(p == phases - 2)
        def _():
            node_unit(0, unit.at[2])

        sum_hook(SUMS_END, p)

        return 0

    def quarter(acc, rows):
        return (
            acc[pl.ds(0, rows), pl.ds(0, D)]
            + acc[pl.ds(D, rows), pl.ds(0, D)]
            + acc[pl.ds(0, rows), pl.ds(D, D)]
            + acc[pl.ds(D, rows), pl.ds(D, D)]
        )

    def fold8(value):
        return jnp.sum(value, 0, keepdims=True)

    def unit_second(out, acc):
        out[pl.ds(0, D), :] = quarter(acc, D)

    def node_unit(l, out):
        unit_second(out, acc_n2.at[l])
        out[pl.ds(UNIT_FIRST, D), :] = quarter(acc_nx.at[l], D)
        out[pl.ds(UNIT_FIRST + D, D), :] = quarter(acc_agg.at[l], D)
        side = acc_nx[l, pl.ds(2 * D, AUX), :] + acc_nx[l, pl.ds(2 * D + AUX, AUX), :]
        out[pl.ds(UNIT_AUX, AUX), :] = halves(side)
        out[pl.ds(UNIT_AUX + A_SECOND, 1), :] = fold8(acc_bn[l])

    def edge_unit(l, out):
        both = acc_x[l, pl.ds(0, D), :] + acc_x[l, pl.ds(D, D), :]
        out[pl.ds(UNIT_FIRST, D), :] = both[:, :D]
        out[pl.ds(UNIT_FIRST + D, D), :] = both[:, D:]
        side = acc_x[l, pl.ds(2 * D, AUX), :] + acc_x[l, pl.ds(2 * D + AUX, AUX), :]
        row = lax.broadcasted_iota(jnp.int32, (AUX, D), 0)
        both = side[:, :D] - side[:, D:]
        out[pl.ds(UNIT_AUX, AUX), :] = jnp.where(
            row < TW, both, jnp.where(row == A_PLACE, both * (1.0 / HALO), side[:, :D])
        )
        out[pl.ds(UNIT_AUX + A_SECOND, 1), :] = fold8(acc_be[l])

    shares = len(links.share_stages)
    pieces = [1]
    for stage in range(shares):
        pieces.append(pieces[-1] * links.share_size(stage))
    lead, unit_rows = unit_sizes(graph)
    sums = (
        (0, 0, unit_rows),
        (1, 0, unit_rows),
        (2, 0, unit_rows),
        (3, 0, lead),
        (3, lead, unit_rows - lead),
    )
    steps = 2 * shares + len(swaps)

    def sum_step(n, step):
        u, start, rows = sums[n]

        def segment(stage, digit=None):
            place = start
            for k in range(stage):
                mine = links.share_digit(k) if digit is None or k < stage - 1 else digit
                place = place + mine * (rows // pieces[k + 1])
            return pl.ds(pl.multiple_of(place, 8), rows // pieces[stage])

        def part(stage):
            return pl.ds(start // pieces[stage], rows // pieces[stage])

        def others(stage):
            return range(1, links.share_size(stage))

        last = part(shares)
        done = step - 1
        value = None
        if 0 <= done < shares:
            into = unit_recv[done].at[u, :, part(done + 1)]
            arrived(into, share_rsem.at[done, n])
            value = unit[u, segment(done + 1), :]
            for shift in others(done):
                value = value + into[shift - 1]
        elif 0 <= done < shares + len(swaps):
            stage = done - shares
            into = swap_recv[stage].at[u, :, last]
            arrived(into, swap_rsem[stage].at[n])
            value = swap[stage][u, last, :]
            for shift in range(1, swaps[stage][1]):
                value = value + into[shift - 1]
        elif done >= 0:
            stage = steps - 1 - done
            arrived(unit_recv[stage].at[u, :, part(stage + 1)], share_rsem.at[shares + stage, n])
        if step < shares:
            if value is not None:
                unit[u, segment(step), :] = value
            for shift in others(step):
                peer, digit = links.share_peer(step, shift)
                remote(
                    unit.at[u, segment(step + 1, digit)],
                    unit_recv[step].at[u, shift - 1, part(step + 1)],
                    share_ssem.at[step],
                    share_rsem.at[step, n],
                    peer,
                ).start()
        elif step < shares + len(swaps):
            stage = step - shares
            swap[stage][u, last, :] = value
            stride, size = swaps[stage]
            for shift in range(1, size):
                remote(
                    swap[stage].at[u, last],
                    swap_recv[stage].at[u, shift - 1, last],
                    swap_ssem[stage].at[0],
                    swap_rsem[stage].at[n],
                    links.digit_peer(stride, size, shift),
                ).start()
        elif step < steps:
            if value is not None:
                unit_all[u, segment(shares), :] = value
            stage = steps - 1 - step
            for shift in others(stage):
                mine = segment(stage + 1)
                remote(
                    unit_all.at[u, mine],
                    unit_all.at[u, mine],
                    share_ssem.at[shares + stage],
                    share_rsem.at[shares + stage, n],
                    links.share_peer(stage, shift)[0],
                ).start()

    def sum_hook(table, p):
        for phase, n, step in table:
            pl.when(p == phase)(functools.partial(sum_step, n, step))

    for g in range(GROUPS):
        first_main(g)
    arrived(first[1], rim_rsem.at[0])
    first_rims()
    for p in range(phases):
        forward(p, 0)
    weave("", node(phases - 1))
    stat_send(phases - 1, 0)
    back_weights()
    stat_finish(GROUPS)
    weave("", back_node(0))
    for p in range(phases):
        backward(p, 0)
    unit_second(unit.at[3], acc_e2.at[0])
    sum_step(3, 0)
    weave("", leave_weights(phases - 1))
    edge_unit(0, unit.at[3])
    sum_step(4, 0)
    weave("", leave_state(phases - 1))
    ring_send(*grad_rims(phases - 1), GROUPS + phases, 1)
    done = {n: 0 for n in range(len(sums))}
    for table in (SUMS_MID, SUMS_END):
        for _, n, step in table:
            done[n] = max(done[n], step)
    for turn in range(2 * steps):
        for n in SUMS_TURNS[min(turn, len(SUMS_TURNS) - 1)]:
            if done[n] < steps:
                done[n] += 1
                sum_step(n, done[n])
        if turn:
            continue
        for g in range(GROUPS):
            arrived(grad_rims(phases - GROUPS + g)[1], rim_rsem.at[phases + 1 + g])
            for c in range(per):
                t = g * per + c
                dst[t, pl.ds(0, RIM), :] += rr[LAYERS, 1, t]
                dst[t, pl.ds(nodes - RIM, RIM), :] += rr[LAYERS, 0, t]

    arrived(hr, rim_ssem.at[0])
    arrived(rs, rim_ssem.at[1])
    for stage in range(len(stages)):
        arrived(stat_recv[stage].at[pl.ds(0, phases)], stat_ssem[stage].at[0])
    for stage in range(len(swaps)):
        arrived(swap_recv[stage], swap_ssem[stage].at[0])
    for stage in range(shares):
        for way in range(2):
            arrived(unit_recv[stage], share_ssem.at[way * shares + stage])


def unit_sizes(graph):
    share = 8 * 4 * graph
    lead = -(-UNIT_FIRST // share) * share
    return lead, lead + -(-(UNIT_ROWS - UNIT_FIRST) // share) * share


def assemble(
    raw,
    grad_mid,
    units,
    state_out,
    grad_out,
    g_ew1,
    g_eb1,
    g_ew2,
    g_eb2,
    g_nw1,
    g_nb1,
    g_nw2,
    g_nb2,
    sems,
):
    parts = sems.shape[1]
    rows = state_out.shape[0] // parts
    copies = []
    for i, (src, dst) in enumerate(((raw.at[LAYERS], state_out), (grad_mid, grad_out))):
        for part in range(parts):
            cut = pl.ds(part * rows, rows)
            copies.append(pltpu.make_async_copy(src.at[cut], dst.at[cut], sems.at[i, part]))
    for copy in copies:
        copy.start()
    for l in range(LAYERS):
        node, edge = units.at[2 * (LAYERS - 1 - l)], units.at[2 * (LAYERS - 1 - l) + 1]
        for unit, first, bias1, second, bias2 in (
            (node, g_nw1, g_nb1, g_nw2, g_nb2),
            (edge, g_ew1, g_eb1, g_ew2, g_eb2),
        ):
            first[pl.ds(0, 2 * D), l, :] = unit[pl.ds(UNIT_FIRST, 2 * D), :]
            bias1[pl.ds(l, 1), :] = unit[pl.ds(UNIT_AUX + A_ONE, 1), :]
            second[l] = unit[pl.ds(0, D), :]
            bias2[pl.ds(l, 1), :] = unit[pl.ds(UNIT_AUX + A_SECOND, 1), :]
        g_nw1[pl.ds(2 * D, NPAR), l, :] = node[pl.ds(UNIT_AUX + A_THETA, NPAR), :]
        g_ew1[pl.ds(2 * D, TW), l, :] = edge[pl.ds(UNIT_AUX, TW), :]
        g_ew1[pl.ds(2 * D + TW, 1), l, :] = edge[pl.ds(UNIT_AUX + A_PLACE, 1), :]
        g_ew1[pl.ds(2 * D + TW + 1, NPAR), l, :] = edge[pl.ds(UNIT_AUX + A_THETA, NPAR), :]
    for copy in copies:
        copy.wait()


def on_device(
    blk,
    graph,
    node_state,
    field_window,
    edge_offset,
    pde_id,
    pde_table,
    cotangent,
    edge_w1,
    edge_b1,
    edge_w2,
    edge_b2,
    node_w1,
    node_b1,
    node_w2,
    node_b2,
):
    traj, nodes, _ = node_state.shape
    per = traj // GROUPS
    ext = nodes + 2 * RIM
    field = jnp.transpose(field_window, (2, 0, 1)).reshape(TW * traj, nodes)
    offset = jnp.transpose(edge_offset, (2, 0, 1)).reshape(K * traj, nodes)
    table = jnp.transpose(pde_table, (1, 0))
    ew1 = jnp.transpose(edge_w1, (1, 0, 2))
    nw1 = jnp.transpose(node_w1, (1, 0, 2))
    vmem = pl.BlockSpec(memory_space=pltpu.VMEM)
    any_space = pl.BlockSpec(memory_space=pl.ANY)
    stages = digit_stages(blk, STAT_SIZES)
    swaps = digit_stages(blk // 4, (4,))
    shares = 4 * graph
    _, rows = unit_sizes(graph)
    seg = rows // shares
    events = 3 * GROUPS

    def f(*shape):
        return pltpu.VMEM(shape, F32)

    def b(*shape):
        return pltpu.VMEM(shape, BF16)

    L = LAYERS
    scratch = [
        f(TW * traj, nodes),
        pltpu.VMEM((K * traj, nodes), jnp.int32),
        pltpu.SMEM((traj,), jnp.int32),
        pltpu.SMEM((NPAR, NPDE), F32),
        f(L, -(-EDGE_IN // 8) * 8, D),
        f(L, D),
        f(L, D, D),
        f(L, D),
        f(L, -(-NODE_IN // 8) * 8, D),
        f(L, D),
        f(L, D, D),
        f(L, D),
        b(L, 4 * D, 3 * D),
        b(L, 2 * D, 2 * D),
        b(L, 2 * D, 2 * D),
        b(L, 2 * D, 2 * D),
        b(L, 2 * D, 2 * D),
        b(L, 2 * D, 2 * D),
        b(L, 3 * D, 2 * D),
        b(L, 2 * D, 2 * D),
        f(AUX, 3 * D),
        b(D, K * D),
        f(8 * traj, nodes),
        f(traj, K * nodes, D),
        f(traj, AUX, nodes),
        b(L, traj, ext, 2 * D),
        b(traj, ext, D),
        f(L, traj, nodes, D),
        f(L, traj, ext, D),
        f(GROUPS, per, nodes, D),
        f(L, traj, K * nodes, D),
        b(L, traj, nodes, 2 * D),
        b(L, traj, nodes, 2 * D),
        f(L, traj, nodes, D),
        f(L, traj, nodes, D),
        f(traj, 2 * RIM, D),
        f(2, per, nodes, D),
        f(2, K, ext, D),
        b(2, per, ext, 2 * D),
        b(2, per, ext, 2 * D),
        f(L, 2 * D, 2 * D),
        f(L, 2 * D, 2 * D),
        f(L, 2 * D + 2 * AUX, 2 * D),
        f(L, 2 * D, 2 * D),
        f(L, 2 * D + 2 * AUX, 2 * D),
        f(L, 8, D),
        f(L, 8, D),
        f(events + GROUPS, 4, per, D),
        f(2, L, traj, RIM, D),
        f(2, 2, traj, RIM, D),
        f(L, 2, traj, RIM, D),
        f(L + 1, 2, traj, RIM, D),
        f(4, rows, D),
        pltpu.SemaphoreType.DMA((16,)),
        pltpu.SemaphoreType.DMA((2,)),
        pltpu.SemaphoreType.DMA((1 + 3 * GROUPS,)),
        pltpu.SemaphoreType.DMA((4,)),
        pltpu.SemaphoreType.DMA((4, 5)),
    ]
    scratch += [f(events, 4 * per, D) for _ in stages]
    scratch += [f(events, size - 1, 4 * per, D) for _, size in stages]
    scratch += [pltpu.SemaphoreType.DMA((1,)) for _ in stages]
    scratch += [pltpu.SemaphoreType.DMA((events,)) for _ in stages]
    scratch += [f(4, seg, D) for _ in swaps]
    scratch += [f(4, size - 1, seg, D) for _, size in swaps]
    scratch += [pltpu.SemaphoreType.DMA((1,)) for _ in swaps]
    scratch += [pltpu.SemaphoreType.DMA((5,)) for _ in swaps]
    scratch += [f(4, 1, rows // 2, D), f(4, 2 * graph - 1, seg, D)]
    hbm = any_space
    mid = pl.pallas_call(
        functools.partial(kernel_body, blk, graph),
        out_shape=[f(L + 1, traj, nodes, D), f(traj, nodes, D), f(4, rows, D)],
        in_specs=[hbm] * 14,
        out_specs=[vmem] * 3,
        scratch_shapes=scratch,
        compiler_params=pltpu.CompilerParams(
            collective_id=0, has_side_effects=True, vmem_limit_bytes=54 * 2**20
        ),
        name="processor",
    )(
        node_state,
        field,
        offset,
        pde_id,
        table,
        cotangent,
        ew1,
        edge_b1,
        edge_w2,
        edge_b2,
        nw1,
        node_b1,
        node_w2,
        node_b2,
    )
    mid = [pltpu.with_memory_space_constraint(part, pltpu.VMEM) for part in mid]
    shapes = [
        (traj, nodes, D),
        (traj, nodes, D),
        (EDGE_IN, L, D),
        (L, D),
        (L, D, D),
        (L, D),
        (NODE_IN, L, D),
        (L, D),
        (L, D, D),
        (L, D),
    ]
    out = pl.pallas_call(
        assemble,
        out_shape=[jax.ShapeDtypeStruct(shape, F32) for shape in shapes],
        in_specs=[vmem] * 3,
        out_specs=[any_space, any_space] + [vmem] * 8,
        scratch_shapes=[pltpu.SemaphoreType.DMA((2, 8))],
        compiler_params=pltpu.CompilerParams(vmem_limit_bytes=8 * 2**20),
        name="assemble",
    )(*mid)
    out = list(out)
    out[2] = jnp.transpose(out[2], (1, 0, 2))
    out[6] = jnp.transpose(out[6], (1, 0, 2))
    return tuple(out)


def solution(mesh):
    rows = P("graph", "blk", None)
    return jax.shard_map(
        functools.partial(on_device, mesh.shape["blk"], mesh.shape["graph"]),
        mesh=mesh,
        in_specs=(rows, rows, rows, P("graph"), P(), rows) + (P(),) * 8,
        out_specs=(rows, rows) + (P(),) * 8,
        check_vma=False,
    )
```
